32 devices in a mesh: ctx: 4 (over z), fsdp: 8 (over y, x, core).
Axes of the slice: x: 2, y: 2, z: 4, core: 2. Of those that a mesh axis runs over, the one named last changes fastest.
Arguments:
- tokens: bfloat16 [16, 1024, 1024], P('fsdp', 'ctx'), may hold values from -6 to 6
- cotangent: bfloat16 [16, 1024, 1024], P('fsdp', 'ctx'), may hold values from -6 to 6
- sequence_lengths: int32 [16], replicated, may hold values from 1 to 1024, 10240 in all
- slot_sequence: int32 [16], replicated, may hold values from 0 to 15, each once
- offset_bucket: int32 [2047], replicated, may hold values from 0 to 31
- first_gain: bfloat16 [1024], P('fsdp'), may hold values from 0.5 to 1.5
- second_gain: bfloat16 [1024], P('fsdp'), may hold values from 0.5 to 1.5
- query_weight: bfloat16 [1024, 1024], P('fsdp'), may hold values from -0.09375 to 0.09375
- key_weight: bfloat16 [1024, 1024], P('fsdp'), may hold values from -0.09375 to 0.09375
- value_weight: bfloat16 [1024, 1024], P('fsdp'), may hold values from -0.1875 to 0.1875
- output_weight: bfloat16 [1024, 1024], P('fsdp'), may hold values from -0.75 to 0.75
- expand_weight: bfloat16 [1024, 4096], P('fsdp'), may hold values from -0.1875 to 0.1875
- contract_weight: bfloat16 [1024, 4096], P('fsdp'), may hold values from -0.125 to 0.125
- bias_table: bfloat16 [32, 16], replicated, may hold values from -4 to 4
- clip_limit: float32 [16], replicated, may hold values from 0.5 to 6
Outputs:
- output: bfloat16 [16, 1024, 1024], P('fsdp', 'ctx')
- input_gradient: float32 [16, 1024, 1024], P('fsdp', 'ctx')
- first_gain_gradient: float32 [1024], P('fsdp')
- second_gain_gradient: float32 [1024], P('fsdp')
- query_weight_gradient: float32 [1024, 1024], P('fsdp')
- key_weight_gradient: float32 [1024, 1024], P('fsdp')
- value_weight_gradient: float32 [1024, 1024], P('fsdp')
- output_weight_gradient: float32 [1024, 1024], P('fsdp')
- expand_weight_gradient: float32 [1024, 4096], P('fsdp')
- contract_weight_gradient: float32 [1024, 4096], P('fsdp')
- bias_table_gradient: float32 [32, 16], P('fsdp')
- head_maximum: float32 [16], replicated
- new_query_weight: float32 [1024, 1024], P('fsdp')
- new_key_weight: float32 [1024, 1024], P('fsdp')
The draws below stay inside these ranges and needn't reach their ends.
Inputs may be any that keep to these rules, and one draw needn't show every extreme that they name: `sequence_lengths`: the longest sequence has exactly 1024 valid positions. `slot_sequence`: every sequence number appears in exactly one slot.
All inputs are finite; a program needn't handle non-finite values.
Results may differ from the reference program's by a relative error of at most 0.015.
The reference program's roundings to bfloat16 on the way count: a program that leaves them out, or rounds other values in their place, can miss the bound.
Values may be sent and summed in bfloat16 or wider, within the bound.
No kernel may reach another device: no remote copies, remote signals or barrier semaphores. Data moves between devices by JAX's collectives and lax.ppermute only.
A program may use at most 512 MiB of HBM per device.

```python
import math
from functools import partial
import jax
import jax.numpy as jnp
import numpy as np
from jax import lax

D = 1024
HEADS = 16
HEAD_DIM = 64
FF = 4096
BUCKETS = 32
LEN = 1024
INNER = 1024
SEQS = 16


def touch_ends(drawn, stream_key, least, high):
    longest = drawn.shape.index(max(drawn.shape))
    spots = []
    for shift in (0, 1):
        where = [jax.random.randint(jax.random.fold_in(stream_key, axis), (), 0, length) for axis, length in enumerate(drawn.shape)]
        where[longest] = (where[longest] + shift) % drawn.shape[longest]
        spots.append(tuple(where))
    return drawn.at[spots[0]].set(least).at[spots[1]].set(high)


def shard_levels(own_key, dims, cuts, low, high):
    level = 1.0
    for axis_at, parts in cuts:
        heights = jax.random.uniform(jax.random.fold_in(jax.random.fold_in(own_key, 6), axis_at), (parts,), jnp.float32, low / len(cuts), high / len(cuts))
        level = level * jnp.repeat(jnp.exp(heights), dims[axis_at] // parts).reshape((-1,) + (1,) * (len(dims) - 1 - axis_at))
    return level


def split_up(number_of, total, bound, lean):
    portions = [(1 << 20) // math.isqrt(grade ** lean) + 1 for grade in range(2, number_of + 1)]
    rest, given = total - bound - (number_of - 1), [1] * (number_of - 1)
    while rest > 0:
        free = [i for i in range(number_of - 1) if given[i] < bound]
        mass, remaining = sum([portions[i] for i in free]), rest
        for i in free:
            addition = min(bound - given[i], max(1, remaining * portions[i] // mass), rest)
            given[i] = given[i] + addition
            rest = rest - addition
    return np.array([bound] + given)


def ragged(rng, count, total, bound, skew):
    if count == 2:
        one = jax.random.randint(rng, (), max(1, total - bound), min(bound, total - 1) + 1)
        return jnp.stack([one, total - one])
    lengths = jnp.asarray(split_up(count, total, bound, skew), jnp.int32)
    couples = (count - 1) // 2
    source_of, receiver = lengths[1:1 + 2 * couples:2], lengths[2:2 + 2 * couples:2]
    slack = jnp.minimum(source_of - 1, bound - receiver)
    shifted = jax.random.randint(jax.random.fold_in(rng, 1), (couples,), 0, 1 << 20) % (slack + 1)
    lengths = lengths.at[1:1 + 2 * couples:2].set(source_of - shifted).at[2:2 + 2 * couples:2].set(receiver + shifted)
    return lengths[jax.random.permutation(jax.random.fold_in(rng, 2), count)]


def bell_draw(key, extent, width, limit, pieces=(), kind=jnp.bfloat16):
    loudness = shard_levels(key, extent, pieces, -0.22, 0.18) if pieces else 1.0
    values = jax.random.normal(key, extent, jnp.float32) * width * loudness
    return jnp.minimum(jnp.maximum(values, -limit), limit).astype(kind)


def setup_inputs(seed: int = 0) -> dict:
    streams_of = jax.random.split(jax.random.key(seed), 16)
    tokens = bell_draw(streams_of[0], (SEQS, LEN, D), 1.0, 6.0, ((0, 8), (1, 4)))
    cotangent = bell_draw(streams_of[1], (SEQS, LEN, D), 1.0, 6.0, ((0, 8), (1, 4)))
    sequence_lengths = ragged(streams_of[2], SEQS, SEQS * LEN * 5 // 8, LEN, 2).astype(jnp.int32)
    slot_sequence = jax.random.permutation(streams_of[3], SEQS).astype(jnp.int32)
    offset_bucket = touch_ends(jax.random.randint(streams_of[4], (2 * LEN - 1,), 0, BUCKETS), jax.random.fold_in(streams_of[4], 1), 0, BUCKETS - 1).astype(jnp.int32)
    first_gain = jnp.clip(1.0 + 0.1 * jax.random.normal(streams_of[5], (D,), jnp.float32), 0.5, 1.5).astype(jnp.bfloat16)
    second_gain = jnp.clip(1.0 + 0.1 * jax.random.normal(streams_of[6], (D,), jnp.float32), 0.5, 1.5).astype(jnp.bfloat16)
    query_weight = bell_draw(streams_of[7], (D, INNER), (4 * D) ** -0.5, 0.09375, ((0, 8),))
    key_weight = bell_draw(streams_of[8], (D, INNER), (4 * D) ** -0.5, 0.09375, ((0, 8),))
    value_weight = bell_draw(streams_of[9], (D, INNER), D ** -0.5, 0.1875, ((0, 8),))
    output_weight = bell_draw(streams_of[10], (D, INNER), (INNER // 16) ** -0.5, 0.75, ((0, 8),))
    expand_weight = bell_draw(streams_of[11], (D, FF), D ** -0.5, 0.1875, ((0, 8),))
    contract_weight = bell_draw(streams_of[12], (D, FF), (FF // 2) ** -0.5, 0.125, ((0, 8),))
    bias_table = bell_draw(streams_of[13], (BUCKETS, HEADS), 1.0, 4.0)
    clip_limit = jnp.clip(jnp.exp(jax.random.uniform(streams_of[14], (HEADS,), jnp.float32, math.log(0.5), math.log(6.0))), 0.5, 6.0)
    return dict(tokens=tokens, cotangent=cotangent, sequence_lengths=sequence_lengths, slot_sequence=slot_sequence, offset_bucket=offset_bucket, first_gain=first_gain, second_gain=second_gain, query_weight=query_weight, key_weight=key_weight, value_weight=value_weight, output_weight=output_weight, expand_weight=expand_weight, contract_weight=contract_weight, bias_table=bias_table, clip_limit=clip_limit)


epsilon = 1e-06
masked = -1e+30
highest = lax.Precision.HIGHEST

@jax.custom_vjp
def low(v):
    return lax.optimization_barrier(v.astype(jnp.bfloat16)).astype(jnp.float32)

@jax.custom_vjp
def low_back(v):
    return v

def low_keep(v):
    return (low(v), None)

def low_pass(kept, grad):
    return (grad,)

def back_keep(v):
    return (v, None)

def back_low(kept, grad):
    return (low(grad),)
low.defvjp(low_keep, low_pass)
low_back.defvjp(back_keep, back_low)

def normalize(values):
    return values * lax.rsqrt(lax.optimization_barrier(jnp.mean(values * values, axis=-1, keepdims=True)) + epsilon)

def attend(queries, key_rows, value_rows, position_bias, valid_rows):
    seq_length = queries.shape[0]
    head_count = position_bias.shape[0]
    head_size = queries.shape[1] // head_count
    query_heads = queries.reshape(seq_length, head_count, head_size)
    key_heads = key_rows.reshape(seq_length, head_count, head_size)
    value_heads = value_rows.reshape(seq_length, head_count, head_size)
    products = jnp.einsum('qhd,khd->hqk', query_heads, key_heads, precision=highest)
    both_ok = valid_rows[None, :, None] & valid_rows[None, None, :]
    largest = lax.optimization_barrier(jnp.max(jnp.where(both_ok, products, masked), axis=(1, 2)))
    scores = low_back(products + position_bias)
    scores = jnp.where(valid_rows[None, None, :], scores, masked)
    weights_low = low(jax.nn.softmax(scores, axis=-1))
    context = jnp.einsum('hqk,khd->qhd', weights_low, value_heads, precision=highest)
    return (context.reshape(seq_length, head_count * head_size), largest)

def layer(params, token_group, valid_group, offset_bucket):
    first_gain, second_gain, query_weight, key_weight, value_weight, output_weight, expand_weight, contract_weight, table_values = params
    group_count, seq_length, model_width = token_group.shape
    inner_width = query_weight.shape[1]
    token_rows = token_group.reshape(-1, model_width)
    normed_one = low(normalize(token_rows))
    stacked = low(first_gain[:, None] * jnp.concatenate([query_weight, key_weight, value_weight], axis=1))
    projected = low_back(low(jnp.dot(normed_one, stacked, precision=highest)))
    per_offset = table_values[offset_bucket.astype(jnp.int32)]
    positions = jnp.arange(seq_length, dtype=jnp.int32)
    offsets = (positions[None, :] - positions[:, None] + (seq_length - 1)).astype(jnp.int32)
    position_bias = jnp.take(per_offset.T, offsets, axis=1)
    per_sequence = projected.reshape(group_count, seq_length, 3 * inner_width)

    def one_sequence(inputs):
        columns, valid_rows = inputs
        return attend(columns[:, :inner_width], columns[:, inner_width:2 * inner_width], columns[:, 2 * inner_width:], position_bias, valid_rows)
    context, largest = lax.map(jax.checkpoint(one_sequence), (per_sequence, valid_group))
    context = low_back(low(context.reshape(-1, inner_width)))
    attended = low_back(jnp.dot(context, output_weight.T, precision=highest))
    hidden_one = token_rows + attended
    normed_two = low(normalize(hidden_one))
    expand_low = low(second_gain[:, None] * expand_weight)
    pre_act = low_back(jnp.dot(normed_two, expand_low, precision=highest))
    activated = low_back(low(jax.nn.gelu(pre_act, approximate=False)))
    mixed = low_back(jnp.dot(activated, contract_weight.T, precision=highest))
    result = jnp.where(valid_group.reshape(-1, 1), hidden_one + mixed, 0.0)
    return (result.reshape(token_group.shape), lax.optimization_barrier(jnp.max(largest, axis=0)))

def reference(tokens, cotangent, sequence_lengths, slot_sequence, offset_bucket, first_gain, second_gain, query_weight, key_weight, value_weight, output_weight, expand_weight, contract_weight, bias_table, clip_limit):
    params = jax.tree.map(lambda weight_value: weight_value.astype(jnp.float32), (first_gain, second_gain, query_weight, key_weight, value_weight, output_weight, expand_weight, contract_weight, bias_table))
    slot_lengths = sequence_lengths.astype(jnp.int32)[slot_sequence.astype(jnp.int32)]
    valid = jnp.arange(LEN, dtype=jnp.int32)[None, :] < slot_lengths[:, None]
    group_size = 4
    groups = SEQS // group_size
    token_groups = tokens.astype(jnp.float32).reshape(groups, group_size, LEN, D)
    cot_groups = cotangent.astype(jnp.float32).reshape(groups, group_size, LEN, D)
    valid_groups = valid.reshape(groups, group_size, LEN)

    def group_step(totals, inputs):
        token_group, cot_group, valid_group = inputs
        result, pullback, largest = jax.vjp(partial(layer, valid_group=valid_group, offset_bucket=offset_bucket), params, token_group, has_aux=True)
        weight_grads, input_grad = pullback(cot_group)
        totals = (jax.tree.map(jnp.add, totals[0], weight_grads), jnp.maximum(totals[1], largest))
        return (totals, (result, input_grad))
    initial = (jax.tree.map(jnp.zeros_like, params), jnp.full((HEADS,), masked, jnp.float32))
    totals, (results, input_grads) = lax.scan(group_step, initial, (token_groups, cot_groups, valid_groups))
    grads, head_maximum = totals
    result_slots = results.reshape(SEQS, LEN, D).astype(jnp.bfloat16)
    output = jnp.zeros((SEQS, LEN, D), jnp.bfloat16).at[slot_sequence.astype(jnp.int32)].set(result_slots)
    input_gradient = input_grads.reshape(SEQS, LEN, D)
    shrink = clip_limit / jnp.maximum(clip_limit, head_maximum)
    column_scale = jnp.repeat(jnp.sqrt(shrink), HEAD_DIM)
    new_query_weight = params[2] * column_scale[None, :]
    new_key_weight = params[3] * column_scale[None, :]
    return (output, input_gradient, grads[0], grads[1], grads[2], grads[3], grads[4], grads[5], grads[6], grads[7], grads[8], head_maximum, new_query_weight, new_key_weight)
```

```python
import functools
import math

import jax
import jax.numpy as jnp
from jax import lax
from jax.experimental import pallas as pl
from jax.experimental.pallas import tpu as pltpu
from jax.sharding import PartitionSpec as P

epsilon = 1e-06
masked = -1e30
tile = 128
half_tile = 64
wide = jnp.float32
low = jnp.bfloat16


def dot(left, right, left_dim, right_dim):
    return lax.dot_general(
        left, right, (((left_dim,), (right_dim,)), ((), ())), preferred_element_type=wide
    )


def strip_kernel(line_ref, strip_ref):
    width = line_ref.shape[-1]
    rows = jnp.broadcast_to(line_ref[0], (tile, width))
    strip_ref[0] = pltpu.roll(rows, width - (tile - 1), 1, stride=1, stride_axis=0)


def bias_strips(lines):
    heads, _, width = lines.shape
    return pl.pallas_call(
        strip_kernel,
        grid=(heads,),
        in_specs=[pl.BlockSpec((1, 1, width), lambda h: (h, 0, 0))],
        out_specs=pl.BlockSpec((1, tile, width), lambda h: (h, 0, 0)),
        out_shape=jax.ShapeDtypeStruct((heads, tile, width), wide),
        compiler_params=pltpu.CompilerParams(vmem_limit_bytes=32 << 20),
        name="bias_strips",
    )(lines)


def diagonal_kernel(strip_ref, line_ref):
    strip = strip_ref[0]
    rows = tile
    while rows > 1:
        rows //= 2
        strip = pltpu.roll(strip[:rows], rows, 1) + strip[rows:]
    line_ref[0] = strip


def diagonal_sums(strips):
    heads, _, width = strips.shape
    return pl.pallas_call(
        diagonal_kernel,
        grid=(heads,),
        in_specs=[pl.BlockSpec((1, tile, width), lambda h: (h, 0, 0))],
        out_specs=pl.BlockSpec((1, 1, width), lambda h: (h, 0, 0)),
        out_shape=jax.ShapeDtypeStruct((heads, 1, width), wide),
        compiler_params=pltpu.CompilerParams(vmem_limit_bytes=32 << 20),
        name="diagonal_sums",
    )(strips)


def one_head(block, head, extra=None):
    lane = lax.broadcasted_iota(jnp.int32, block.shape, 1)
    kept = jnp.where((lane >= half_tile) if head else (lane < half_tile), block, 0)
    if extra is None:
        return kept
    return jnp.where(lane == (0 if head else half_tile), extra, kept)


def key_masks(total, length):
    position = lax.broadcasted_iota(jnp.int32, (total, tile), 0)
    return jnp.where(position < length, 0.0, masked).astype(low)


def strip_columns(total, first, width):
    return [
        pl.ds(pl.multiple_of(total - tile - row + first, tile), width)
        for row in range(0, total, tile)
    ]


def add_bias(products, strip_ref, head, columns):
    return jnp.concatenate(
        [
            products[block * tile : (block + 1) * tile] + strip_ref[head, :, where]
            for block, where in enumerate(columns)
        ],
        axis=0,
    )


def forward_kernel(
    length_ref, query_ref, key_ref, value_ref, strip_ref, context_ref, total_ref, top_ref, *, step
):
    length = length_ref[0]
    total = query_ref.shape[0]
    masks = key_masks(total, length)
    ones = jnp.ones((step, tile), low)
    keys = [one_head(key_ref[...], head, masks) for head in (0, 1)]
    values = [one_head(value_ref[...], head).astype(wide).T.astype(low) for head in (0, 1)]

    def body(index, tops):
        first = pl.multiple_of(index * step, step)
        queries = query_ref[pl.ds(first, step), :]
        columns = strip_columns(total, first, step)
        query_okay = first + lax.broadcasted_iota(jnp.int32, (1, step), 1) < length
        context = None
        peaks = []
        for head in (0, 1):
            products = dot(keys[head], one_head(queries, head, ones), 1, 1)
            scores = add_bias(products, strip_ref, head, columns)
            row_max = jnp.max(scores, axis=0, keepdims=True)
            exponent = jnp.exp(scores - row_max)
            summed = jnp.sum(exponent, axis=0, keepdims=True)
            part = dot(values[head], exponent.astype(low), 1, 0) * (1.0 / summed)
            context = part if context is None else context + part
            total_ref[0, head : head + 1, pl.ds(first, step)] = row_max + jnp.log(summed)
            peaks.append(
                jnp.where(query_okay, jnp.max(products, axis=0, keepdims=True), masked)
            )
        context_ref[pl.ds(first, step), :] = context.T.astype(low)
        return tuple(jnp.maximum(top, peak) for top, peak in zip(tops, peaks))

    tops = lax.fori_loop(
        0, total // step, body, tuple(jnp.full((1, step), masked, wide) for _ in (0, 1))
    )
    for head in (0, 1):
        peak = jnp.max(tops[head], axis=1, keepdims=True)
        top_ref[0, head : head + 1, :] = jnp.broadcast_to(peak, (1, tile))


def attention_forward(length, qkv, strips, step=512):
    total = qkv.shape[0]
    pairs = qkv.shape[1] // (3 * tile)
    strip_width = strips.shape[2]

    def columns(which):
        return pl.BlockSpec((total, tile), lambda p, _: (0, which * pairs + p))

    return pl.pallas_call(
        functools.partial(forward_kernel, step=step),
        grid_spec=pltpu.PrefetchScalarGridSpec(
            num_scalar_prefetch=1,
            grid=(pairs,),
            in_specs=[
                columns(0),
                columns(1),
                columns(2),
                pl.BlockSpec((2, tile, strip_width), lambda p, _: (p, 0, 0)),
            ],
            out_specs=[
                columns(0),
                pl.BlockSpec((1, 2, total), lambda p, _: (p, 0, 0)),
                pl.BlockSpec((1, 2, tile), lambda p, _: (p, 0, 0)),
            ],
        ),
        out_shape=[
            jax.ShapeDtypeStruct((total, pairs * tile), low),
            jax.ShapeDtypeStruct((pairs, 2, total), wide),
            jax.ShapeDtypeStruct((pairs, 2, tile), wide),
        ],
        compiler_params=pltpu.CompilerParams(vmem_limit_bytes=48 << 20),
        cost_estimate=pl.CostEstimate(
            flops=40_000_000_000, bytes_accessed=12 << 20, transcendentals=0
        ),
        name="attention_forward",
    )(length, qkv, qkv, qkv, strips)


def backward_kernel(
    length_ref,
    query_ref,
    key_ref,
    value_ref,
    context_ref,
    grad_ref,
    total_ref,
    strip_ref,
    query_grad_ref,
    key_grad_ref,
    value_grad_ref,
    strip_grad_ref,
    key_sum,
    value_sum,
    *,
    step,
):
    length = length_ref[0]
    total = query_ref.shape[0]
    masks = key_masks(total, length)
    ones = jnp.ones((step, tile), low)
    keys = [one_head(key_ref[...], head, masks) for head in (0, 1)]
    plain_keys = [one_head(key_ref[...], head) for head in (0, 1)]
    values = [one_head(value_ref[...], head) for head in (0, 1)]
    key_sum[...] = jnp.zeros_like(key_sum)
    value_sum[...] = jnp.zeros_like(value_sum)
    strip_grad_ref[...] = jnp.zeros_like(strip_grad_ref)

    def body(index, carry):
        first = pl.multiple_of(index * step, step)
        queries = query_ref[pl.ds(first, step), :]
        grads = grad_ref[pl.ds(first, step), :]
        columns = strip_columns(total, first, step)
        inner = grads.astype(wide) * context_ref[pl.ds(first, step), :].astype(wide)
        query_grad = None
        for head in (0, 1):
            head_grads = one_head(grads, head)
            pick = one_head(jnp.ones((8, tile), wide), head)
            row_inner = lax.dot_general(
                pick,
                inner,
                (((1,), (1,)), ((), ())),
                precision=lax.Precision.HIGHEST,
                preferred_element_type=wide,
            )[:1]
            log_total = total_ref[0, head : head + 1, pl.ds(first, step)]
            products = dot(keys[head], one_head(queries, head, ones), 1, 1)
            probs = jnp.exp(add_bias(products, strip_ref, head, columns) - log_total)
            value_sum[...] += dot(probs.astype(low), head_grads, 1, 0)
            score_grad = probs * (dot(values[head], head_grads, 1, 1) - row_inner)
            for block, where in enumerate(columns):
                strip_grad_ref[head, :, where] += score_grad[block * tile : (block + 1) * tile]
            score_low = score_grad.astype(low)
            key_sum[...] += dot(score_low, one_head(queries, head), 1, 0)
            part = dot(score_low, plain_keys[head], 0, 0)
            query_grad = part if query_grad is None else query_grad + part
        query_grad_ref[pl.ds(first, step), :] = query_grad.astype(low)
        return carry

    lax.fori_loop(0, total // step, body, 0)
    key_grad_ref[...] = key_sum[...].astype(low)
    value_grad_ref[...] = value_sum[...].astype(low)


def attention_backward(length, qkv, context, context_grad, log_totals, strips, step=256):
    total = qkv.shape[0]
    pairs = qkv.shape[1] // (3 * tile)
    strip_width = strips.shape[2]

    def columns(which):
        return pl.BlockSpec((total, tile), lambda p, _: (0, which * pairs + p))

    strip_block = pl.BlockSpec((2, tile, strip_width), lambda p, _: (p, 0, 0))
    return pl.pallas_call(
        functools.partial(backward_kernel, step=step),
        grid_spec=pltpu.PrefetchScalarGridSpec(
            num_scalar_prefetch=1,
            grid=(pairs,),
            in_specs=[
                columns(0),
                columns(1),
                columns(2),
                columns(0),
                columns(0),
                pl.BlockSpec((1, 2, total), lambda p, _: (p, 0, 0)),
                strip_block,
            ],
            out_specs=[columns(0), columns(0), columns(0), strip_block],
            scratch_shapes=[pltpu.VMEM((total, tile), wide), pltpu.VMEM((total, tile), wide)],
        ),
        out_shape=[jax.ShapeDtypeStruct((total, pairs * tile), low)] * 3
        + [jax.ShapeDtypeStruct((2 * pairs, tile, strip_width), wide)],
        compiler_params=pltpu.CompilerParams(vmem_limit_bytes=48 << 20),
        cost_estimate=pl.CostEstimate(
            flops=60_000_000_000, bytes_accessed=24 << 20, transcendentals=0
        ),
        name="attention_backward",
    )(length, qkv, qkv, qkv, context, context_grad, log_totals, strips)


def gelu_and_slope(values):
    distance = jnp.abs(values) * math.sqrt(0.5)
    ratio = 1.0 / (1.0 + 0.3275911 * distance)
    density = jnp.exp(-distance * distance)
    poly = 1.061405429 * ratio - 1.453152027
    poly = poly * ratio + 1.421413741
    poly = poly * ratio - 0.284496736
    poly = poly * ratio + 0.254829592
    tail = (0.5 * ratio) * poly * density
    cumulative = jnp.where(values >= 0, 1.0 - tail, tail)
    slope = cumulative + values * density * (1.0 / math.sqrt(2.0 * math.pi))
    return values * cumulative, slope


def feed_forward_kernel(
    normed_ref,
    normed_t_ref,
    grad_ref,
    grad_t_ref,
    expand_ref,
    contract_ref,
    mixed_ref,
    normed_grad_ref,
    expand_grad_ref,
    contract_grad_ref,
    mixed_sum,
    normed_sum,
):
    index = pl.program_id(0)
    pre_act = dot(normed_ref[...], expand_ref[...], 1, 0)
    act_grad = dot(grad_ref[...], contract_ref[...], 1, 0).astype(low).astype(wide)
    activated, slope = gelu_and_slope(pre_act)
    activated = activated.astype(low)
    pre_grad = (act_grad * slope).astype(low)
    contract_grad_ref[...] = dot(grad_t_ref[...], activated, 1, 0).astype(low)
    expand_grad_ref[...] = dot(normed_t_ref[...], pre_grad, 1, 0).astype(low)
    mixed = dot(activated, contract_ref[...], 1, 1)
    normed_grad = dot(pre_grad, expand_ref[...], 1, 1)

    @pl.when(index == 0)
    def _():
        mixed_sum[...] = mixed
        normed_sum[...] = normed_grad

    @pl.when(index > 0)
    def _():
        mixed_sum[...] += mixed
        normed_sum[...] += normed_grad

    @pl.when(index == pl.num_programs(0) - 1)
    def _():
        mixed_ref[...] = mixed_sum[...].astype(low)
        normed_grad_ref[...] = normed_sum[...].astype(low)


def feed_forward(normed, normed_t, grad, grad_t, expand, contract, step=512):
    rows, width = normed.shape
    hidden = expand.shape[1]
    whole = pl.BlockSpec((rows, width), lambda i: (0, 0), pipeline_mode=pl.Buffered(1))
    whole_t = pl.BlockSpec((width, rows), lambda i: (0, 0), pipeline_mode=pl.Buffered(1))
    block = pl.BlockSpec((width, step), lambda i: (0, i))
    whole_out = pl.BlockSpec((rows, width), lambda i: (0, 0))
    return pl.pallas_call(
        feed_forward_kernel,
        grid=(hidden // step,),
        in_specs=[whole, whole_t, whole, whole_t, block, block],
        out_specs=[whole_out, whole_out, block, block],
        out_shape=[jax.ShapeDtypeStruct((rows, width), low)] * 2
        + [jax.ShapeDtypeStruct((width, hidden), low)] * 2,
        scratch_shapes=[pltpu.VMEM((rows, width), wide), pltpu.VMEM((rows, width), wide)],
        compiler_params=pltpu.CompilerParams(vmem_limit_bytes=56 << 20),
        cost_estimate=pl.CostEstimate(
            flops=12 * rows * width * hidden * 3 // 2, bytes_accessed=40 << 20, transcendentals=0
        ),
        name="feed_forward",
    )(normed, normed_t, grad, grad_t, expand, contract)


def normalize(values):
    scaled = lax.rsqrt(jnp.mean(values * values, axis=-1, keepdims=True) + epsilon)
    return (values * scaled, scaled)


def normalize_back(values, scaled, upstream):
    unit_rows = values * scaled
    return scaled * (upstream - unit_rows * jnp.mean(upstream * unit_rows, axis=-1, keepdims=True))


def scaled_rows(weight, scaling):
    return (scaling.astype(wide)[:, None] * weight.astype(wide)).astype(low)


def take(array, index):
    return lax.dynamic_index_in_dim(array, index, 0, keepdims=False)


def put(array, part, index):
    return lax.dynamic_update_slice_in_dim(array, part[None], index, 0)


def after(array, *others):
    return lax.optimization_barrier((array, *others))[0]


class Links:
    def __init__(self):
        self.shards = lax.axis_size("fsdp")
        self.depth = lax.axis_size("ctx")
        self.shard = lax.axis_index("fsdp")
        self.level = lax.axis_index("ctx")
        self.chips = self.shards // 2
        self.chip = self.shard // 2
        self.core = self.shard % 2
        self.groups = [list(range(core, self.shards, 2)) for core in (0, 1)]

    def sibling(self, array):
        return lax.ppermute(array, "fsdp", [(i, i ^ 1) for i in range(self.shards)])

    def across(self, array, bit):
        return lax.ppermute(array, "fsdp", [(i, i ^ (2 * bit)) for i in range(self.shards)])

    def vertical(self, array, distance):
        count = self.depth
        return lax.ppermute(array, "ctx", [(i, (i + distance) % count) for i in range(count)])

    def in_order(self, mine, other, axis):
        return jnp.concatenate(
            [jnp.where(self.core == 0, mine, other), jnp.where(self.core == 0, other, mine)],
            axis=axis,
        )

    def gather(self, shard, behind=()):
        if self.chips != 4:
            return (
                lax.all_gather(shard, "fsdp", axis=0, tiled=True, axis_index_groups=self.groups),
                (),
            )
        if behind:
            shard = after(shard, *behind)
        half = shard.shape[0] // 2
        first = self.across(shard, 1)
        second = self.across(shard, 2)
        upper = self.across(first[:half], 2)
        lower = self.across(second[half:], 1)
        whole = jnp.zeros((4,) + shard.shape, shard.dtype)
        whole = put(whole, shard, self.chip)
        whole = put(whole, first, self.chip ^ 1)
        whole = put(whole, second, self.chip ^ 2)
        whole = put(whole, jnp.concatenate([upper, lower], axis=0), self.chip ^ 3)
        return whole.reshape((4 * shard.shape[0],) + shard.shape[1:]), (first, second)

    def scatter(self, terms, behind=()):
        if self.chips != 4:
            summed = lax.psum_scatter(
                terms, "fsdp", scatter_dimension=0, tiled=True, axis_index_groups=self.groups
            )
            return summed.astype(wide), ()
        if behind:
            terms = after(terms, *behind)
        parts = terms.reshape((4, terms.shape[0] // 4) + terms.shape[1:])
        half = parts.shape[1] // 2
        corner = take(parts, self.chip ^ 3)
        upper = self.across(corner[:half], 1)
        lower = self.across(corner[half:], 2)
        beside = take(parts, self.chip ^ 1).astype(wide)
        below = take(parts, self.chip ^ 2).astype(wide)
        beside = jnp.concatenate([beside[:half], beside[half:] + lower.astype(wide)], axis=0)
        below = jnp.concatenate([below[:half] + upper.astype(wide), below[half:]], axis=0)
        first = self.across(beside.astype(low), 1)
        second = self.across(below.astype(low), 2)
        own = take(parts, self.chip).astype(wide)
        return own + first.astype(wide) + second.astype(wide), (first, second)

    def level_sum(self, terms):
        count = self.depth
        parts = terms.reshape((count, terms.shape[0] // count) + terms.shape[1:])
        total = take(parts, self.level).astype(wide)
        for distance in range(1, count):
            part = take(parts, (self.level + distance) % count)
            total = total + self.vertical(part, distance).astype(wide)
        total = total.astype(low)
        whole = put(jnp.zeros_like(parts), total, self.level)
        for distance in range(1, count):
            part = self.vertical(total, distance)
            whole = put(whole, part, (self.level - distance) % count)
        return whole.reshape(terms.shape)

    def exchange_rows(self, rows):
        parts = rows.reshape((2, rows.shape[0] // 2) + rows.shape[1:])
        mine = take(parts, self.core)
        other = self.sibling(take(parts, 1 - self.core))
        return self.in_order(mine[None], other[None], 0)

    def trade(self, array, outward, swapped):
        pairs = []
        for level in range(self.depth):
            for shard in range(self.shards):
                chip, core = divmod(shard, 2)
                side, odd = divmod(level, 2)
                slot = odd if not swapped else 1 - odd
                held = level * self.shards + shard
                worked = (2 * core + slot) * self.shards + 2 * chip + side
                pairs.append((held, worked) if outward else (worked, held))
        return lax.ppermute(array, ("ctx", "fsdp"), pairs)

    def to_slots(self, blocks):
        odd = self.level % 2
        first = self.trade(take(blocks, odd), True, False)
        second = self.trade(take(blocks, 1 - odd), True, True)
        flip = odd == 0
        return jnp.concatenate(
            [jnp.where(flip, first, second), jnp.where(flip, second, first)], axis=0
        )

    def from_slots(self, rows):
        odd = self.level % 2
        blocks = rows.reshape((2, rows.shape[0] // 2) + rows.shape[1:])
        first = self.trade(take(blocks, odd), False, False)
        second = self.trade(take(blocks, 1 - odd), False, True)
        flip = odd == 0
        return jnp.stack([jnp.where(flip, first, second), jnp.where(flip, second, first)])


def local(
    tokens,
    cotangent,
    sequence_lengths,
    slot_sequence,
    offset_bucket,
    first_gain,
    second_gain,
    query_weight,
    key_weight,
    value_weight,
    output_weight,
    expand_weight,
    contract_weight,
    bias_table,
    clip_limit,
):
    links = Links()
    core = links.core
    held_count, local_length, model_width = tokens.shape
    total_length = local_length * links.depth
    half_length = total_length // 2
    bucket_count, head_count = bias_table.shape
    inner_width = query_weight.shape[1]
    head_size = inner_width // head_count
    hidden_width = expand_weight.shape[1]
    row_share = query_weight.shape[0]
    own_heads = head_count // 2
    own_inner = inner_width // 2
    own_hidden = hidden_width // 2
    slot_count = slot_sequence.shape[0]
    assert held_count == 2 and links.depth == 4

    slots = jnp.arange(slot_count)
    slot = links.chip * (2 * held_count) + links.level
    sequence = jnp.sum(jnp.where(slots == slot, slot_sequence, 0))
    length = jnp.sum(jnp.where(slots == sequence, sequence_lengths, 0))
    row_okay = jnp.arange(total_length)[:, None] < length

    stacked = jnp.concatenate([query_weight, key_weight, value_weight], axis=1)
    effective_qkv = scaled_rows(stacked, first_gain)
    effective_expand = scaled_rows(expand_weight, second_gain)

    def side_columns(which):
        def cut(weight, blocks):
            parts = weight.reshape(row_share, blocks, 2, weight.shape[1] // (2 * blocks))
            return lax.dynamic_index_in_dim(parts, which, 2, keepdims=False).reshape(row_share, -1)

        return jnp.concatenate(
            [
                cut(effective_qkv, 3),
                cut(output_weight, 1),
                cut(effective_expand, 1),
                cut(contract_weight, 1),
            ],
            axis=1,
        )

    mine = side_columns(core)
    other = links.sibling(side_columns(1 - core))
    chip_rows = links.in_order(mine, other, 0)
    cuts = [0, 3 * own_inner, 4 * own_inner, 4 * own_inner + own_hidden]
    cuts.append(cuts[-1] + own_hidden)
    qkv_shard, output_shard, expand_shard, contract_shard = (
        chip_rows[:, start:stop] for start, stop in zip(cuts[:-1], cuts[1:])
    )

    token_half = links.to_slots(tokens)
    token_low = links.in_order(token_half, links.sibling(token_half), 0)
    cotangent_half = links.to_slots(after(cotangent, token_low))
    cotangent_low = links.in_order(cotangent_half, links.sibling(cotangent_half), 0)

    whole_qkv, sent = links.gather(qkv_shard)
    whole_output, sent = links.gather(output_shard, sent)
    whole_expand, sent = links.gather(expand_shard, sent)
    whole_contract, sent = links.gather(contract_shard, sent)

    line_width = 2 * total_length
    falling = jnp.concatenate([jnp.flip(offset_bucket), jnp.full((1,), -1, jnp.int32)])
    matching = falling[:, None] == jnp.arange(bucket_count)[None, :]
    own_table = lax.dynamic_slice_in_dim(bias_table, core * own_heads, own_heads, 1)
    lines = dot(own_table, matching.astype(low), 0, 1)
    strips = bias_strips(lines.reshape(own_heads, 1, line_width))

    token_rows = token_low.astype(wide)
    unit_one, scale_one = normalize(token_rows)
    normed_one = unit_one.astype(low)
    qkv = dot(normed_one, whole_qkv, 1, 0).astype(low)
    length_line = length.reshape(1).astype(jnp.int32)
    context, log_totals, tops = attention_forward(length_line, qkv, strips)
    attended = dot(context, whole_output, 1, 1).astype(low)
    hidden_one = token_rows + (
        attended.astype(wide) + links.sibling(attended).astype(wide)
    )
    unit_two, scale_two = normalize(hidden_one)
    normed_two = unit_two.astype(low)
    out_low = jnp.where(row_okay, cotangent_low, 0)
    mixed, normed_two_part, expand_terms, contract_terms = feed_forward(
        normed_two, normed_two.T, out_low, out_low.T, whole_expand, whole_contract
    )
    normed_two_grad = normed_two_part.astype(wide) + links.sibling(normed_two_part).astype(wide)
    hidden_grad = out_low.astype(wide) + normalize_back(hidden_one, scale_two, normed_two_grad)
    attended_grad = hidden_grad.astype(low)

    def own_half(array, which):
        return lax.dynamic_slice_in_dim(array, which * half_length, half_length, 0)

    mixed_half = own_half(mixed, core).astype(wide) + links.sibling(
        own_half(mixed, 1 - core)
    ).astype(wide)
    result_half = jnp.where(
        own_half(row_okay, core), own_half(hidden_one, core) + mixed_half, 0.0
    ).astype(low)
    result = links.from_slots(result_half)

    context_grad = dot(attended_grad, whole_output, 1, 0).astype(low)
    output_terms = dot(attended_grad, context, 0, 0).astype(low)
    query_grad, key_grad, value_grad, strip_grads = attention_backward(
        length_line, qkv, context, context_grad, log_totals, strips
    )
    qkv_grad = jnp.concatenate([query_grad, key_grad, value_grad], axis=1)
    qkv_terms = dot(normed_one, qkv_grad, 0, 0).astype(low)
    normed_one_part = dot(qkv_grad, whole_qkv, 1, 1)
    normed_one_grad = own_half(normed_one_part, core) + links.sibling(
        own_half(normed_one_part, 1 - core).astype(low)
    ).astype(wide)
    input_half = own_half(hidden_grad, core) + normalize_back(
        own_half(token_rows, core), own_half(scale_one, core), normed_one_grad
    )
    input_gradient = links.from_slots(input_half.astype(low)).astype(wide)

    contract_sum, sent = links.scatter(contract_terms)
    expand_sum, sent = links.scatter(expand_terms, sent)
    output_sum, sent = links.scatter(output_terms, sent)
    qkv_sum, sent = links.scatter(qkv_terms, sent)
    gathered, _ = links.gather(result.reshape(held_count * local_length, model_width), sent)

    def finished(summed):
        parts = links.exchange_rows(summed.astype(low))
        flat = parts.reshape(2 * row_share, -1)
        return links.level_sum(flat).reshape(parts.shape)

    contract_parts = finished(contract_sum)
    expand_parts = finished(expand_sum)
    output_parts = finished(output_sum)
    qkv_parts = finished(qkv_sum)

    def columns_of(parts, blocks):
        width = parts.shape[2] // blocks
        shaped = parts.reshape(2, row_share, blocks, width).transpose(1, 2, 0, 3)
        return shaped.reshape(row_share, 2 * blocks * width).astype(wide)

    contract_weight_gradient = columns_of(contract_parts, 1)
    raw_two = columns_of(expand_parts, 1)
    output_weight_gradient = columns_of(output_parts, 1)
    raw_one = columns_of(qkv_parts, 3)
    first_scale = first_gain.astype(wide)[:, None]
    second_scale = second_gain.astype(wide)[:, None]
    first_gain_gradient = jnp.sum(stacked.astype(wide) * raw_one, axis=1)
    second_gain_gradient = jnp.sum(expand_weight.astype(wide) * raw_two, axis=1)
    query_weight_gradient = first_scale * raw_one[:, :inner_width]
    key_weight_gradient = first_scale * raw_one[:, inner_width : 2 * inner_width]
    value_weight_gradient = first_scale * raw_one[:, 2 * inner_width :]
    expand_weight_gradient = second_scale * raw_two

    gathered = gathered.reshape(links.chips * held_count, local_length, model_width)

    def slot_of(wanted):
        return jnp.sum(jnp.where(slot_sequence == wanted, slots, 0))

    def place_of(found):
        return (found // 4) * held_count + found % 2

    own_slots = [slot_of(links.shard * held_count + row) for row in range(held_count)]
    other_slots = [slot_of((links.shard ^ 1) * held_count + row) for row in range(held_count)]
    from_other = links.sibling(jnp.stack([take(gathered, place_of(s)) for s in other_slots]))
    output = jnp.stack(
        [
            jnp.where((s // 2) % 2 == core, take(gathered, place_of(s)), from_other[row])
            for row, s in enumerate(own_slots)
        ]
    )

    diagonals = diagonal_sums(strip_grads).reshape(own_heads, line_width)
    table_grad = lax.dot_general(
        diagonals,
        matching.astype(wide),
        (((1,), (0,)), ((), ())),
        precision=lax.Precision.HIGHEST,
        preferred_element_type=wide,
    )
    small = jnp.concatenate([table_grad, tops.reshape(own_heads, -1)[:, :1]], axis=1)

    def joined(left, right):
        return jnp.concatenate(
            [
                left[:, :bucket_count] + right[:, :bucket_count],
                jnp.maximum(left[:, bucket_count:], right[:, bucket_count:]),
            ],
            axis=1,
        )

    bit = 1
    while bit < links.chips:
        small = joined(small, links.across(small, bit))
        bit *= 2
    bit = 1
    while bit < links.depth:
        swap = [(i, i ^ bit) for i in range(links.depth)]
        small = joined(small, lax.ppermute(small, "ctx", swap))
        bit *= 2
    small = links.in_order(small, links.sibling(small), 0)
    table_rows = bucket_count // links.shards
    bias_table_gradient = lax.dynamic_slice_in_dim(
        small[:, :bucket_count].T, links.shard * table_rows, table_rows, 0
    )
    largest = small[:, bucket_count]
    shrink = clip_limit / jnp.maximum(clip_limit, largest)
    column_scale = jnp.repeat(jnp.sqrt(shrink), head_size)
    new_query_weight = query_weight.astype(wide) * column_scale[None, :]
    new_key_weight = key_weight.astype(wide) * column_scale[None, :]
    return (
        output,
        input_gradient,
        first_gain_gradient,
        second_gain_gradient,
        query_weight_gradient,
        key_weight_gradient,
        value_weight_gradient,
        output_weight_gradient,
        expand_weight_gradient,
        contract_weight_gradient,
        bias_table_gradient,
        largest,
        new_query_weight,
        new_key_weight,
    )


def solution(mesh):
    return jax.shard_map(
        local,
        mesh=mesh,
        in_specs=(
            P("fsdp", "ctx", None),
            P("fsdp", "ctx", None),
            P(),
            P(),
            P(),
            P("fsdp"),
            P("fsdp"),
            P("fsdp", None),
            P("fsdp", None),
            P("fsdp", None),
            P("fsdp", None),
            P("fsdp", None),
            P("fsdp", None),
            P(),
            P(),
        ),
        out_specs=(
            P("fsdp", "ctx", None),
            P("fsdp", "ctx", None),
            P("fsdp"),
            P("fsdp"),
            P("fsdp", None),
            P("fsdp", None),
            P("fsdp", None),
            P("fsdp", None),
            P("fsdp", None),
            P("fsdp", None),
            P("fsdp", None),
            P(),
            P("fsdp", None),
            P("fsdp", None),
        ),
        check_vma=False,
    )
```

```python
import functools
import math

import jax
import jax.numpy as jnp
from jax import lax
from jax.experimental import pallas as pl
from jax.experimental.pallas import tpu as pltpu
from jax.sharding import PartitionSpec as P

epsilon = 1e-06
masked = -1e30
tile = 128
half_tile = 64
wide = jnp.float32
low = jnp.bfloat16


def dot(left, right, left_dim, right_dim):
    return lax.dot_general(
        left, right, (((left_dim,), (right_dim,)), ((), ())), preferred_element_type=wide
    )


def strip_kernel(line_ref, strip_ref):
    width = line_ref.shape[-1]
    rows = jnp.broadcast_to(line_ref[0], (tile, width))
    strip_ref[0] = pltpu.roll(rows, width - (tile - 1), 1, stride=1, stride_axis=0)


def bias_strips(lines):
    heads, _, width = lines.shape
    return pl.pallas_call(
        strip_kernel,
        grid=(heads,),
        in_specs=[pl.BlockSpec((1, 1, width), lambda h: (h, 0, 0))],
        out_specs=pl.BlockSpec((1, tile, width), lambda h: (h, 0, 0)),
        out_shape=jax.ShapeDtypeStruct((heads, tile, width), wide),
        compiler_params=pltpu.CompilerParams(vmem_limit_bytes=32 << 20),
        name="bias_strips",
    )(lines)


def diagonal_kernel(strip_ref, line_ref):
    strip = strip_ref[0]
    rows = tile
    while rows > 1:
        rows //= 2
        strip = pltpu.roll(strip[:rows], rows, 1) + strip[rows:]
    line_ref[0] = strip


def diagonal_sums(strips):
    heads, _, width = strips.shape
    return pl.pallas_call(
        diagonal_kernel,
        grid=(heads,),
        in_specs=[pl.BlockSpec((1, tile, width), lambda h: (h, 0, 0))],
        out_specs=pl.BlockSpec((1, 1, width), lambda h: (h, 0, 0)),
        out_shape=jax.ShapeDtypeStruct((heads, 1, width), wide),
        compiler_params=pltpu.CompilerParams(vmem_limit_bytes=32 << 20),
        name="diagonal_sums",
    )(strips)


def one_head(block, head, extra=None):
    lane = lax.broadcasted_iota(jnp.int32, block.shape, 1)
    kept = jnp.where((lane >= half_tile) if head else (lane < half_tile), block, 0)
    if extra is None:
        return kept
    return jnp.where(lane == (0 if head else half_tile), extra, kept)


def key_masks(total, length):
    position = lax.broadcasted_iota(jnp.int32, (total, tile), 0)
    return jnp.where(position < length, 0.0, masked).astype(low)


def strip_columns(total, first, width):
    return [
        pl.ds(pl.multiple_of(total - tile - row + first, tile), width)
        for row in range(0, total, tile)
    ]


def add_bias(products, strip_ref, head, columns):
    return jnp.concatenate(
        [
            products[block * tile : (block + 1) * tile] + strip_ref[head, :, where]
            for block, where in enumerate(columns)
        ],
        axis=0,
    )


def forward_kernel(
    length_ref, query_ref, key_ref, value_ref, strip_ref, context_ref, total_ref, top_ref, *, step
):
    length = length_ref[0]
    total = query_ref.shape[0]
    masks = key_masks(total, length)
    ones = jnp.ones((step, tile), low)
    keys = [one_head(key_ref[...], head, masks) for head in (0, 1)]
    values = [one_head(value_ref[...], head).astype(wide).T.astype(low) for head in (0, 1)]

    def body(index, tops):
        first = pl.multiple_of(index * step, step)
        queries = query_ref[pl.ds(first, step), :]
        columns = strip_columns(total, first, step)
        query_okay = first + lax.broadcasted_iota(jnp.int32, (1, step), 1) < length
        context = None
        peaks = []
        for head in (0, 1):
            products = dot(keys[head], one_head(queries, head, ones), 1, 1)
            scores = add_bias(products, strip_ref, head, columns)
            row_max = jnp.max(scores, axis=0, keepdims=True)
            exponent = jnp.exp(scores - row_max)
            summed = jnp.sum(exponent, axis=0, keepdims=True)
            part = dot(values[head], exponent.astype(low), 1, 0) * (1.0 / summed)
            context = part if context is None else context + part
            total_ref[0, head : head + 1, pl.ds(first, step)] = row_max + jnp.log(summed)
            peaks.append(
                jnp.where(query_okay, jnp.max(products, axis=0, keepdims=True), masked)
            )
        context_ref[pl.ds(first, step), :] = context.T.astype(low)
        return tuple(jnp.maximum(top, peak) for top, peak in zip(tops, peaks))

    tops = lax.fori_loop(
        0, total // step, body, tuple(jnp.full((1, step), masked, wide) for _ in (0, 1))
    )
    for head in (0, 1):
        peak = jnp.max(tops[head], axis=1, keepdims=True)
        top_ref[0, head : head + 1, :] = jnp.broadcast_to(peak, (1, tile))


def attention_forward(length, qkv, strips, step=512):
    total = qkv.shape[0]
    pairs = qkv.shape[1] // (3 * tile)
    strip_width = strips.shape[2]

    def columns(which):
        return pl.BlockSpec((total, tile), lambda p, _: (0, which * pairs + p))

    return pl.pallas_call(
        functools.partial(forward_kernel, step=step),
        grid_spec=pltpu.PrefetchScalarGridSpec(
            num_scalar_prefetch=1,
            grid=(pairs,),
            in_specs=[
                columns(0),
                columns(1),
                columns(2),
                pl.BlockSpec((2, tile, strip_width), lambda p, _: (p, 0, 0)),
            ],
            out_specs=[
                columns(0),
                pl.BlockSpec((1, 2, total), lambda p, _: (p, 0, 0)),
                pl.BlockSpec((1, 2, tile), lambda p, _: (p, 0, 0)),
            ],
        ),
        out_shape=[
            jax.ShapeDtypeStruct((total, pairs * tile), low),
            jax.ShapeDtypeStruct((pairs, 2, total), wide),
            jax.ShapeDtypeStruct((pairs, 2, tile), wide),
        ],
        compiler_params=pltpu.CompilerParams(vmem_limit_bytes=48 << 20),
        cost_estimate=pl.CostEstimate(
            flops=40_000_000_000, bytes_accessed=12 << 20, transcendentals=0
        ),
        name="attention_forward",
    )(length, qkv, qkv, qkv, strips)


def backward_kernel(
    length_ref,
    query_ref,
    key_ref,
    value_ref,
    context_ref,
    grad_ref,
    total_ref,
    strip_ref,
    query_grad_ref,
    key_grad_ref,
    value_grad_ref,
    strip_grad_ref,
    key_sum,
    value_sum,
    *,
    step,
):
    length = length_ref[0]
    total = query_ref.shape[0]
    masks = key_masks(total, length)
    ones = jnp.ones((step, tile), low)
    keys = [one_head(key_ref[...], head, masks) for head in (0, 1)]
    plain_keys = [one_head(key_ref[...], head) for head in (0, 1)]
    values = [one_head(value_ref[...], head) for head in (0, 1)]
    key_sum[...] = jnp.zeros_like(key_sum)
    value_sum[...] = jnp.zeros_like(value_sum)
    strip_grad_ref[...] = jnp.zeros_like(strip_grad_ref)

    def body(index, carry):
        first = pl.multiple_of(index * step, step)
        queries = query_ref[pl.ds(first, step), :]
        grads = grad_ref[pl.ds(first, step), :]
        columns = strip_columns(total, first, step)
        inner = grads.astype(wide) * context_ref[pl.ds(first, step), :].astype(wide)
        query_grad = None
        for head in (0, 1):
            head_grads = one_head(grads, head)
            pick = one_head(jnp.ones((8, tile), wide), head)
            row_inner = lax.dot_general(
                pick,
                inner,
                (((1,), (1,)), ((), ())),
                precision=lax.Precision.HIGHEST,
                preferred_element_type=wide,
            )[:1]
            log_total = total_ref[0, head : head + 1, pl.ds(first, step)]
            products = dot(keys[head], one_head(queries, head, ones), 1, 1)
            probs = jnp.exp(add_bias(products, strip_ref, head, columns) - log_total)
            value_sum[...] += dot(probs.astype(low), head_grads, 1, 0)
            score_grad = probs * (dot(values[head], head_grads, 1, 1) - row_inner)
            for block, where in enumerate(columns):
                strip_grad_ref[head, :, where] += score_grad[block * tile : (block + 1) * tile]
            score_low = score_grad.astype(low)
            key_sum[...] += dot(score_low, one_head(queries, head), 1, 0)
            part = dot(score_low, plain_keys[head], 0, 0)
            query_grad = part if query_grad is None else query_grad + part
        query_grad_ref[pl.ds(first, step), :] = query_grad.astype(low)
        return carry

    lax.fori_loop(0, total // step, body, 0)
    key_grad_ref[...] = key_sum[...].astype(low)
    value_grad_ref[...] = value_sum[...].astype(low)


def attention_backward(length, qkv, context, context_grad, log_totals, strips, step=256):
    total = qkv.shape[0]
    pairs = qkv.shape[1] // (3 * tile)
    strip_width = strips.shape[2]

    def columns(which):
        return pl.BlockSpec((total, tile), lambda p, _: (0, which * pairs + p))

    strip_block = pl.BlockSpec((2, tile, strip_width), lambda p, _: (p, 0, 0))
    return pl.pallas_call(
        functools.partial(backward_kernel, step=step),
        grid_spec=pltpu.PrefetchScalarGridSpec(
            num_scalar_prefetch=1,
            grid=(pairs,),
            in_specs=[
                columns(0),
                columns(1),
                columns(2),
                columns(0),
                columns(0),
                pl.BlockSpec((1, 2, total), lambda p, _: (p, 0, 0)),
                strip_block,
            ],
            out_specs=[columns(0), columns(0), columns(0), strip_block],
            scratch_shapes=[pltpu.VMEM((total, tile), wide), pltpu.VMEM((total, tile), wide)],
        ),
        out_shape=[jax.ShapeDtypeStruct((total, pairs * tile), low)] * 3
        + [jax.ShapeDtypeStruct((2 * pairs, tile, strip_width), wide)],
        compiler_params=pltpu.CompilerParams(vmem_limit_bytes=48 << 20),
        cost_estimate=pl.CostEstimate(
            flops=60_000_000_000, bytes_accessed=24 << 20, transcendentals=0
        ),
        name="attention_backward",
    )(length, qkv, qkv, qkv, context, context_grad, log_totals, strips)


def gelu_and_slope(values):
    distance = jnp.abs(values) * math.sqrt(0.5)
    ratio = 1.0 / (1.0 + 0.3275911 * distance)
    density = jnp.exp(-distance * distance)
    poly = 1.061405429 * ratio - 1.453152027
    poly = poly * ratio + 1.421413741
    poly = poly * ratio - 0.284496736
    poly = poly * ratio + 0.254829592
    tail = (0.5 * ratio) * poly * density
    cumulative = jnp.where(values >= 0, 1.0 - tail, tail)
    slope = cumulative + values * density * (1.0 / math.sqrt(2.0 * math.pi))
    return values * cumulative, slope


def block_copies(index_ref, offset, pieces, target, semaphores):
    copies = []
    for number, piece in enumerate(pieces):
        rows = piece.shape[-2]
        where = pl.ds(pl.multiple_of(index_ref[offset + number] * rows, rows), rows)
        place = target.at[where, :] if len(piece.shape) == 2 else target.at[:, where, :]
        copies.append(pltpu.make_async_copy(piece, place, semaphores.at[offset + number]))
    return copies


anywhere = pl.BlockSpec(memory_space=pl.ANY)


def cost(flops, moved):
    return pl.CostEstimate(flops=flops, bytes_accessed=moved, transcendentals=0)


def side_kernel(
    core_ref, q_ref, k_ref, v_ref, o_ref, e_ref, c_ref, first_ref, second_ref, *outs
):
    def scaled(block, gain_ref):
        return (gain_ref[...] * block.astype(wide)).astype(low)

    for side in (0, 1):
        core = core_ref[0] if side == 0 else 1 - core_ref[0]
        qkv_ref, out_ref, early_ref, late_ref = outs[4 * side : 4 * side + 4]
        inner = out_ref.shape[1]
        hidden = early_ref.shape[2]
        columns = pl.ds(pl.multiple_of(core * inner, inner), inner)
        for block, ref in enumerate((q_ref, k_ref, v_ref)):
            qkv_ref[:, block * inner : (block + 1) * inner] = scaled(ref[:, columns], first_ref)
        out_ref[...] = o_ref[:, columns]
        for part, ref in enumerate((early_ref, late_ref)):
            columns = pl.ds(pl.multiple_of((2 * core + part) * hidden, hidden), hidden)
            ref[0] = scaled(e_ref[:, columns], second_ref)
            ref[1] = c_ref[:, columns]


def weight_sides(core, query, key, value, output, expand, contract, first_gain, second_gain):
    rows, inner = query.shape
    hidden = expand.shape[1] // 4
    one_side = [
        jax.ShapeDtypeStruct((rows, 3 * inner // 2), low),
        jax.ShapeDtypeStruct((rows, inner // 2), low),
        jax.ShapeDtypeStruct((2, rows, hidden), low),
        jax.ShapeDtypeStruct((2, rows, hidden), low),
    ]
    vmem = pl.BlockSpec(memory_space=pltpu.VMEM)
    outs = pl.pallas_call(
        side_kernel,
        in_specs=[pl.BlockSpec(memory_space=pltpu.SMEM)] + [vmem] * 8,
        out_specs=[vmem] * 8,
        out_shape=one_side * 2,
        compiler_params=pltpu.CompilerParams(vmem_limit_bytes=32 << 20),
        cost_estimate=cost(0, 7 << 20),
        name="weight_sides",
    )(
        core,
        query,
        key,
        value,
        output,
        expand,
        contract,
        first_gain.astype(wide)[:, None],
        second_gain.astype(wide)[:, None],
    )
    return outs[:4], outs[4:]


def token_kernel(place_ref, *refs, normed):
    pieces = refs[:4]
    plain_ref, first_ref, first_t_ref, semaphores = refs[4:]
    copies = block_copies(place_ref, 0, pieces, plain_ref, semaphores)
    for copy in copies:
        copy.start()
    for copy in copies:
        copy.wait()
    total = plain_ref.shape[0]
    step = total // 4
    for block in range(4):
        rows = slice(block * step, (block + 1) * step)
        values = plain_ref[rows, :].astype(wide)
        if normed:
            values = normalize(values)[0]
        else:
            position = block * step + lax.broadcasted_iota(jnp.int32, values.shape, 0)
            values = jnp.where(position < place_ref[4], values, 0.0)
        first_ref[rows, :] = values.astype(low)
        first_t_ref[:, rows] = values.T.astype(low)


def token_rows_of(places, pieces, normed):
    total, width = 4 * pieces[0].shape[0], pieces[0].shape[1]
    vmem = pl.BlockSpec(memory_space=pltpu.VMEM)
    return pl.pallas_call(
        functools.partial(token_kernel, normed=normed),
        in_specs=[pl.BlockSpec(memory_space=pltpu.SMEM)] + [anywhere] * 4,
        out_specs=[vmem] * 3,
        out_shape=[
            jax.ShapeDtypeStruct((total, width), low),
            jax.ShapeDtypeStruct((total, width), low),
            jax.ShapeDtypeStruct((width, total), low),
        ],
        scratch_shapes=[pltpu.SemaphoreType.DMA((4,))],
        compiler_params=pltpu.CompilerParams(vmem_limit_bytes=40 << 20),
        cost_estimate=cost(0, 12 << 20),
        name="token_rows" if normed else "cotangent_rows",
    )(places, *pieces)


def rows_product_kernel(place_ref, rows_ref, *refs, count, across):
    pieces = refs[:count]
    out_ref, weight, semaphores = refs[count:]

    @pl.when(pl.program_id(0) == 0)
    def _():
        copies = block_copies(place_ref, 0, pieces, weight, semaphores)
        for copy in copies:
            copy.start()
        for copy in copies:
            copy.wait()

    out_ref[...] = dot(rows_ref[...], weight[...], 1, 1 if across else 0).astype(low)


def rows_product(places, rows, pieces, across, name, step=256):
    total, depth = rows.shape
    count = len(pieces)
    whole = (count * pieces[0].shape[0], pieces[0].shape[1])
    width = whole[0] if across else whole[1]
    return pl.pallas_call(
        functools.partial(rows_product_kernel, count=count, across=across),
        grid_spec=pltpu.PrefetchScalarGridSpec(
            num_scalar_prefetch=1,
            grid=(total // step,),
            in_specs=[pl.BlockSpec((step, depth), lambda i, _: (i, 0))] + [anywhere] * count,
            out_specs=pl.BlockSpec((step, width), lambda i, _: (i, 0)),
            scratch_shapes=[pltpu.VMEM(whole, low), pltpu.SemaphoreType.DMA((count,))],
        ),
        out_shape=jax.ShapeDtypeStruct((total, width), low),
        compiler_params=pltpu.CompilerParams(vmem_limit_bytes=40 << 20),
        cost_estimate=cost(3 * total * whole[0] * whole[1], 8 << 20),
        name=name,
    )(places, rows, *pieces)


def second_norm_kernel(token_ref, mine_ref, other_ref, hidden_ref, normed_ref, normed_t_ref):
    attended = mine_ref[...].astype(wide) + other_ref[...].astype(wide)
    hidden = token_ref[...].astype(wide) + attended
    hidden_ref[...] = hidden
    normed = normalize(hidden)[0]
    normed_ref[...] = normed.astype(low)
    normed_t_ref[...] = normed.T.astype(low)


def second_norm(tokens, mine, other, step=256):
    total, width = tokens.shape
    block = pl.BlockSpec((step, width), lambda i: (i, 0))
    return pl.pallas_call(
        second_norm_kernel,
        grid=(total // step,),
        in_specs=[block] * 3,
        out_specs=[block, block, pl.BlockSpec((width, step), lambda i: (0, i))],
        out_shape=[
            jax.ShapeDtypeStruct((total, width), wide),
            jax.ShapeDtypeStruct((total, width), low),
            jax.ShapeDtypeStruct((width, total), low),
        ],
        compiler_params=pltpu.CompilerParams(vmem_limit_bytes=40 << 20),
        cost_estimate=cost(0, 16 << 20),
        name="second_norm",
    )(tokens, mine, other)


def feed_forward_kernel(
    place_ref, normed_ref, normed_t_ref, grad_ref, grad_t_ref, *refs, count, first
):
    pieces = refs[:count]
    refs = refs[count:]
    if first:
        mixed_sum, normed_sum, terms_ref, upper_ref, lower_ref, weight, semaphores = refs
        before = ()
    else:
        before = refs[:2]
        own_ref, other_ref, normed_grad_ref, terms_ref, upper_ref, lower_ref = refs[2:8]
        weight, semaphores, mixed_sum, normed_sum = refs[8:]
    index = pl.program_id(0)
    step = terms_ref.shape[2]

    @pl.when(index == 0)
    def _():
        copies = block_copies(place_ref, 0, pieces, weight, semaphores)
        for number, (source, target) in enumerate(zip(before, (mixed_sum, normed_sum))):
            copies.append(
                pltpu.make_async_copy(source, target, semaphores.at[count + number])
            )
        for copy in copies:
            copy.start()
        for copy in copies:
            copy.wait()

    columns = pl.ds(pl.multiple_of(index * step, step), step)
    expand = weight[0, :, columns]
    contract = weight[1, :, columns]
    pre_act = dot(normed_ref[...], expand, 1, 0)
    act_grad = dot(grad_ref[...], contract, 1, 0).astype(low).astype(wide)
    activated, slope = gelu_and_slope(pre_act)
    activated = activated.astype(low)
    pre_grad = (act_grad * slope).astype(low)
    terms_ref[1] = dot(grad_t_ref[...], activated, 1, 0).astype(low)
    terms_ref[0] = dot(normed_t_ref[...], pre_grad, 1, 0).astype(low)
    half = upper_ref.shape[1]
    corner = pl.multiple_of(place_ref[count] * (2 * half), 2 * half)
    for part in (0, 1):
        upper_ref[part] = terms_ref[part, pl.ds(corner, half), :]
        lower_ref[part] = terms_ref[part, pl.ds(corner + half, half), :]
    mixed = dot(activated, contract, 1, 1)
    normed_grad = dot(pre_grad, expand, 1, 1)
    if first:

        @pl.when(index == 0)
        def _():
            mixed_sum[...] = mixed
            normed_sum[...] = normed_grad

        @pl.when(index > 0)
        def _():
            mixed_sum[...] += mixed
            normed_sum[...] += normed_grad

    else:
        mixed_sum[...] += mixed
        normed_sum[...] += normed_grad

        @pl.when(index == pl.num_programs(0) - 1)
        def _():
            rows = own_ref.shape[0]
            core = place_ref[count + 1]
            own = pl.multiple_of(core * rows, rows)
            away = pl.multiple_of((1 - core) * rows, rows)
            own_ref[...] = mixed_sum[pl.ds(own, rows), :].astype(low)
            other_ref[...] = mixed_sum[pl.ds(away, rows), :].astype(low)
            normed_grad_ref[...] = normed_sum[...].astype(low)


def feed_forward(places, normed, normed_t, grad, grad_t, pieces, chips, before=None, step=512):
    rows, width = normed.shape
    count = len(pieces)
    hidden = pieces[0].shape[2]
    half = width // chips // 2
    first = before is None

    def fixed(shape):
        return pl.BlockSpec(shape, lambda i, _: (0,) * len(shape), pipeline_mode=pl.Buffered(1))

    def moving(leading):
        return pl.BlockSpec((2, leading, step), lambda i, _: (0, 0, i))

    whole = fixed((rows, width))
    term_specs = [moving(width), moving(half), moving(half)]
    term_shapes = [jax.ShapeDtypeStruct((2, n, hidden), low) for n in (width, half, half)]
    scratch = [
        pltpu.VMEM((2, width, hidden), low),
        pltpu.SemaphoreType.DMA((count + 2,)),
    ]
    if first:
        out_specs = [whole, whole] + term_specs
        out_shape = [jax.ShapeDtypeStruct((rows, width), wide)] * 2 + term_shapes
    else:
        part = fixed((rows // 2, width))
        out_specs = [part, part, whole] + term_specs
        out_shape = [
            jax.ShapeDtypeStruct((rows // 2, width), low),
            jax.ShapeDtypeStruct((rows // 2, width), low),
            jax.ShapeDtypeStruct((rows, width), low),
        ] + term_shapes
        scratch += [pltpu.VMEM((rows, width), wide)] * 2
    return pl.pallas_call(
        functools.partial(feed_forward_kernel, count=count, first=first),
        grid_spec=pltpu.PrefetchScalarGridSpec(
            num_scalar_prefetch=1,
            grid=(hidden // step,),
            in_specs=[whole, fixed((width, rows))] * 2
            + [anywhere] * (count + (0 if first else 2)),
            out_specs=out_specs,
            scratch_shapes=scratch,
        ),
        out_shape=out_shape,
        compiler_params=pltpu.CompilerParams(vmem_limit_bytes=58 << 20),
        cost_estimate=cost(20 * rows * width * hidden, 40 << 20),
        name="feed_forward",
    )(places, normed, normed_t, grad, grad_t, *pieces, *(() if first else before))


def hidden_back_kernel(place_ref, mine_ref, other_ref, hidden_ref, grad_ref, *refs, count):
    pieces = refs[:count]
    hidden_grad_ref, low_ref, low_t_ref, context_grad_ref, weight, semaphores = refs[count:]

    @pl.when(pl.program_id(0) == 0)
    def _():
        copies = block_copies(place_ref, 0, pieces, weight, semaphores)
        for copy in copies:
            copy.start()
        for copy in copies:
            copy.wait()

    upstream = mine_ref[...].astype(wide) + other_ref[...].astype(wide)
    hidden = hidden_ref[...]
    scale = normalize(hidden)[1]
    hidden_grad = grad_ref[...].astype(wide) + normalize_back(hidden, scale, upstream)
    hidden_grad_ref[...] = hidden_grad
    attended_grad = hidden_grad.astype(low)
    low_ref[...] = attended_grad
    low_t_ref[...] = hidden_grad.T.astype(low)
    context_grad_ref[...] = dot(attended_grad, weight[...], 1, 0).astype(low)


def hidden_back(places, mine, other, hidden, grad, pieces, step=256):
    total, width = hidden.shape
    count = len(pieces)
    inner = pieces[0].shape[1]
    block = pl.BlockSpec((step, width), lambda i, _: (i, 0))
    return pl.pallas_call(
        functools.partial(hidden_back_kernel, count=count),
        grid_spec=pltpu.PrefetchScalarGridSpec(
            num_scalar_prefetch=1,
            grid=(total // step,),
            in_specs=[block] * 4 + [anywhere] * count,
            out_specs=[
                block,
                block,
                pl.BlockSpec((width, step), lambda i, _: (0, i)),
                pl.BlockSpec((step, inner), lambda i, _: (i, 0)),
            ],
            scratch_shapes=[pltpu.VMEM((width, inner), low), pltpu.SemaphoreType.DMA((count,))],
        ),
        out_shape=[
            jax.ShapeDtypeStruct((total, width), wide),
            jax.ShapeDtypeStruct((total, width), low),
            jax.ShapeDtypeStruct((width, total), low),
            jax.ShapeDtypeStruct((total, inner), low),
        ],
        compiler_params=pltpu.CompilerParams(vmem_limit_bytes=40 << 20),
        cost_estimate=cost(4 * total * width * inner, 24 << 20),
        name="hidden_back",
    )(places, mine, other, hidden, grad, *pieces)


def attention_terms_kernel(
    corner_ref, grad_t_ref, normed_t_ref, context_ref, q_ref, k_ref, v_ref, terms_ref, upper_ref, lower_ref
):
    inner = context_ref.shape[1]
    terms_ref[0, :, :inner] = dot(grad_t_ref[...], context_ref[...], 1, 0).astype(low)
    for number, ref in enumerate((q_ref, k_ref, v_ref)):
        columns = slice((number + 1) * inner, (number + 2) * inner)
        terms_ref[0, :, columns] = dot(normed_t_ref[...], ref[...], 1, 0).astype(low)

    @pl.when(pl.program_id(0) == corner_ref[0])
    def _():
        half = upper_ref.shape[0]
        upper_ref[...] = terms_ref[0, :half, :]
        lower_ref[...] = terms_ref[0, half:, :]


def attention_terms(corner, grad_t, normed_t, context, query_grad, key_grad, value_grad, chips):
    width, total = normed_t.shape
    inner = context.shape[1]
    share = width // chips
    block = pl.BlockSpec((share, total), lambda i, _: (i, 0))
    whole = pl.BlockSpec((total, inner), lambda i, _: (0, 0), pipeline_mode=pl.Buffered(1))
    corner_block = pl.BlockSpec((share // 2, 4 * inner), lambda i, _: (0, 0))
    return pl.pallas_call(
        attention_terms_kernel,
        grid_spec=pltpu.PrefetchScalarGridSpec(
            num_scalar_prefetch=1,
            grid=(chips,),
            in_specs=[block, block] + [whole] * 4,
            out_specs=[
                pl.BlockSpec((1, share, 4 * inner), lambda i, _: (i, 0, 0)),
                corner_block,
                corner_block,
            ],
        ),
        out_shape=[
            jax.ShapeDtypeStruct((chips, share, 4 * inner), low),
            jax.ShapeDtypeStruct((share // 2, 4 * inner), low),
            jax.ShapeDtypeStruct((share // 2, 4 * inner), low),
        ],
        compiler_params=pltpu.CompilerParams(vmem_limit_bytes=40 << 20),
        cost_estimate=cost(4 * total * width * 4 * inner, 16 << 20),
        name="attention_terms",
    )(corner, grad_t, normed_t, context, query_grad, key_grad, value_grad)


def input_product_kernel(place_ref, q_ref, k_ref, v_ref, *refs, count):
    pieces = refs[:count]
    own_ref, other_ref, weight, semaphores = refs[count:]
    index = pl.program_id(0)

    @pl.when(index == 0)
    def _():
        copies = block_copies(place_ref, 0, pieces, weight, semaphores)
        for copy in copies:
            copy.start()
        for copy in copies:
            copy.wait()

    inner = q_ref.shape[1]
    product = dot(q_ref[...], weight[:, :inner], 1, 1)
    product += dot(k_ref[...], weight[:, inner : 2 * inner], 1, 1)
    product += dot(v_ref[...], weight[:, 2 * inner :], 1, 1)

    @pl.when(index < 2)
    def _():
        other_ref[...] = product.astype(low)

    @pl.when(index >= 2)
    def _():
        own_ref[...] = product


def input_product(places, query_grad, key_grad, value_grad, pieces):
    total, inner = query_grad.shape
    count = len(pieces)
    width = count * pieces[0].shape[0]
    step = total // 4

    def rows(i, place_ref):
        core = place_ref[count]
        return (jnp.where(i < 2, 2 * (1 - core) + i, 2 * core + i - 2), 0)

    return pl.pallas_call(
        functools.partial(input_product_kernel, count=count),
        grid_spec=pltpu.PrefetchScalarGridSpec(
            num_scalar_prefetch=1,
            grid=(4,),
            in_specs=[pl.BlockSpec((step, inner), rows)] * 3 + [anywhere] * count,
            out_specs=[
                pl.BlockSpec((step, width), lambda i, _: (jnp.maximum(i - 2, 0), 0)),
                pl.BlockSpec((step, width), lambda i, _: (jnp.minimum(i, 1), 0)),
            ],
            scratch_shapes=[
                pltpu.VMEM((width, 3 * inner), low),
                pltpu.SemaphoreType.DMA((count,)),
            ],
        ),
        out_shape=[
            jax.ShapeDtypeStruct((total // 2, width), wide),
            jax.ShapeDtypeStruct((total // 2, width), low),
        ],
        compiler_params=pltpu.CompilerParams(vmem_limit_bytes=40 << 20),
        cost_estimate=cost(4 * total * width * 3 * inner, 16 << 20),
        name="input_product",
    )(places, query_grad, key_grad, value_grad, *pieces)


def finish_kernel(place_ref, own_ref, other_ref, base_ref, token_ref, first_ref, second_ref, *, back):
    index = pl.program_id(0)
    summed = own_ref[...].astype(wide) + other_ref[...].astype(wide)
    if back:
        tokens = token_ref[...].astype(wide)
        values = base_ref[...] + normalize_back(tokens, normalize(tokens)[1], summed)
    else:
        row = (2 * place_ref[0] + index) * summed.shape[0]
        position = row + lax.broadcasted_iota(jnp.int32, summed.shape, 0)
        values = jnp.where(position < place_ref[2], base_ref[...] + summed, 0.0)
    values = values.astype(low)

    @pl.when(index == place_ref[1])
    def _():
        first_ref[...] = values

    @pl.when(index != place_ref[1])
    def _():
        second_ref[...] = values


def finish_half(core, odd, length, own, other, base, tokens, back):
    rows, width = own.shape
    step = rows // 2
    half = pl.BlockSpec((step, width), lambda i, _: (i, 0))
    whole = pl.BlockSpec((step, width), lambda i, place_ref: (2 * place_ref[0] + i, 0))
    quarter = pl.BlockSpec((step, width), lambda i, _: (0, 0))
    return pl.pallas_call(
        functools.partial(finish_kernel, back=back),
        grid_spec=pltpu.PrefetchScalarGridSpec(
            num_scalar_prefetch=1,
            grid=(2,),
            in_specs=[half, half, whole, whole],
            out_specs=[quarter, quarter],
        ),
        out_shape=[jax.ShapeDtypeStruct((step, width), low)] * 2,
        compiler_params=pltpu.CompilerParams(vmem_limit_bytes=32 << 20),
        cost_estimate=cost(0, 8 << 20),
        name="input_gradient_rows" if back else "result_rows",
    )(jnp.stack([core, odd, length]).astype(jnp.int32), own, other, base, tokens)


def pick_kernel(slot_ref, *refs, count):
    pieces = refs[:count]
    own_ref, other_ref, semaphores = refs[count:]
    for row in range(4):
        target = (own_ref if row < 2 else other_ref).at[row % 2]
        for number in range(count):

            @pl.when(slot_ref[row] == slot_ref[4 + number])
            def _():
                copy = pltpu.make_async_copy(pieces[number], target, semaphores.at[row])
                copy.start()
                copy.wait()


def pick_slots(slots, pieces):
    count = len(pieces)
    shape = (2,) + pieces[0].shape
    return pl.pallas_call(
        functools.partial(pick_kernel, count=count),
        in_specs=[pl.BlockSpec(memory_space=pltpu.SMEM)] + [anywhere] * count,
        out_specs=[anywhere] * 2,
        out_shape=[jax.ShapeDtypeStruct(shape, low)] * 2,
        scratch_shapes=[pltpu.SemaphoreType.DMA((4,))],
        compiler_params=pltpu.CompilerParams(vmem_limit_bytes=32 << 20),
        cost_estimate=cost(0, 8 << 20),
        name="pick_slots",
    )(slots, *pieces)


def normalize(values):
    scaled = lax.rsqrt(jnp.mean(values * values, axis=-1, keepdims=True) + epsilon)
    return (values * scaled, scaled)


def normalize_back(values, scaled, upstream):
    unit_rows = values * scaled
    return scaled * (upstream - unit_rows * jnp.mean(upstream * unit_rows, axis=-1, keepdims=True))


def scaled_rows(weight, scaling):
    return (scaling.astype(wide)[:, None] * weight.astype(wide)).astype(low)


def take(array, index):
    return lax.dynamic_index_in_dim(array, index, 0, keepdims=False)


def put(array, part, index):
    return lax.dynamic_update_slice_in_dim(array, part[None], index, 0)


def after(array, *others):
    return lax.optimization_barrier((array, *others))[0]


class Links:
    def __init__(self):
        self.shards = lax.axis_size("fsdp")
        self.depth = lax.axis_size("ctx")
        self.shard = lax.axis_index("fsdp")
        self.level = lax.axis_index("ctx")
        self.chips = self.shards // 2
        self.chip = self.shard // 2
        self.core = self.shard % 2
        self.groups = [list(range(core, self.shards, 2)) for core in (0, 1)]
        self.square = self.chips == 4

    def sibling(self, array):
        return lax.ppermute(array, "fsdp", [(i, i ^ 1) for i in range(self.shards)])

    def across(self, array, bit):
        return lax.ppermute(array, "fsdp", [(i, i ^ (2 * bit)) for i in range(self.shards)])

    def in_order(self, mine, other, axis):
        return jnp.concatenate(
            [jnp.where(self.core == 0, mine, other), jnp.where(self.core == 0, other, mine)],
            axis=axis,
        )

    def gather(self, parts, behind=()):
        if not self.square:
            whole = [
                lax.all_gather(part, "fsdp", axis=0, axis_index_groups=self.groups)
                for part in parts
            ]
            return [tuple(w[chip] for w in whole) for chip in range(self.chips)], ()
        if behind:
            parts = tuple(after(part, *behind) for part in parts)
        first = tuple(self.across(part, 1) for part in parts)
        second = tuple(self.across(part, 2) for part in parts)
        corner = (self.across(first[0], 2), self.across(second[1], 1))
        return [parts, first, second, corner], (*first, *second)

    def chip_numbers(self):
        return [self.chip ^ k for k in range(4)] if self.square else list(range(self.chips))

    def gather_weight(self, mine, behind=(), other=None):
        pairs, sent = self.gather((mine, other), behind)
        return [piece for pair in pairs for piece in pair], sent

    def weight_places(self):
        return [2 * chip + side for chip in self.chip_numbers() for side in (self.core, 1 - self.core)]

    def scatter(self, terms, upper, lower, behind=()):
        dim = terms.ndim - 2
        if not self.square:
            summed = lax.psum_scatter(
                terms, "fsdp", scatter_dimension=dim, tiled=True, axis_index_groups=self.groups
            )
            return summed.astype(low), ()
        share = terms.shape[dim] // 4
        half = share // 2

        def rows(chip):
            return lax.dynamic_slice_in_dim(terms, chip * share, share, dim).astype(wide)

        if behind:
            upper, lower = after(upper, *behind), after(lower, *behind)
        upper = self.across(upper, 1).astype(wide)
        lower = self.across(lower, 2).astype(wide)
        top = [(0, 0, 0)] * dim + [(0, half, 0), (0, 0, 0)]
        bottom = [(0, 0, 0)] * dim + [(half, 0, 0), (0, 0, 0)]
        zero = jnp.zeros((), wide)
        beside = (rows(self.chip ^ 1) + lax.pad(lower, zero, bottom)).astype(low)
        below = (rows(self.chip ^ 2) + lax.pad(upper, zero, top)).astype(low)
        first = self.across(beside, 1)
        second = self.across(below, 2)
        summed = rows(self.chip) + first.astype(wide) + second.astype(wide)
        return summed.astype(low), (first, second)

    def level_sum(self, terms):
        inward = lax.ppermute(terms, "ctx", [(0, 1), (3, 2)])
        joined = (terms.astype(wide) + inward.astype(wide)).astype(low)
        across = lax.ppermute(joined, "ctx", [(1, 2), (2, 1)])
        total = (joined.astype(wide) + across.astype(wide)).astype(low)
        outward = lax.ppermute(total, "ctx", [(1, 0), (2, 3)])
        inner = (self.level == 1) | (self.level == 2)
        return jnp.where(inner, total, outward)

    def exchange_rows(self, rows):
        dim = rows.ndim - 2
        half = rows.shape[dim] // 2
        mine = lax.dynamic_slice_in_dim(rows, self.core * half, half, dim)
        other = self.sibling(lax.dynamic_slice_in_dim(rows, (1 - self.core) * half, half, dim))
        return jnp.where(self.core == 0, mine, other), jnp.where(self.core == 0, other, mine)

    def trade(self, array, outward, swapped):
        pairs = []
        for level in range(self.depth):
            for shard in range(self.shards):
                chip, core = divmod(shard, 2)
                side, odd = divmod(level, 2)
                slot = odd if not swapped else 1 - odd
                held = level * self.shards + shard
                worked = (2 * core + slot) * self.shards + 2 * chip + side
                pairs.append((held, worked) if outward else (worked, held))
        return lax.ppermute(array, ("ctx", "fsdp"), pairs)

    def to_slot(self, blocks):
        odd = self.level % 2
        first = self.trade(take(blocks, odd), True, False)
        second = self.trade(take(blocks, 1 - odd), True, True)
        return [first, second, self.sibling(first), self.sibling(second)]

    def quarter_places(self):
        odd = self.level % 2
        near, far = 2 * self.core, 2 * (1 - self.core)
        return [near + odd, near + 1 - odd, far + odd, far + 1 - odd]

    def from_slot(self, quarters):
        first = self.trade(quarters[0], False, False)
        second = self.trade(quarters[1], False, True)
        flip = self.level % 2 == 0
        return jnp.where(flip, first, second), jnp.where(flip, second, first)


def local(
    tokens,
    cotangent,
    sequence_lengths,
    slot_sequence,
    offset_bucket,
    first_gain,
    second_gain,
    query_weight,
    key_weight,
    value_weight,
    output_weight,
    expand_weight,
    contract_weight,
    bias_table,
    clip_limit,
):
    links = Links()
    core = links.core
    held_count, local_length, model_width = tokens.shape
    total_length = local_length * links.depth
    bucket_count, head_count = bias_table.shape
    inner_width = query_weight.shape[1]
    head_size = inner_width // head_count
    own_heads = head_count // 2
    own_inner = inner_width // 2
    slot_count = slot_sequence.shape[0]
    assert held_count == 2 and links.depth == 4

    slots = jnp.arange(slot_count)
    slot = links.chip * (2 * held_count) + links.level
    sequence = jnp.sum(jnp.where(slots == slot, slot_sequence, 0))
    length = jnp.sum(jnp.where(slots == sequence, sequence_lengths, 0)).astype(jnp.int32)
    odd = links.level % 2

    def numbers(*values):
        return jnp.stack([jnp.asarray(value, jnp.int32) for value in values])

    token_quarters = links.to_slot(tokens)
    mine, other = weight_sides(
        numbers(core),
        query_weight,
        key_weight,
        value_weight,
        output_weight,
        expand_weight,
        contract_weight,
        first_gain,
        second_gain,
    )
    arrived = [links.sibling(array) for array in other]
    sent = ()
    gathered = []
    for own_part, arrived_part in zip(mine, arrived):
        pieces, sent = links.gather_weight(own_part, sent, arrived_part)
        gathered.append(pieces)
    qkv_pieces, output_pieces, early_pieces, late_pieces = gathered
    weight_places = links.weight_places()
    corner = links.chip ^ 3 if links.square else 0
    places = numbers(*weight_places, corner, core)
    core_places = numbers(*weight_places, core)
    slot_places = numbers(*links.quarter_places(), length)

    line_width = 2 * total_length
    falling = jnp.concatenate([jnp.flip(offset_bucket), jnp.full((1,), -1, jnp.int32)])
    matching = falling[:, None] == jnp.arange(bucket_count)[None, :]
    own_table = lax.dynamic_slice_in_dim(bias_table, core * own_heads, own_heads, 1)
    lines = dot(own_table, matching.astype(low), 0, 1)
    strips = bias_strips(lines.reshape(own_heads, 1, line_width))

    token_low, normed_one, normed_one_t = token_rows_of(slot_places, token_quarters, True)
    cotangent_quarters = links.to_slot(after(cotangent, *token_quarters))
    _, out_low, out_low_t = token_rows_of(slot_places, cotangent_quarters, False)

    qkv = rows_product(places, normed_one, qkv_pieces, False, "qkv_product")
    length_line = length.reshape(1)
    context, log_totals, tops = attention_forward(length_line, qkv, strips)
    attended = rows_product(places, context, output_pieces, True, "attended_product")
    hidden_one, normed_two, normed_two_t = second_norm(
        token_low, attended, links.sibling(attended)
    )
    operands = (normed_two, normed_two_t, out_low, out_low_t)
    mixed_sum, normed_sum, early_terms, early_upper, early_lower = feed_forward(
        places, *operands, early_pieces, links.chips
    )
    mixed_own, mixed_away, normed_two_part, late_terms, late_upper, late_lower = feed_forward(
        places, *operands, late_pieces, links.chips, (mixed_sum, normed_sum)
    )
    hidden_grad, attended_grad, attended_grad_t, context_grad = hidden_back(
        places,
        normed_two_part,
        links.sibling(normed_two_part),
        hidden_one,
        out_low,
        output_pieces,
    )
    query_grad, key_grad, value_grad, strip_grads = attention_backward(
        length_line, qkv, context, context_grad, log_totals, strips
    )
    attention_parts, attention_upper, attention_lower = attention_terms(
        numbers(corner),
        attended_grad_t,
        normed_one_t,
        context,
        query_grad,
        key_grad,
        value_grad,
        links.chips,
    )
    attention_parts = attention_parts.reshape(model_width, -1)

    early_sum, sent = links.scatter(early_terms, early_upper, early_lower)
    late_sum, sent = links.scatter(late_terms, late_upper, late_lower, sent)
    attention_sum, sent = links.scatter(
        attention_parts, attention_upper, attention_lower, sent
    )
    early_left, early_right = links.exchange_rows(links.level_sum(early_sum))
    late_left, late_right = links.exchange_rows(links.level_sum(late_sum))
    attention_left, attention_right = links.exchange_rows(links.level_sum(attention_sum))

    own_part, away_part = input_product(core_places, query_grad, key_grad, value_grad, qkv_pieces)
    input_quarters = finish_half(
        core, odd, length, own_part, links.sibling(away_part), hidden_grad, token_low, True
    )
    input_gradient = jnp.stack(links.from_slot(input_quarters)).astype(wide)

    result_quarters = finish_half(
        core, odd, length, mixed_own, links.sibling(mixed_away), hidden_one, token_low, False
    )
    results = links.from_slot(result_quarters)
    result_pairs, _ = links.gather(results, sent)

    def slot_of(wanted):
        return jnp.sum(jnp.where(slot_sequence == wanted, slots, 0))

    own_slots = [slot_of(links.shard * held_count + row) for row in range(held_count)]
    other_slots = [slot_of((links.shard ^ 1) * held_count + row) for row in range(held_count)]
    piece_slots = [
        (2 * chip + core) * held_count + row
        for chip in links.chip_numbers()
        for row in range(held_count)
    ]
    picked, picked_other = pick_slots(
        numbers(*own_slots, *other_slots, *piece_slots),
        [piece for pair in result_pairs for piece in pair],
    )
    from_other = links.sibling(picked_other)
    output = jnp.stack(
        [
            jnp.where((s // held_count) % 2 == core, picked[row], from_other[row])
            for row, s in enumerate(own_slots)
        ]
    )

    def side_by_side(*parts):
        return jnp.concatenate(parts, axis=1).astype(wide)

    raw_two = side_by_side(early_left[0], late_left[0], early_right[0], late_right[0])
    contract_weight_gradient = side_by_side(
        early_left[1], late_left[1], early_right[1], late_right[1]
    )

    def inner_columns(block):
        columns = slice(block * own_inner, (block + 1) * own_inner)
        return side_by_side(attention_left[:, columns], attention_right[:, columns])

    output_weight_gradient = inner_columns(0)
    raw_query, raw_key, raw_value = (inner_columns(block) for block in (1, 2, 3))
    first_scale = first_gain.astype(wide)[:, None]
    second_scale = second_gain.astype(wide)[:, None]
    first_gain_gradient = jnp.sum(
        query_weight.astype(wide) * raw_query
        + key_weight.astype(wide) * raw_key
        + value_weight.astype(wide) * raw_value,
        axis=1,
    )
    second_gain_gradient = jnp.sum(expand_weight.astype(wide) * raw_two, axis=1)
    query_weight_gradient = first_scale * raw_query
    key_weight_gradient = first_scale * raw_key
    value_weight_gradient = first_scale * raw_value
    expand_weight_gradient = second_scale * raw_two

    diagonals = diagonal_sums(strip_grads).reshape(own_heads, line_width)
    table_grad = lax.dot_general(
        diagonals,
        matching.astype(wide),
        (((1,), (0,)), ((), ())),
        precision=lax.Precision.HIGHEST,
        preferred_element_type=wide,
    )
    small = jnp.concatenate([table_grad, tops.reshape(own_heads, -1)[:, :1]], axis=1)

    def joined(left, right):
        return jnp.concatenate(
            [
                left[:, :bucket_count] + right[:, :bucket_count],
                jnp.maximum(left[:, bucket_count:], right[:, bucket_count:]),
            ],
            axis=1,
        )

    bit = 1
    while bit < links.chips:
        small = joined(small, links.across(small, bit))
        bit *= 2
    bit = 1
    while bit < links.depth:
        swap = [(i, i ^ bit) for i in range(links.depth)]
        small = joined(small, lax.ppermute(small, "ctx", swap))
        bit *= 2
    small = links.in_order(small, links.sibling(small), 0)
    table_rows = bucket_count // links.shards
    bias_table_gradient = lax.dynamic_slice_in_dim(
        small[:, :bucket_count].T, links.shard * table_rows, table_rows, 0
    )
    largest = small[:, bucket_count]
    shrink = clip_limit / jnp.maximum(clip_limit, largest)
    column_scale = jnp.repeat(jnp.sqrt(shrink), head_size)
    new_query_weight = query_weight.astype(wide) * column_scale[None, :]
    new_key_weight = key_weight.astype(wide) * column_scale[None, :]
    return (
        output,
        input_gradient,
        first_gain_gradient,
        second_gain_gradient,
        query_weight_gradient,
        key_weight_gradient,
        value_weight_gradient,
        output_weight_gradient,
        expand_weight_gradient,
        contract_weight_gradient,
        bias_table_gradient,
        largest,
        new_query_weight,
        new_key_weight,
    )


def solution(mesh):
    return jax.shard_map(
        local,
        mesh=mesh,
        in_specs=(
            P("fsdp", "ctx", None),
            P("fsdp", "ctx", None),
            P(),
            P(),
            P(),
            P("fsdp"),
            P("fsdp"),
            P("fsdp", None),
            P("fsdp", None),
            P("fsdp", None),
            P("fsdp", None),
            P("fsdp", None),
            P("fsdp", None),
            P(),
            P(),
        ),
        out_specs=(
            P("fsdp", "ctx", None),
            P("fsdp", "ctx", None),
            P("fsdp"),
            P("fsdp"),
            P("fsdp", None),
            P("fsdp", None),
            P("fsdp", None),
            P("fsdp", None),
            P("fsdp", None),
            P("fsdp", None),
            P("fsdp", None),
            P(),
            P("fsdp", None),
            P("fsdp", None),
        ),
        check_vma=False,
    )
```

```python
import functools
import math

import jax
import jax.numpy as jnp
from jax import lax
from jax.experimental import pallas as pl
from jax.experimental.pallas import tpu as pltpu
from jax.sharding import PartitionSpec as P

epsilon = 1e-06
masked = -1e30
tile = 128
half_tile = 64
wide = jnp.float32
low = jnp.bfloat16
anywhere = pl.BlockSpec(memory_space=pl.ANY)
in_vmem = pl.BlockSpec(memory_space=pltpu.VMEM)
in_hbm = pl.BlockSpec(memory_space=pltpu.HBM)


class Steps:
    def __init__(self):
        self.behind = ()

    def wait(self, *arrays):
        self.behind += arrays

    def launch(
        self,
        name,
        kernel,
        operands,
        in_specs,
        out_specs,
        out_shape,
        grid=(1,),
        prefetch=1,
        scratch=(),
        estimate=(0, 1 << 20),
        memory=24,
        stored=(),
    ):
        inputs, idle = len(operands), self.behind

        def run(*refs):
            refs = list(refs)
            mark_ref = refs.pop(inputs + len(idle) + len(out_specs))
            mark_ref[...] = jnp.zeros_like(mark_ref)
            kernel(*refs[:inputs], *refs[inputs + len(idle) :])

        out_specs, out_shape = list(out_specs), list(out_shape)
        outs = pl.pallas_call(
            run,
            grid_spec=pltpu.PrefetchScalarGridSpec(
                num_scalar_prefetch=prefetch,
                grid=grid,
                in_specs=list(in_specs) + [anywhere] * len(idle),
                out_specs=out_specs + [pl.BlockSpec((8, tile), lambda *_: (0, 0))],
                scratch_shapes=list(scratch),
            ),
            out_shape=[
                pltpu.HBM(shape, kind) if number in stored else jax.ShapeDtypeStruct(shape, kind)
                for number, (shape, kind) in enumerate(out_shape + [((8, tile), wide)])
            ],
            compiler_params=pltpu.CompilerParams(vmem_limit_bytes=memory << 20),
            cost_estimate=pl.CostEstimate(
                flops=int(estimate[0]), bytes_accessed=int(estimate[1]), transcendentals=0
            ),
            name=name,
        )(*operands, *idle)
        self.behind = (outs[-1],)
        return outs[:-1]


def dot(left, right, left_dim, right_dim):
    return lax.dot_general(
        left, right, (((left_dim,), (right_dim,)), ((), ())), preferred_element_type=wide
    )


def strip_kernel(line_ref, strip_ref):
    width = line_ref.shape[-1]
    rows = jnp.broadcast_to(line_ref[0], (tile, width))
    strip_ref[0] = pltpu.roll(rows, width - (tile - 1), 1, stride=1, stride_axis=0)


def bias_strips(steps, lines):
    heads, _, width = lines.shape
    return steps.launch(
        "bias_strips",
        strip_kernel,
        [lines],
        [pl.BlockSpec((1, 1, width), lambda h: (h, 0, 0))],
        [pl.BlockSpec((1, tile, width), lambda h: (h, 0, 0))],
        [((heads, tile, width), wide)],
        grid=(heads,),
        prefetch=0,
        memory=16,
        stored=(0,),
        estimate=(0, 8 << 20),
    )[0]


def diagonal_kernel(strip_ref, line_ref):
    strip = strip_ref[0]
    rows = tile
    while rows > 1:
        rows //= 2
        strip = pltpu.roll(strip[:rows], rows, 1) + strip[rows:]
    line_ref[0] = strip


def diagonal_sums(steps, strips):
    heads, _, width = strips.shape
    return steps.launch(
        "diagonal_sums",
        diagonal_kernel,
        [strips],
        [pl.BlockSpec((1, tile, width), lambda h: (h, 0, 0))],
        [pl.BlockSpec((1, 1, width), lambda h: (h, 0, 0))],
        [((heads, 1, width), wide)],
        grid=(heads,),
        prefetch=0,
        memory=16,
        estimate=(0, 2 << 20),
    )[0]


def one_head(block, head, extra=None):
    lane = lax.broadcasted_iota(jnp.int32, block.shape, 1)
    kept = jnp.where((lane >= half_tile) if head else (lane < half_tile), block, 0)
    if extra is None:
        return kept
    return jnp.where(lane == (0 if head else half_tile), extra, kept)


def key_masks(total, length):
    position = lax.broadcasted_iota(jnp.int32, (total, tile), 0)
    return jnp.where(position < length, 0.0, masked).astype(low)


def strip_columns(total, first, width):
    return [
        pl.ds(pl.multiple_of(total - tile - row + first, tile), width)
        for row in range(0, total, tile)
    ]


def add_bias(products, strip_ref, head, columns):
    return jnp.concatenate(
        [
            products[block * tile : (block + 1) * tile] + strip_ref[head, :, where]
            for block, where in enumerate(columns)
        ],
        axis=0,
    )


def forward_kernel(
    length_ref, query_ref, key_ref, value_ref, strip_ref, context_ref, total_ref, top_ref, *, step
):
    length = length_ref[0]
    total = query_ref.shape[0]
    masks = key_masks(total, length)
    ones = jnp.ones((step, tile), low)
    keys = [one_head(key_ref[...], head, masks) for head in (0, 1)]
    values = [one_head(value_ref[...], head).astype(wide).T.astype(low) for head in (0, 1)]

    def body(index, tops):
        first = pl.multiple_of(index * step, step)
        queries = query_ref[pl.ds(first, step), :]
        columns = strip_columns(total, first, step)
        query_okay = first + lax.broadcasted_iota(jnp.int32, (1, step), 1) < length
        context = None
        peaks = []
        for head in (0, 1):
            products = dot(keys[head], one_head(queries, head, ones), 1, 1)
            scores = add_bias(products, strip_ref, head, columns)
            row_max = jnp.max(scores, axis=0, keepdims=True)
            exponent = jnp.exp(scores - row_max)
            summed = jnp.sum(exponent, axis=0, keepdims=True)
            part = dot(values[head], exponent.astype(low), 1, 0) * (1.0 / summed)
            context = part if context is None else context + part
            total_ref[0, head : head + 1, pl.ds(first, step)] = row_max + jnp.log(summed)
            peaks.append(
                jnp.where(query_okay, jnp.max(products, axis=0, keepdims=True), masked)
            )
        context_ref[pl.ds(first, step), :] = context.T.astype(low)
        return tuple(jnp.maximum(top, peak) for top, peak in zip(tops, peaks))

    tops = lax.fori_loop(
        0, total // step, body, tuple(jnp.full((1, step), masked, wide) for _ in (0, 1))
    )
    for head in (0, 1):
        peak = jnp.max(tops[head], axis=1, keepdims=True)
        top_ref[0, head : head + 1, :] = jnp.broadcast_to(peak, (1, tile))


def attention_forward(steps, length, qkv, strips, start, count, step=512):
    total = qkv.shape[0]
    pairs = qkv.shape[1] // (3 * tile)
    strip_width = strips.shape[2]

    def columns(which):
        return pl.BlockSpec((total, tile), lambda p, _: (0, which * pairs + start + p))

    return steps.launch(
        "attention_forward",
        functools.partial(forward_kernel, step=step),
        [length, qkv, qkv, qkv, strips],
        [columns(which) for which in range(3)]
        + [pl.BlockSpec((2, tile, strip_width), lambda p, _: (start + p, 0, 0))],
        [
            pl.BlockSpec((total, tile), lambda p, _: (0, p)),
            pl.BlockSpec((1, 2, total), lambda p, _: (p, 0, 0)),
            pl.BlockSpec((1, 2, tile), lambda p, _: (p, 0, 0)),
        ],
        [((total, count * tile), low), ((count, 2, total), wide), ((count, 2, tile), wide)],
        grid=(count,),
        memory=32,
        estimate=(6e9 * count, (3 << 20) * count),
    )


def backward_kernel(
    length_ref,
    query_ref,
    key_ref,
    value_ref,
    context_ref,
    grad_ref,
    total_ref,
    strip_ref,
    query_grad_ref,
    key_grad_ref,
    value_grad_ref,
    strip_grad_ref,
    key_sum,
    value_sum,
    *,
    step,
):
    length = length_ref[0]
    total = query_ref.shape[0]
    masks = key_masks(total, length)
    ones = jnp.ones((step, tile), low)
    keys = [one_head(key_ref[...], head, masks) for head in (0, 1)]
    plain_keys = [one_head(key_ref[...], head) for head in (0, 1)]
    values = [one_head(value_ref[...], head) for head in (0, 1)]
    key_sum[...] = jnp.zeros_like(key_sum)
    value_sum[...] = jnp.zeros_like(value_sum)
    strip_grad_ref[...] = jnp.zeros_like(strip_grad_ref)

    def body(index, carry):
        first = pl.multiple_of(index * step, step)
        queries = query_ref[pl.ds(first, step), :]
        grads = grad_ref[pl.ds(first, step), :]
        columns = strip_columns(total, first, step)
        inner = grads.astype(wide) * context_ref[pl.ds(first, step), :].astype(wide)
        query_grad = None
        for head in (0, 1):
            head_grads = one_head(grads, head)
            pick = one_head(jnp.ones((8, tile), wide), head)
            row_inner = lax.dot_general(
                pick,
                inner,
                (((1,), (1,)), ((), ())),
                precision=lax.Precision.HIGHEST,
                preferred_element_type=wide,
            )[:1]
            log_total = total_ref[0, head : head + 1, pl.ds(first, step)]
            products = dot(keys[head], one_head(queries, head, ones), 1, 1)
            probs = jnp.exp(add_bias(products, strip_ref, head, columns) - log_total)
            value_sum[...] += dot(probs.astype(low), head_grads, 1, 0)
            score_grad = probs * (dot(values[head], head_grads, 1, 1) - row_inner)
            for block, where in enumerate(columns):
                strip_grad_ref[head, :, where] += score_grad[block * tile : (block + 1) * tile]
            score_low = score_grad.astype(low)
            key_sum[...] += dot(score_low, one_head(queries, head), 1, 0)
            part = dot(score_low, plain_keys[head], 0, 0)
            query_grad = part if query_grad is None else query_grad + part
        query_grad_ref[pl.ds(first, step), :] = query_grad.astype(low)
        return carry

    lax.fori_loop(0, total // step, body, 0)
    key_grad_ref[...] = key_sum[...].astype(low)
    value_grad_ref[...] = value_sum[...].astype(low)


def attention_backward(
    steps, length, qkv, context, context_grad, log_totals, strips, start, held, step=256
):
    total = qkv.shape[0]
    pairs = qkv.shape[1] // (3 * tile)
    strip_width = strips.shape[2]

    def columns(which, first=start):
        return pl.BlockSpec((total, tile), lambda p, _: (0, which * pairs + first + p))

    part = pl.BlockSpec((total, tile), lambda p, _: (0, p))
    return steps.launch(
        "attention_backward",
        functools.partial(backward_kernel, step=step),
        [length, qkv, qkv, qkv, context, context_grad, log_totals, strips],
        [
            columns(0),
            columns(1),
            columns(2),
            columns(0, start - held),
            columns(0),
            pl.BlockSpec((1, 2, total), lambda p, _: (start - held + p, 0, 0)),
            pl.BlockSpec((2, tile, strip_width), lambda p, _: (start + p, 0, 0)),
        ],
        [part, part, part, pl.BlockSpec((2, tile, strip_width), lambda p, _: (p, 0, 0))],
        [((total, tile), low)] * 3 + [((2, tile, strip_width), wide)],
        scratch=[pltpu.VMEM((total, tile), wide)] * 2,
        memory=32,
        stored=(3,),
        estimate=(1e10, 6 << 20),
    )


def gelu_and_slope(values):
    distance = jnp.abs(values) * math.sqrt(0.5)
    ratio = 1.0 / (1.0 + 0.3275911 * distance)
    density = jnp.exp(-distance * distance)
    poly = 1.061405429 * ratio - 1.453152027
    poly = poly * ratio + 1.421413741
    poly = poly * ratio - 0.284496736
    poly = poly * ratio + 0.254829592
    tail = (0.5 * ratio) * poly * density
    cumulative = jnp.where(values >= 0, 1.0 - tail, tail)
    slope = cumulative + values * density * (1.0 / math.sqrt(2.0 * math.pi))
    return values * cumulative, slope


def beside(refs):
    return jnp.concatenate([ref[...] for ref in refs], axis=1)


def pinned(array):
    return pltpu.with_memory_space_constraint(array, pltpu.HBM)


def start_copies(index_ref, pieces, target, semaphores, columns=None):
    copies = []
    for number, piece in enumerate(pieces):
        for side in (0, 1):
            entry = 2 * number + side
            rows = piece.shape[-2]
            where = pl.ds(pl.multiple_of(index_ref[entry] * rows, rows), rows)
            if columns is not None:
                source, place = piece.at[side, :, columns], target.at[where, :]
            else:
                source, place = piece.at[side], target.at[:, where, :]
            copies.append(pltpu.make_async_copy(source, place, semaphores.at[entry]))
    for copy in copies:
        copy.start()
    return copies


def transposed_rows(order_ref, source_ref, target_ref, columns, chips, ordered):
    share = source_ref.shape[1] // chips
    for block in range(chips):
        if ordered:
            first = pl.multiple_of(order_ref[block] * share, share)
            part = source_ref[:, pl.ds(first, share)]
        else:
            part = source_ref[:, block * share : (block + 1) * share]
        target_ref[block * share : (block + 1) * share, columns] = part.T.astype(low)


def send_kernel(odd_ref, block_ref, first_ref, second_ref):
    @pl.when(pl.program_id(0) == 0)
    def _():
        first_ref[...] = block_ref[0]

    @pl.when(pl.program_id(0) == 1)
    def _():
        second_ref[...] = block_ref[0]


def send_blocks(steps, odd, blocks):
    shape = blocks.shape[1:]
    out = pl.BlockSpec(shape, lambda i, _: (0, 0))
    return steps.launch(
        "send_blocks",
        send_kernel,
        [odd, pinned(blocks)],
        [pl.BlockSpec((1,) + shape, lambda i, odd_ref: ((odd_ref[0] + i) % 2, 0, 0))],
        [out, out],
        [(shape, low)] * 2,
        grid=(2,),
        memory=8,
        estimate=(0, 2 << 20),
    )


def scaled(block, gain):
    return (gain * block.astype(wide)).astype(low)


def column_copies(core, weights, targets, semaphores, first=0, parts=1, part=0):
    copies = []
    for number, (weight, target) in enumerate(zip(weights, targets)):
        width = weight.shape[1] // (2 * parts)
        columns = pl.ds(pl.multiple_of((parts * core + part) * width, width), width)
        copies.append(
            pltpu.make_async_copy(weight.at[:, columns], target, semaphores.at[first + number])
        )
    return copies


def run_copies(copies):
    for copy in copies:
        copy.start()
    for copy in copies:
        copy.wait()


def side_kernel(core_ref, *refs):
    attention, feed = refs[:4], refs[4:6]
    gain_ref, out_ref, semaphores = refs[6:]
    core = 1 - core_ref[0]
    inner = attention[0].shape[1] // 2
    hidden = feed[0].shape[1] // 4
    targets = [out_ref.at[:, n * inner : (n + 1) * inner] for n in range(4)]
    copies = column_copies(core, attention, targets, semaphores)
    first = 4 * inner
    for part in (0, 1):
        start = first + 2 * part * hidden
        targets = [out_ref.at[:, start + n * hidden : start + (n + 1) * hidden] for n in (0, 1)]
        copies += column_copies(core, feed, targets, semaphores, 4 + 2 * part, 2, part)
    run_copies(copies)
    out_ref[:, : 3 * inner] = scaled(out_ref[:, : 3 * inner], gain_ref[:, :1])
    for part in (0, 1):
        columns = slice(first + 2 * part * hidden, first + (2 * part + 1) * hidden)
        out_ref[:, columns] = scaled(out_ref[:, columns], gain_ref[:, 1:])


def pair_kernel(first_ref, second_ref, out_ref):
    out_ref[0] = first_ref[...]
    out_ref[1] = second_ref[...]


def pair(steps, first, second):
    rows, width = first.shape
    step = rows // 2
    block = pl.BlockSpec((step, width), lambda i: (i, 0))
    return steps.launch(
        "pair",
        pair_kernel,
        [first, second],
        [block] * 2,
        [pl.BlockSpec((2, step, width), lambda i: (0, i, 0))],
        [((2, rows, width), low)],
        grid=(2,),
        prefetch=0,
        memory=8,
    )[0]


def other_side(steps, core, attention, feed, gains):
    rows = attention[0].shape[0]
    columns = sum(weight.shape[1] for weight in attention + feed) // 2
    return steps.launch(
        "other_side",
        side_kernel,
        [core, *map(pinned, (*attention, *feed)), gains],
        [in_hbm] * 6 + [in_vmem],
        [in_vmem],
        [((rows, columns), low)],
        scratch=[pltpu.SemaphoreType.DMA((8,))],
        memory=8,
    )[0]


def attention_shard_kernel(core_ref, *refs):
    attention = refs[:4]
    gain_ref, arrived_ref, out_ref, semaphores = refs[4:]
    inner = attention[0].shape[1] // 2
    targets = [out_ref.at[0, :, n * inner : (n + 1) * inner] for n in range(4)]
    copies = column_copies(core_ref[0], attention, targets, semaphores)
    source = arrived_ref.at[:, : 4 * inner]
    copies.append(pltpu.make_async_copy(source, out_ref.at[1], semaphores.at[4]))
    run_copies(copies)
    out_ref[0, :, : 3 * inner] = scaled(out_ref[0, :, : 3 * inner], gain_ref[:, :1])


def attention_shard(steps, core, weights, gains, arrived):
    rows = weights[0].shape[0]
    columns = sum(weight.shape[1] for weight in weights) // 2
    return steps.launch(
        "attention_shard",
        attention_shard_kernel,
        [core, *map(pinned, weights), gains, arrived],
        [in_hbm] * 4 + [in_vmem, anywhere],
        [in_vmem],
        [((2, rows, columns), low)],
        scratch=[pltpu.SemaphoreType.DMA((5,))],
        memory=8,
    )[0]


def hidden_shard_kernel(core_ref, *refs, part):
    feed = refs[:2]
    gain_ref, arrived_ref, out_ref, semaphores = refs[2:]
    hidden = out_ref.shape[3]
    targets = [out_ref.at[0, number] for number in (0, 1)]
    copies = column_copies(core_ref[0], feed, targets, semaphores, 0, 2, part)
    for number in (0, 1):
        start = 2 * hidden * (1 + part) + number * hidden
        source = arrived_ref.at[:, start : start + hidden]
        copies.append(
            pltpu.make_async_copy(source, out_ref.at[1, number], semaphores.at[2 + number])
        )
    run_copies(copies)
    out_ref[0, 0] = scaled(out_ref[0, 0], gain_ref[:, 1:])


def hidden_shard(steps, core, part, weights, gains, arrived):
    rows, columns = weights[0].shape
    return steps.launch(
        "hidden_shard",
        functools.partial(hidden_shard_kernel, part=part),
        [core, *map(pinned, weights), gains, arrived],
        [in_hbm] * 2 + [in_vmem, anywhere],
        [in_vmem],
        [((2, 2, rows, columns // 4), low)],
        scratch=[pltpu.SemaphoreType.DMA((4,))],
        memory=8,
    )[0]


def token_kernel(place_ref, *refs, normed, chips, ordered):
    halves = refs[:2]
    plain_ref, first_ref, first_t_ref, semaphores = refs[-4:]
    total = plain_ref.shape[0]
    step = total // 4
    copies = []
    for number in range(4):
        where = pl.ds(pl.multiple_of(place_ref[number] * step, step), step)
        source = halves[number // 2].at[number % 2]
        copies.append(
            pltpu.make_async_copy(source, plain_ref.at[where, :], semaphores.at[number])
        )
    for copy in copies:
        copy.start()
    for copy in copies:
        copy.wait()
    for block in range(4):
        rows = slice(block * step, (block + 1) * step)
        values = plain_ref[rows, :].astype(wide)
        if normed:
            values = normalize(values)[0]
        else:
            position = block * step + lax.broadcasted_iota(jnp.int32, values.shape, 0)
            values = jnp.where(position < place_ref[4], values, 0.0)
        first_ref[rows, :] = values.astype(low)
        transposed_rows(
            place_ref.at[pl.ds(5, chips)],
            first_ref.at[rows, :],
            first_t_ref,
            rows,
            chips,
            ordered,
        )


def token_rows_of(steps, places, pieces, normed, chips, ordered):
    total, width = 4 * pieces[0].shape[1], pieces[0].shape[2]
    return steps.launch(
        "token_rows" if normed else "cotangent_rows",
        functools.partial(token_kernel, normed=normed, chips=chips, ordered=ordered),
        [places, *pieces],
        [anywhere] * 2,
        [in_vmem] * 3,
        [((total, width), low), ((total, width), low), ((width, total), low)],
        scratch=[pltpu.SemaphoreType.DMA((4,))],
        memory=24,
        estimate=(0, 10 << 20),
    )


def rows_product_kernel(place_ref, *refs, factors, count, columns, across):
    rows = refs[:factors]
    pieces = refs[factors : factors + count]
    out_ref, weight, semaphores = refs[factors + count :]

    @pl.when(pl.program_id(0) == 0)
    def _():
        for copy in start_copies(place_ref, pieces, weight, semaphores, columns):
            copy.wait()

    operand = beside(rows)
    out_ref[...] = dot(operand, weight[...], 1, 1 if across else 0).astype(low)


def rows_product(steps, places, rows, pieces, first, last, across, name, step=256):
    total, depth = rows[0].shape
    count = len(pieces)
    whole = (2 * count * pieces[0].shape[1], last - first)
    width = whole[0] if across else whole[1]
    return steps.launch(
        name,
        functools.partial(
            rows_product_kernel,
            factors=len(rows),
            count=count,
            columns=pl.ds(first, last - first),
            across=across,
        ),
        [places, *rows, *pieces],
        [pl.BlockSpec((step, depth), lambda i, _: (i, 0))] * len(rows) + [anywhere] * count,
        [pl.BlockSpec((step, width), lambda i, _: (i, 0))],
        [((total, width), low)],
        grid=(total // step,),
        scratch=[pltpu.VMEM(whole, low), pltpu.SemaphoreType.DMA((2 * count,))],
        estimate=(2 * total * whole[0] * whole[1], 8 << 20),
    )[0]


def second_norm_kernel(
    order_ref, token_ref, mine_ref, other_ref, hidden_ref, normed_ref, normed_t_ref, *, chips, ordered
):
    attended = mine_ref[...].astype(wide) + other_ref[...].astype(wide)
    hidden = token_ref[...].astype(wide) + attended
    hidden_ref[...] = hidden
    normed_ref[...] = normalize(hidden)[0].astype(low)
    transposed_rows(order_ref, normed_ref, normed_t_ref, slice(None), chips, ordered)


def second_norm(steps, order, tokens, mine, other, chips, ordered, step=256):
    total, width = tokens.shape
    block = pl.BlockSpec((step, width), lambda i, _: (i, 0))
    return steps.launch(
        "second_norm",
        functools.partial(second_norm_kernel, chips=chips, ordered=ordered),
        [order, tokens, mine, other],
        [block] * 3,
        [block, block, pl.BlockSpec((width, step), lambda i, _: (0, i))],
        [((total, width), wide), ((total, width), low), ((width, total), low)],
        grid=(total // step,),
        estimate=(0, 14 << 20),
    )


def feed_forward_kernel(
    place_ref, normed_ref, normed_t_ref, grad_ref, grad_t_ref, *refs, count, first
):
    pieces = refs[:count]
    refs = refs[count:]
    if first:
        mixed_sum, normed_sum, keep_ref, send_ref, weight, semaphores = refs
        before = ()
    else:
        before = refs[:2]
        own_ref, other_ref, normed_grad_ref, keep_ref, send_ref = refs[2:7]
        weight, semaphores, mixed_sum, normed_sum = refs[7:]
    index = pl.program_id(0)
    step = keep_ref.shape[2]
    half = keep_ref.shape[1]
    carried = [
        pltpu.make_async_copy(source, target, semaphores.at[2 * count + number])
        for number, (source, target) in enumerate(zip(before, (mixed_sum, normed_sum)))
    ]

    @pl.when(index == 0)
    def _():
        copies = start_copies(place_ref, pieces, weight, semaphores)
        for copy in carried:
            copy.start()
        for copy in copies:
            copy.wait()

    columns = pl.ds(pl.multiple_of(index * step, step), step)
    expand = weight[0, :, columns]
    contract = weight[1, :, columns]
    pre_act = dot(normed_ref[...], expand, 1, 0)
    act_grad = dot(grad_ref[...], contract, 1, 0).astype(low).astype(wide)
    activated, slope = gelu_and_slope(pre_act)
    activated = activated.astype(low)
    pre_grad = (act_grad * slope).astype(low)
    for part, (rows_ref, values) in enumerate(
        ((normed_t_ref, pre_grad), (grad_t_ref, activated))
    ):
        keep_ref[part] = dot(rows_ref[:half, :], values, 1, 0).astype(low)
        send_ref[part] = dot(rows_ref[half:, :], values, 1, 0).astype(low)
    mixed = dot(activated, contract, 1, 1)
    normed_grad = dot(pre_grad, expand, 1, 1)
    if first:

        @pl.when(index == 0)
        def _():
            mixed_sum[...] = mixed
            normed_sum[...] = normed_grad

        @pl.when(index > 0)
        def _():
            mixed_sum[...] += mixed
            normed_sum[...] += normed_grad

    else:

        @pl.when(index == 0)
        def _():
            for copy in carried:
                copy.wait()

        mixed_sum[...] += mixed
        normed_sum[...] += normed_grad

        @pl.when(index == pl.num_programs(0) - 1)
        def _():
            rows = own_ref.shape[0]
            core = place_ref[2 * count]
            own = pl.multiple_of(core * rows, rows)
            away = pl.multiple_of((1 - core) * rows, rows)
            own_ref[...] = mixed_sum[pl.ds(own, rows), :].astype(low)
            other_ref[...] = mixed_sum[pl.ds(away, rows), :].astype(low)
            normed_grad_ref[...] = normed_sum[...].astype(low)


def feed_forward(steps, places, normed, normed_t, grad, grad_t, pieces, before=None, step=512):
    rows, width = normed.shape
    count = len(pieces)
    hidden = pieces[0].shape[3]
    first = before is None

    def fixed(shape):
        return pl.BlockSpec(shape, lambda i, _: (0,) * len(shape), pipeline_mode=pl.Buffered(1))

    whole = fixed((rows, width))
    scratch = [
        pltpu.VMEM((2, width, hidden), low),
        pltpu.SemaphoreType.DMA((2 * count + 2,)),
    ]
    if first:
        before = ()
        out_specs = [whole, whole]
        out_shape = [((rows, width), wide)] * 2
    else:
        part = fixed((rows // 2, width))
        out_specs = [part, part, whole]
        out_shape = [((rows // 2, width), low)] * 2 + [((rows, width), low)]
        scratch += [pltpu.VMEM((rows, width), wide)] * 2
    return steps.launch(
        "feed_forward",
        functools.partial(feed_forward_kernel, count=count, first=first),
        [places, normed, normed_t, grad, grad_t, *pieces, *before],
        [whole, fixed((width, rows))] * 2 + [anywhere] * (count + len(before)),
        out_specs + [pl.BlockSpec((2, width // 2, step), lambda i, _: (0, 0, i))] * 2,
        out_shape + [((2, width // 2, hidden), low)] * 2,
        grid=(hidden // step,),
        scratch=scratch,
        memory=58,
        stored=(0, 1) if first else (),
        estimate=(20 * rows * width * hidden, 40 << 20),
    )


def hidden_back_kernel(
    place_ref, mine_ref, other_ref, hidden_ref, grad_ref, *refs, count, columns, chips, ordered
):
    pieces = refs[:count]
    hidden_grad_ref, low_ref, low_t_ref, context_grad_ref, weight, semaphores = refs[count:]

    @pl.when(pl.program_id(0) == 0)
    def _():
        for copy in start_copies(place_ref, pieces, weight, semaphores, columns):
            copy.wait()

    upstream = mine_ref[...].astype(wide) + other_ref[...].astype(wide)
    hidden = hidden_ref[...]
    scale = normalize(hidden)[1]
    hidden_grad = grad_ref[...].astype(wide) + normalize_back(hidden, scale, upstream)
    hidden_grad_ref[...] = hidden_grad
    low_ref[...] = hidden_grad.astype(low)
    context_grad_ref[...] = dot(low_ref[...], weight[...], 1, 0).astype(low)
    order_ref = place_ref.at[pl.ds(2 * count + 1, chips)]
    transposed_rows(order_ref, low_ref, low_t_ref, slice(None), chips, ordered)


def hidden_back(
    steps, places, mine, other, hidden, grad, pieces, first, last, chips, ordered, step=256
):
    total, width = hidden.shape
    count = len(pieces)
    inner = last - first
    block = pl.BlockSpec((step, width), lambda i, _: (i, 0))
    return steps.launch(
        "hidden_back",
        functools.partial(
            hidden_back_kernel,
            count=count,
            columns=pl.ds(first, inner),
            chips=chips,
            ordered=ordered,
        ),
        [places, mine, other, hidden, grad, *pieces],
        [block] * 4 + [anywhere] * count,
        [
            block,
            block,
            pl.BlockSpec((width, step), lambda i, _: (0, i)),
            pl.BlockSpec((step, inner), lambda i, _: (i, 0)),
        ],
        [((total, width), wide), ((total, width), low), ((width, total), low), ((total, inner), low)],
        grid=(total // step,),
        scratch=[pltpu.VMEM((width, inner), low), pltpu.SemaphoreType.DMA((2 * count,))],
        estimate=(4 * total * width * inner, 24 << 20),
    )


def terms_kernel(*refs, contexts):
    grad_t_ref, normed_t_ref = refs[:2]
    factors = refs[2:-2]
    for number, target in enumerate(refs[-2:]):

        @pl.when(pl.program_id(0) == number)
        def _():
            first = 0
            if contexts:
                part = dot(grad_t_ref[...], beside(factors[:contexts]), 1, 0)
                first = part.shape[1]
                target[:, :first] = part.astype(low)
            part = dot(normed_t_ref[...], beside(factors[contexts:]), 1, 0)
            target[:, first:] = part.astype(low)


def attention_terms(steps, grad_t, normed_t, contexts, grads):
    width, total = normed_t.shape
    factors = list(contexts) + list(grads)
    columns = sum(factor.shape[1] for factor in factors)
    block = pl.BlockSpec((width // 2, total), lambda i: (i, 0))
    fixed = pl.BlockSpec((width // 2, columns), lambda i: (0, 0))
    return steps.launch(
        "attention_terms",
        functools.partial(terms_kernel, contexts=len(contexts)),
        [grad_t, normed_t, *factors],
        [block, block]
        + [
            pl.BlockSpec(factor.shape, lambda i: (0, 0), pipeline_mode=pl.Buffered(1))
            for factor in factors
        ],
        [fixed, fixed],
        [((width // 2, columns), low)] * 2,
        grid=(2,),
        prefetch=0,
        estimate=(2 * total * width * columns, 10 << 20),
    )


def sum_kernel(*refs):
    total = refs[0][...].astype(wide)
    for ref in refs[1:-1]:
        total += ref[...].astype(wide)
    refs[-1][...] = total.astype(low)


def row_sums(steps, parts):
    first = parts[0]
    rows = first[0].shape[-2] // (1 if first[1] is None else 2)
    shape = first[0].shape[:-2] + (rows, first[0].shape[-1])
    count = 4
    block = shape[:-2] + (rows // count, shape[-1])
    leading = (0,) * (len(shape) - 2)

    def spec(offset):
        return pl.BlockSpec(block, lambda i: leading + (i + offset, 0))

    return steps.launch(
        "row_sums",
        sum_kernel,
        [part for part, _ in parts],
        [spec(count if which else 0) for _, which in parts],
        [spec(0)],
        [(shape, low)],
        grid=(count,),
        prefetch=0,
        memory=12,
        estimate=(0, 4 << 20),
    )[0]


def input_product_kernel(place_ref, *refs, count, factors):
    grads = refs[:factors]
    pieces = refs[factors : factors + count]
    own_ref, other_ref, weight, semaphores = refs[factors + count :]
    index = pl.program_id(0)

    @pl.when(index == 0)
    def _():
        columns = pl.ds(0, weight.shape[1])
        for copy in start_copies(place_ref, pieces, weight, semaphores, columns):
            copy.wait()

    ordered = [ref for block in range(3) for ref in grads[block::3]]
    product = dot(beside(ordered), weight[...], 1, 1)

    @pl.when(index < 2)
    def _():
        other_ref[...] = product.astype(low)

    @pl.when(index >= 2)
    def _():
        own_ref[...] = product


def input_product(steps, places, grads, pieces):
    total = grads[0].shape[0]
    count = len(pieces)
    inner = sum(grad.shape[1] for grad in grads)
    width = 2 * count * pieces[0].shape[1]
    step = total // 4

    def rows(i, place_ref):
        core = place_ref[2 * count]
        return (jnp.where(i < 2, 2 * (1 - core) + i, 2 * core + i - 2), 0)

    return steps.launch(
        "input_product",
        functools.partial(input_product_kernel, count=count, factors=len(grads)),
        [places, *grads, *pieces],
        [pl.BlockSpec((step, grad.shape[1]), rows) for grad in grads] + [anywhere] * count,
        [
            pl.BlockSpec((step, width), lambda i, _: (jnp.maximum(i - 2, 0), 0)),
            pl.BlockSpec((step, width), lambda i, _: (jnp.minimum(i, 1), 0)),
        ],
        [((total // 2, width), wide), ((total // 2, width), low)],
        grid=(4,),
        scratch=[pltpu.VMEM((width, inner), low), pltpu.SemaphoreType.DMA((2 * count,))],
        memory=24,
        estimate=(2 * total * width * inner, 14 << 20),
    )


def finish_kernel(
    place_ref, own_ref, other_ref, base_ref, token_ref, first_ref, second_ref, *, back
):
    index = pl.program_id(0)
    summed = own_ref[...].astype(wide) + other_ref[...].astype(wide)
    if back:
        tokens = token_ref[...].astype(wide)
        values = base_ref[...] + normalize_back(tokens, normalize(tokens)[1], summed)
    else:
        row = (2 * place_ref[0] + index) * summed.shape[0]
        position = row + lax.broadcasted_iota(jnp.int32, summed.shape, 0)
        values = jnp.where(position < place_ref[2], base_ref[...] + summed, 0.0)
    values = values.astype(low)

    @pl.when(index == place_ref[1])
    def _():
        first_ref[...] = values

    @pl.when(index != place_ref[1])
    def _():
        second_ref[...] = values


def finish_half(steps, core, odd, length, own, other, base, tokens, back):
    rows, width = own.shape
    step = rows // 2
    half = pl.BlockSpec((step, width), lambda i, _: (i, 0))
    whole = pl.BlockSpec((step, width), lambda i, place_ref: (2 * place_ref[0] + i, 0))
    quarter = pl.BlockSpec((step, width), lambda i, _: (0, 0))
    return steps.launch(
        "input_gradient_rows" if back else "result_rows",
        functools.partial(finish_kernel, back=back),
        [jnp.stack([core, odd, length]).astype(jnp.int32), own, other, base, tokens],
        [half, half, whole, whole],
        [quarter, quarter],
        [((step, width), low)] * 2,
        grid=(2,),
        memory=12,
        estimate=(0, 6 << 20),
    )


def pick_kernel(slot_ref, *refs, count):
    pieces = refs[:count]
    own_ref, other_ref, semaphores = refs[count:]
    for row in range(4):
        target = (own_ref if row < 2 else other_ref).at[row % 2]
        for number in range(2 * count):

            @pl.when(slot_ref[row] == slot_ref[4 + number])
            def _():
                source = pieces[number // 2].at[number % 2]
                copy = pltpu.make_async_copy(source, target, semaphores.at[row])
                copy.start()
                copy.wait()


def pick_slots(steps, slots, pieces):
    count = len(pieces)
    return steps.launch(
        "pick_slots",
        functools.partial(pick_kernel, count=count),
        [slots, *pieces],
        [anywhere] * count,
        [in_vmem] * 2,
        [(pieces[0].shape, low)] * 2,
        scratch=[pltpu.SemaphoreType.DMA((4,))],
        memory=8,
        estimate=(0, 4 << 20),
    )


def normalize(values):
    scaled = lax.rsqrt(jnp.mean(values * values, axis=-1, keepdims=True) + epsilon)
    return (values * scaled, scaled)


def normalize_back(values, scaled, upstream):
    unit_rows = values * scaled
    return scaled * (upstream - unit_rows * jnp.mean(upstream * unit_rows, axis=-1, keepdims=True))


class Links:
    def __init__(self, buckets):
        self.buckets = buckets
        self.shards = lax.axis_size("fsdp")
        self.depth = lax.axis_size("ctx")
        self.shard = lax.axis_index("fsdp")
        self.level = lax.axis_index("ctx")
        self.chips = self.shards // 2
        self.chip = self.shard // 2
        self.core = self.shard % 2
        self.groups = [list(range(core, self.shards, 2)) for core in (0, 1)]
        self.square = self.chips == 4

    def sibling(self, array):
        return lax.ppermute(array, "fsdp", [(i, i ^ 1) for i in range(self.shards)])

    def across(self, array, bit):
        return lax.ppermute(array, "fsdp", [(i, i ^ (2 * bit)) for i in range(self.shards)])

    def in_order(self, mine, other):
        return jnp.concatenate(
            [jnp.where(self.core == 0, mine, other), jnp.where(self.core == 0, other, mine)], axis=0
        )

    def turn(self, array, second):
        pairs = [(i, i ^ (2 if (i % 2 == 0) != second else 4)) for i in range(self.shards)]
        return lax.ppermute(array, "fsdp", pairs)

    def order(self):
        if not self.square:
            return list(range(self.chips))
        return [self.chip, self.chip ^ (1 + self.core), self.chip ^ (2 - self.core), self.chip ^ 3]

    def gather(self, shard):
        if not self.square:
            whole = lax.all_gather(shard, "fsdp", axis=0, axis_index_groups=self.groups)
            return [whole[chip] for chip in range(self.chips)]
        first = self.turn(shard, False)
        second = self.turn(shard, True)
        return [shard, first, second, self.turn(first, True)]

    def weight_places(self):
        return [2 * chip + side for chip in self.order() for side in (self.core, 1 - self.core)]

    def scatter(self, keep, send):
        dim = keep.ndim - 2
        if not self.square:
            summed = lax.psum_scatter(
                jnp.concatenate([keep, send], axis=dim),
                "fsdp",
                scatter_dimension=dim,
                tiled=True,
                axis_index_groups=self.groups,
            )
            return keep, summed.astype(low)
        return keep, self.turn(send, True)

    def scatter_near(self, steps, terms):
        keep, arrived = terms
        if not self.square:
            return keep, arrived, None
        near = row_sums(steps, [(keep, True), (arrived, True)])
        return keep, arrived, self.turn(near, False)

    def scatter_own(self, steps, terms):
        keep, arrived, last = terms
        total = arrived
        if self.square:
            total = row_sums(steps, [(keep, False), (arrived, False), (last, None)])
        return total, lax.ppermute(total, "ctx", [(0, 1), (3, 2)])

    def small_hops(self, small):
        hops = []
        bit = 1
        while bit < self.chips:
            hops.append(("fsdp", [(i, i ^ (2 * bit)) for i in range(self.shards)]))
            bit *= 2
        bit = 1
        while bit < self.depth:
            hops.append(("ctx", [(i, i ^ bit) for i in range(self.depth)]))
            bit *= 2
        for axis, pairs in hops:
            other = lax.ppermute(small, axis, pairs)
            lane = lax.broadcasted_iota(jnp.int32, small.shape, 1)
            small = jnp.where(lane < self.buckets, small + other, jnp.maximum(small, other))
            yield small

    def level_across(self, steps, terms):
        joined = row_sums(steps, [(part, None) for part in terms])
        return joined, lax.ppermute(joined, "ctx", [(1, 2), (2, 1)])

    def level_out(self, steps, terms):
        total = row_sums(steps, [(part, None) for part in terms])
        outward = lax.ppermute(total, "ctx", [(1, 0), (2, 3)])
        inner = (self.level == 1) | (self.level == 2)
        return self.exchange_rows(jnp.where(inner, total, outward))

    def exchange_rows(self, rows):
        dim = rows.ndim - 2
        half = rows.shape[dim] // 2
        mine = lax.dynamic_slice_in_dim(rows, self.core * half, half, dim)
        other = self.sibling(lax.dynamic_slice_in_dim(rows, (1 - self.core) * half, half, dim))
        return jnp.where(self.core == 0, mine, other), jnp.where(self.core == 0, other, mine)

    def trade(self, array, outward, swapped):
        pairs = []
        for level in range(self.depth):
            for shard in range(self.shards):
                chip, core = divmod(shard, 2)
                side, odd = divmod(level, 2)
                slot = odd if not swapped else 1 - odd
                held = level * self.shards + shard
                worked = (2 * core + slot) * self.shards + 2 * chip + side
                pairs.append((held, worked) if outward else (worked, held))
        return lax.ppermute(array, ("ctx", "fsdp"), pairs)

    def to_slot(self, sends):
        return self.trade(sends[0], True, False), self.trade(sends[1], True, True)

    def both_halves(self, steps, trades):
        half = pair(steps, *trades)
        return half, self.sibling(half)

    def quarter_places(self):
        odd = self.level % 2
        near, far = 2 * self.core, 2 * (1 - self.core)
        return [near + odd, near + 1 - odd, far + odd, far + 1 - odd]

    def from_slot(self, quarters):
        return self.trade(quarters[0], False, False), self.trade(quarters[1], False, True)

    def received(self, trades):
        first, second = trades
        flip = self.level % 2 == 0
        return jnp.stack([jnp.where(flip, first, second), jnp.where(flip, second, first)])


def local(
    tokens,
    cotangent,
    sequence_lengths,
    slot_sequence,
    offset_bucket,
    first_gain,
    second_gain,
    query_weight,
    key_weight,
    value_weight,
    output_weight,
    expand_weight,
    contract_weight,
    bias_table,
    clip_limit,
):
    links = Links(bias_table.shape[0])
    core = links.core
    held_count, local_length, model_width = tokens.shape
    total_length = local_length * links.depth
    bucket_count, head_count = bias_table.shape
    inner_width = query_weight.shape[1]
    head_size = inner_width // head_count
    own_heads = head_count // 2
    own_inner = inner_width // 2
    slot_count = slot_sequence.shape[0]
    assert held_count == 2 and links.depth == 4

    slots = jnp.arange(slot_count)
    slot = links.chip * (2 * held_count) + links.level
    sequence = jnp.sum(jnp.where(slots == slot, slot_sequence, 0))
    length = jnp.sum(jnp.where(slots == sequence, sequence_lengths, 0)).astype(jnp.int32)
    odd = links.level % 2

    def numbers(*values):
        return jnp.stack([jnp.asarray(value, jnp.int32) for value in values])

    core_line = numbers(core)
    first_column = first_gain.astype(wide)[:, None]
    second_column = second_gain.astype(wide)[:, None]
    gains = jnp.concatenate([first_column, second_column], axis=1)
    attention_weights = (query_weight, key_weight, value_weight, output_weight)
    feed_weights = (expand_weight, contract_weight)
    steps = Steps()
    odd_line = odd.reshape(1)
    chips, square = links.chips, links.square
    order = links.order()
    places = numbers(*links.weight_places(), core, *order)
    order_line = numbers(*order)
    slot_places = numbers(*links.quarter_places(), length, *order)
    length_line = length.reshape(1)

    line_width = 2 * total_length
    falling = jnp.concatenate([jnp.flip(offset_bucket), jnp.full((1,), -1, jnp.int32)])
    matching = falling[:, None] == jnp.arange(bucket_count)[None, :]
    own_table = lax.dynamic_slice_in_dim(bias_table, core * own_heads, own_heads, 1)
    lines = dot(own_table, matching.astype(low), 0, 1)

    token_trades = links.to_slot(send_blocks(steps, odd_line, tokens))
    arrived = links.sibling(other_side(steps, core_line, attention_weights, feed_weights, gains))
    attention_pieces = links.gather(
        attention_shard(steps, core_line, attention_weights, gains, arrived)
    )
    strips = bias_strips(steps, lines.reshape(own_heads, 1, line_width))
    cotangent_sends = send_blocks(steps, odd_line, cotangent)
    late_shard = hidden_shard(steps, core_line, 1, feed_weights, gains, arrived)
    token_halves = links.both_halves(steps, token_trades)
    steps.wait(*attention_pieces[1:3])
    early_shard = hidden_shard(steps, core_line, 0, feed_weights, gains, arrived)
    cotangent_trades = links.to_slot(cotangent_sends)
    early_pieces = links.gather(early_shard)
    token_low, normed_one, normed_one_t = token_rows_of(
        steps, slot_places, token_halves, True, chips, square
    )
    qkv_width = 3 * own_inner
    qkv = rows_product(
        steps, places, [normed_one], attention_pieces, 0, qkv_width, False, "qkv_product"
    )
    pairs = own_inner // tile
    half_pairs = pairs // 2
    forward = functools.partial(attention_forward, steps, length_line, qkv, strips)
    first_context, first_totals, first_tops = forward(0, half_pairs)
    cotangent_halves = links.both_halves(steps, cotangent_trades)
    steps.wait(*early_pieces[1:3])
    last_context, last_totals, last_tops = forward(half_pairs, half_pairs)
    contexts = [first_context, last_context]
    output_columns = (qkv_width, qkv_width + own_inner)
    attended = rows_product(
        steps, places, contexts, attention_pieces, *output_columns, True, "attended_product"
    )
    attended_other = links.sibling(attended)
    _, out_low, out_low_t = token_rows_of(
        steps, slot_places, cotangent_halves, False, chips, square
    )
    late_pieces = links.gather(late_shard)
    hidden_one, normed_two, normed_two_t = second_norm(
        steps, order_line, token_low, attended, attended_other, chips, square
    )
    operands = (normed_two, normed_two_t, out_low, out_low_t)
    steps.wait(late_pieces[1])
    mixed_sum, normed_sum, *early_terms = feed_forward(steps, places, *operands, early_pieces)
    early = links.scatter(*early_terms)
    mixed_own, mixed_away, normed_two_part, *late_terms = feed_forward(
        steps, places, *operands, late_pieces, (mixed_sum, normed_sum)
    )
    normed_two_other = links.sibling(normed_two_part)
    mixed_other = links.sibling(mixed_away)
    late = links.scatter(*late_terms)
    early = links.scatter_near(steps, early)
    hidden_grad, attended_grad, attended_grad_t, context_grad = hidden_back(
        steps,
        places,
        normed_two_part,
        normed_two_other,
        hidden_one,
        out_low,
        attention_pieces,
        *output_columns,
        chips,
        square,
    )
    result_quarters = finish_half(
        steps, core, odd, length, mixed_own, mixed_other, hidden_one, token_low, False
    )
    result_trades = links.from_slot(result_quarters)

    def backward(pair):
        half = pair // half_pairs
        return attention_backward(
            steps,
            length_line,
            qkv,
            contexts[half],
            context_grad,
            (first_totals, last_totals)[half],
            strips,
            pair,
            half * half_pairs,
        )

    *grads_a, strips_a = backward(0)
    *grads_b, strips_b = backward(1)
    early = links.scatter_own(steps, early)
    late = links.scatter_near(steps, late)
    first = links.scatter(
        *attention_terms(steps, attended_grad_t, normed_one_t, contexts, grads_a + grads_b)
    )
    *grads_c, strips_c = backward(2)
    late = links.scatter_own(steps, late)
    *grads_d, strips_d = backward(3)
    early = links.level_across(steps, early)
    first = links.scatter_near(steps, first)
    last = links.scatter(
        *attention_terms(steps, attended_grad_t, normed_one_t, (), grads_c + grads_d)
    )
    own_part, away_part = input_product(
        steps, places, grads_a + grads_b + grads_c + grads_d, attention_pieces
    )
    away_other = links.sibling(away_part)
    first = links.scatter_own(steps, first)
    late = links.level_across(steps, late)
    last = links.scatter_near(steps, last)
    early_left, early_right = links.level_out(steps, early)
    input_quarters = finish_half(
        steps, core, odd, length, own_part, away_other, hidden_grad, token_low, True
    )
    last = links.scatter_own(steps, last)
    first = links.level_across(steps, first)
    result_pieces = links.gather(links.received(result_trades))
    late_left, late_right = links.level_out(steps, late)
    input_trades = links.from_slot(input_quarters)
    last = links.level_across(steps, last)
    first_left, first_right = links.level_out(steps, first)
    diagonals = jnp.concatenate(
        [diagonal_sums(steps, part) for part in (strips_a, strips_b, strips_c, strips_d)], axis=0
    ).reshape(own_heads, line_width)
    table_grad = lax.dot_general(
        diagonals,
        matching.astype(wide),
        (((1,), (0,)), ((), ())),
        precision=lax.Precision.HIGHEST,
        preferred_element_type=wide,
    )
    tops = jnp.concatenate([first_tops, last_tops], axis=0).reshape(own_heads, tile)
    small = jnp.concatenate([table_grad, tops[:, : tile - bucket_count]], axis=1)
    for small in links.small_hops(small):
        pass
    last_left, last_right = links.level_out(steps, last)
    input_gradient = links.received(input_trades).astype(wide)

    def slot_of(wanted):
        return jnp.sum(jnp.where(slot_sequence == wanted, slots, 0))

    own_slots = [slot_of(links.shard * held_count + row) for row in range(held_count)]
    other_slots = [slot_of((links.shard ^ 1) * held_count + row) for row in range(held_count)]
    piece_slots = [
        (2 * chip + core) * held_count + row
        for chip in order
        for row in range(held_count)
    ]
    picked, picked_other = pick_slots(
        steps,
        numbers(*own_slots, *other_slots, *piece_slots),
        result_pieces,
    )
    from_other = links.sibling(picked_other)
    output = jnp.stack(
        [
            jnp.where((s // held_count) % 2 == core, picked[row], from_other[row])
            for row, s in enumerate(own_slots)
        ]
    )

    def side_by_side(*parts):
        return jnp.concatenate(parts, axis=1).astype(wide)

    raw_two = side_by_side(early_left[0], late_left[0], early_right[0], late_right[0])
    contract_weight_gradient = side_by_side(
        early_left[1], late_left[1], early_right[1], late_right[1]
    )

    output_weight_gradient = side_by_side(first_left[:, :own_inner], first_right[:, :own_inner])

    def inner_columns(block):
        pieces = []
        for first_side, last_side in ((first_left, last_left), (first_right, last_right)):
            for start, side in ((own_inner, first_side), (0, last_side)):
                for pair in range(half_pairs):
                    first = start + (3 * pair + block) * tile
                    pieces.append(side[:, first : first + tile])
        return side_by_side(*pieces)

    raw_query, raw_key, raw_value = (inner_columns(block) for block in range(3))
    first_gain_gradient = jnp.sum(
        query_weight.astype(wide) * raw_query
        + key_weight.astype(wide) * raw_key
        + value_weight.astype(wide) * raw_value,
        axis=1,
    )
    second_gain_gradient = jnp.sum(expand_weight.astype(wide) * raw_two, axis=1)
    query_weight_gradient = first_column * raw_query
    key_weight_gradient = first_column * raw_key
    value_weight_gradient = first_column * raw_value
    expand_weight_gradient = second_column * raw_two

    small = links.in_order(small, links.sibling(small))
    table_rows = bucket_count // links.shards
    bias_table_gradient = lax.dynamic_slice_in_dim(
        small[:, :bucket_count].T, links.shard * table_rows, table_rows, 0
    )
    largest = small[:, bucket_count]
    shrink = clip_limit / jnp.maximum(clip_limit, largest)
    column_scale = jnp.repeat(jnp.sqrt(shrink), head_size)
    new_query_weight = query_weight.astype(wide) * column_scale[None, :]
    new_key_weight = key_weight.astype(wide) * column_scale[None, :]
    return (
        output,
        input_gradient,
        first_gain_gradient,
        second_gain_gradient,
        query_weight_gradient,
        key_weight_gradient,
        value_weight_gradient,
        output_weight_gradient,
        expand_weight_gradient,
        contract_weight_gradient,
        bias_table_gradient,
        largest,
        new_query_weight,
        new_key_weight,
    )


def solution(mesh):
    return jax.shard_map(
        local,
        mesh=mesh,
        in_specs=(
            P("fsdp", "ctx", None),
            P("fsdp", "ctx", None),
            P(),
            P(),
            P(),
            P("fsdp"),
            P("fsdp"),
            P("fsdp", None),
            P("fsdp", None),
            P("fsdp", None),
            P("fsdp", None),
            P("fsdp", None),
            P("fsdp", None),
            P(),
            P(),
        ),
        out_specs=(
            P("fsdp", "ctx", None),
            P("fsdp", "ctx", None),
            P("fsdp"),
            P("fsdp"),
            P("fsdp", None),
            P("fsdp", None),
            P("fsdp", None),
            P("fsdp", None),
            P("fsdp", None),
            P("fsdp", None),
            P("fsdp", None),
            P(),
            P("fsdp", None),
            P("fsdp", None),
        ),
        check_vma=False,
    )
```

```python
import functools
import math

import jax
import jax.numpy as jnp
from jax import lax
from jax.experimental import pallas as pl
from jax.experimental.pallas import tpu as pltpu
from jax.sharding import PartitionSpec as P

epsilon = 1e-06
masked = -1e30
tile = 128
half_tile = 64
wide = jnp.float32
low = jnp.bfloat16
anywhere = pl.BlockSpec(memory_space=pl.ANY)
in_vmem = pl.BlockSpec(memory_space=pltpu.VMEM)
in_hbm = pl.BlockSpec(memory_space=pltpu.HBM)


def pinned(array):
    return pltpu.with_memory_space_constraint(array, pltpu.HBM)


class Steps:
    def __init__(self):
        self.behind = ()

    def wait(self, *arrays):
        self.behind += arrays

    def launch(
        self,
        name,
        kernel,
        operands,
        in_specs,
        out_specs,
        out_shape,
        grid=(1,),
        prefetch=1,
        scratch=(),
        estimate=(0, 1 << 20),
        memory=24,
        stored=(),
    ):
        inputs, idle = len(operands), self.behind

        def run(*refs):
            refs = list(refs)
            mark_ref = refs.pop(inputs + len(idle) + len(out_specs))
            mark_ref[...] = jnp.zeros_like(mark_ref)
            kernel(*refs[:inputs], *refs[inputs + len(idle) :])

        out_specs, out_shape = list(out_specs), list(out_shape)
        outs = pl.pallas_call(
            run,
            grid_spec=pltpu.PrefetchScalarGridSpec(
                num_scalar_prefetch=prefetch,
                grid=grid,
                in_specs=list(in_specs) + [anywhere] * len(idle),
                out_specs=out_specs + [pl.BlockSpec((8, tile), lambda *_: (0, 0))],
                scratch_shapes=list(scratch),
            ),
            out_shape=[
                pltpu.HBM(shape, kind) if number in stored else jax.ShapeDtypeStruct(shape, kind)
                for number, (shape, kind) in enumerate(out_shape + [((8, tile), wide)])
            ],
            compiler_params=pltpu.CompilerParams(vmem_limit_bytes=memory << 20),
            cost_estimate=pl.CostEstimate(
                flops=int(estimate[0]), bytes_accessed=int(estimate[1]), transcendentals=0
            ),
            name=name,
        )(*operands, *idle)
        self.behind = (outs[-1],)
        return outs[:-1]


def dot(left, right, left_dim, right_dim):
    return lax.dot_general(
        left, right, (((left_dim,), (right_dim,)), ((), ())), preferred_element_type=wide
    )


def strip_kernel(line_ref, strip_ref):
    width = line_ref.shape[-1]
    rows = jnp.broadcast_to(line_ref[0], (tile, width))
    strip_ref[0] = pltpu.roll(rows, width - (tile - 1), 1, stride=1, stride_axis=0)


def bias_strips(steps, lines):
    heads, _, width = lines.shape
    return steps.launch(
        "bias_strips",
        strip_kernel,
        [lines],
        [pl.BlockSpec((1, 1, width), lambda h: (h, 0, 0))],
        [pl.BlockSpec((1, tile, width), lambda h: (h, 0, 0))],
        [((heads, tile, width), wide)],
        grid=(heads,),
        prefetch=0,
        memory=16,
        stored=(0,),
        estimate=(0, 8 << 20),
    )[0]


def diagonal_kernel(strip_ref, line_ref):
    strip = strip_ref[0]
    rows = tile
    while rows > 1:
        rows //= 2
        strip = pltpu.roll(strip[:rows], rows, 1) + strip[rows:]
    line_ref[0] = strip


def diagonal_sums(steps, strips):
    heads, _, width = strips.shape
    return steps.launch(
        "diagonal_sums",
        diagonal_kernel,
        [strips],
        [pl.BlockSpec((1, tile, width), lambda h: (h, 0, 0))],
        [pl.BlockSpec((1, 1, width), lambda h: (h, 0, 0))],
        [((heads, 1, width), wide)],
        grid=(heads,),
        prefetch=0,
        memory=16,
        estimate=(0, 2 << 20),
    )[0]


def one_head(block, head, extra=None):
    lane = lax.broadcasted_iota(jnp.int32, block.shape, 1)
    kept = jnp.where((lane >= half_tile) if head else (lane < half_tile), block, 0)
    if extra is None:
        return kept
    return jnp.where(lane == (0 if head else half_tile), extra, kept)


def key_masks(total, length):
    position = lax.broadcasted_iota(jnp.int32, (total, tile), 0)
    return jnp.where(position < length, 0.0, masked).astype(low)


def strip_columns(total, first, width):
    return [
        pl.ds(pl.multiple_of(total - tile - row + first, tile), width)
        for row in range(0, total, tile)
    ]


def add_bias(products, strip_ref, head, columns):
    return jnp.concatenate(
        [
            products[block * tile : (block + 1) * tile] + strip_ref[head, :, where]
            for block, where in enumerate(columns)
        ],
        axis=0,
    )


def forward_kernel(
    length_ref, query_ref, key_ref, value_ref, strip_ref, context_ref, total_ref, top_ref, *, step
):
    length = length_ref[0]
    total = query_ref.shape[0]
    masks = key_masks(total, length)
    ones = jnp.ones((step, tile), low)
    keys = [one_head(key_ref[...], head, masks) for head in (0, 1)]
    values = [one_head(value_ref[...], head).astype(wide).T.astype(low) for head in (0, 1)]

    def body(index, tops):
        first = pl.multiple_of(index * step, step)
        queries = query_ref[pl.ds(first, step), :]
        columns = strip_columns(total, first, step)
        query_okay = first + lax.broadcasted_iota(jnp.int32, (1, step), 1) < length
        context = None
        peaks = []
        for head in (0, 1):
            products = dot(keys[head], one_head(queries, head, ones), 1, 1)
            scores = add_bias(products, strip_ref, head, columns)
            row_max = jnp.max(scores, axis=0, keepdims=True)
            exponent = jnp.exp(scores - row_max)
            summed = jnp.sum(exponent, axis=0, keepdims=True)
            part = dot(values[head], exponent.astype(low), 1, 0) * (1.0 / summed)
            context = part if context is None else context + part
            total_ref[0, head : head + 1, pl.ds(first, step)] = row_max + jnp.log(summed)
            peaks.append(
                jnp.where(query_okay, jnp.max(products, axis=0, keepdims=True), masked)
            )
        context_ref[pl.ds(first, step), :] = context.T.astype(low)
        return tuple(jnp.maximum(top, peak) for top, peak in zip(tops, peaks))

    tops = lax.fori_loop(
        0, total // step, body, tuple(jnp.full((1, step), masked, wide) for _ in (0, 1))
    )
    for head in (0, 1):
        peak = jnp.max(tops[head], axis=1, keepdims=True)
        top_ref[0, head : head + 1, :] = jnp.broadcast_to(peak, (1, tile))


def attention_forward(steps, length, qkv, strips, start, count, step=512):
    total = qkv.shape[0]
    pairs = qkv.shape[1] // (3 * tile)
    strip_width = strips.shape[2]

    def columns(which):
        return pl.BlockSpec((total, tile), lambda p, _: (0, which * pairs + start + p))

    return steps.launch(
        "attention_forward",
        functools.partial(forward_kernel, step=step),
        [length, qkv, qkv, qkv, pinned(strips)],
        [columns(which) for which in range(3)]
        + [pl.BlockSpec((2, tile, strip_width), lambda p, _: (start + p, 0, 0))],
        [
            pl.BlockSpec((total, tile), lambda p, _: (0, p)),
            pl.BlockSpec((1, 2, total), lambda p, _: (p, 0, 0)),
            pl.BlockSpec((1, 2, tile), lambda p, _: (p, 0, 0)),
        ],
        [((total, count * tile), low), ((count, 2, total), wide), ((count, 2, tile), wide)],
        grid=(count,),
        memory=32,
        estimate=(6e9 * count, (3 << 20) * count),
    )


def backward_kernel(
    length_ref,
    query_ref,
    key_ref,
    value_ref,
    context_ref,
    grad_ref,
    total_ref,
    strip_ref,
    query_grad_ref,
    key_grad_ref,
    value_grad_ref,
    strip_grad_ref,
    key_sum,
    value_sum,
    *,
    step,
):
    length = length_ref[0]
    total = query_ref.shape[0]
    masks = key_masks(total, length)
    ones = jnp.ones((step, tile), low)
    keys = [one_head(key_ref[...], head, masks) for head in (0, 1)]
    plain_keys = [one_head(key_ref[...], head) for head in (0, 1)]
    values = [one_head(value_ref[...], head) for head in (0, 1)]
    key_sum[...] = jnp.zeros_like(key_sum)
    value_sum[...] = jnp.zeros_like(value_sum)
    strip_grad_ref[...] = jnp.zeros_like(strip_grad_ref)

    def body(index, carry):
        first = pl.multiple_of(index * step, step)
        queries = query_ref[pl.ds(first, step), :]
        grads = grad_ref[pl.ds(first, step), :]
        columns = strip_columns(total, first, step)
        inner = grads.astype(wide) * context_ref[pl.ds(first, step), :].astype(wide)
        query_grad = None
        for head in (0, 1):
            head_grads = one_head(grads, head)
            pick = one_head(jnp.ones((8, tile), wide), head)
            row_inner = lax.dot_general(
                pick,
                inner,
                (((1,), (1,)), ((), ())),
                precision=lax.Precision.HIGHEST,
                preferred_element_type=wide,
            )[:1]
            log_total = total_ref[0, head : head + 1, pl.ds(first, step)]
            products = dot(keys[head], one_head(queries, head, ones), 1, 1)
            probs = jnp.exp(add_bias(products, strip_ref, head, columns) - log_total)
            value_sum[...] += dot(probs.astype(low), head_grads, 1, 0)
            score_grad = probs * (dot(values[head], head_grads, 1, 1) - row_inner)
            for block, where in enumerate(columns):
                strip_grad_ref[head, :, where] += score_grad[block * tile : (block + 1) * tile]
            score_low = score_grad.astype(low)
            key_sum[...] += dot(score_low, one_head(queries, head), 1, 0)
            part = dot(score_low, plain_keys[head], 0, 0)
            query_grad = part if query_grad is None else query_grad + part
        query_grad_ref[pl.ds(first, step), :] = query_grad.astype(low)
        return carry

    lax.fori_loop(0, total // step, body, 0)
    key_grad_ref[...] = key_sum[...].astype(low)
    value_grad_ref[...] = value_sum[...].astype(low)


def attention_backward(
    steps, length, qkv, context, context_grad, log_totals, strips, start, held, step=256
):
    total = qkv.shape[0]
    pairs = qkv.shape[1] // (3 * tile)
    strip_width = strips.shape[2]

    def columns(which, first=start):
        return pl.BlockSpec((total, tile), lambda p, _: (0, which * pairs + first + p))

    part = pl.BlockSpec((total, tile), lambda p, _: (0, p))
    return steps.launch(
        "attention_backward",
        functools.partial(backward_kernel, step=step),
        [length, qkv, qkv, qkv, context, context_grad, log_totals, pinned(strips)],
        [
            columns(0),
            columns(1),
            columns(2),
            columns(0, start - held),
            columns(0),
            pl.BlockSpec((1, 2, total), lambda p, _: (start - held + p, 0, 0)),
            pl.BlockSpec((2, tile, strip_width), lambda p, _: (start + p, 0, 0)),
        ],
        [part, part, part, pl.BlockSpec((2, tile, strip_width), lambda p, _: (p, 0, 0))],
        [((total, tile), low)] * 3 + [((2, tile, strip_width), wide)],
        scratch=[pltpu.VMEM((total, tile), wide)] * 2,
        memory=32,
        stored=(3,),
        estimate=(1e10, 6 << 20),
    )


def gelu_and_slope(values):
    distance = jnp.abs(values) * math.sqrt(0.5)
    ratio = 1.0 / (1.0 + 0.3275911 * distance)
    density = jnp.exp(-distance * distance)
    poly = 1.061405429 * ratio - 1.453152027
    poly = poly * ratio + 1.421413741
    poly = poly * ratio - 0.284496736
    poly = poly * ratio + 0.254829592
    tail = (0.5 * ratio) * poly * density
    cumulative = jnp.where(values >= 0, 1.0 - tail, tail)
    slope = cumulative + values * density * (1.0 / math.sqrt(2.0 * math.pi))
    return values * cumulative, slope


def beside(refs):
    return jnp.concatenate([ref[...] for ref in refs], axis=1)


def start_copies(index_ref, pieces, target, semaphores, columns=None):
    copies = []
    for number, piece in enumerate(pieces):
        for side in (0, 1):
            entry = 2 * number + side
            rows = piece.shape[-2]
            where = pl.ds(pl.multiple_of(index_ref[entry] * rows, rows), rows)
            if columns is not None:
                source, place = piece.at[side, :, columns], target.at[where, :]
            else:
                source, place = piece.at[side], target.at[:, where, :]
            copies.append(pltpu.make_async_copy(source, place, semaphores.at[entry]))
    for copy in copies:
        copy.start()
    return copies


def transposed_rows(order_ref, source_ref, target_ref, columns, chips, ordered):
    share = source_ref.shape[1] // chips
    for block in range(chips):
        if ordered:
            first = pl.multiple_of(order_ref[block] * share, share)
            part = source_ref[:, pl.ds(first, share)]
        else:
            part = source_ref[:, block * share : (block + 1) * share]
        target_ref[block * share : (block + 1) * share, columns] = part.T.astype(low)


def send_kernel(odd_ref, block_ref, first_ref, second_ref):
    @pl.when(pl.program_id(0) == 0)
    def _():
        first_ref[...] = block_ref[0]

    @pl.when(pl.program_id(0) == 1)
    def _():
        second_ref[...] = block_ref[0]


def send_blocks(steps, odd, blocks):
    shape = blocks.shape[1:]
    out = pl.BlockSpec(shape, lambda i, _: (0, 0))
    return steps.launch(
        "send_blocks",
        send_kernel,
        [odd, pinned(blocks)],
        [pl.BlockSpec((1,) + shape, lambda i, odd_ref: ((odd_ref[0] + i) % 2, 0, 0))],
        [out, out],
        [(shape, low)] * 2,
        grid=(2,),
        memory=8,
        estimate=(0, 2 << 20),
    )


def scaled(block, gain):
    return (gain * block.astype(wide)).astype(low)


def column_copies(core, weights, targets, semaphores, first=0, parts=1, part=0):
    copies = []
    for number, (weight, target) in enumerate(zip(weights, targets)):
        width = weight.shape[1] // (2 * parts)
        columns = pl.ds(pl.multiple_of((parts * core + part) * width, width), width)
        copies.append(
            pltpu.make_async_copy(weight.at[:, columns], target, semaphores.at[first + number])
        )
    return copies


def run_copies(copies):
    for copy in copies:
        copy.start()
    for copy in copies:
        copy.wait()


def side_kernel(core_ref, *refs):
    attention, feed = refs[:4], refs[4:6]
    gain_ref, out_ref, semaphores = refs[6:]
    core = 1 - core_ref[0]
    inner = attention[0].shape[1] // 2
    hidden = feed[0].shape[1] // 4
    targets = [out_ref.at[:, n * inner : (n + 1) * inner] for n in range(4)]
    copies = column_copies(core, attention, targets, semaphores)
    first = 4 * inner
    for part in (0, 1):
        start = first + 2 * part * hidden
        targets = [out_ref.at[:, start + n * hidden : start + (n + 1) * hidden] for n in (0, 1)]
        copies += column_copies(core, feed, targets, semaphores, 4 + 2 * part, 2, part)
    run_copies(copies)
    out_ref[:, : 3 * inner] = scaled(out_ref[:, : 3 * inner], gain_ref[:, :1])
    for part in (0, 1):
        columns = slice(first + 2 * part * hidden, first + (2 * part + 1) * hidden)
        out_ref[:, columns] = scaled(out_ref[:, columns], gain_ref[:, 1:])


def relay_kernel(source_ref, target_ref):
    target_ref[...] = source_ref[...]


def relay(steps, array):
    block = pl.BlockSpec((1,) + array.shape[1:], lambda i: (i,) + (0,) * (array.ndim - 1))
    return steps.launch(
        "relay",
        relay_kernel,
        [array],
        [block],
        [block],
        [(array.shape, low)],
        grid=(array.shape[0],),
        prefetch=0,
        memory=8,
    )[0]


def pair_kernel(first_ref, second_ref, out_ref):
    out_ref[0] = first_ref[...]
    out_ref[1] = second_ref[...]


def pair(steps, first, second):
    rows, width = first.shape
    step = rows // 2
    block = pl.BlockSpec((step, width), lambda i: (i, 0))
    return steps.launch(
        "pair",
        pair_kernel,
        [first, second],
        [block] * 2,
        [pl.BlockSpec((2, step, width), lambda i: (0, i, 0))],
        [((2, rows, width), low)],
        grid=(2,),
        prefetch=0,
        memory=8,
    )[0]


def other_side(steps, core, attention, feed, gains):
    rows = attention[0].shape[0]
    columns = sum(weight.shape[1] for weight in attention + feed) // 2
    return steps.launch(
        "other_side",
        side_kernel,
        [core, *map(pinned, (*attention, *feed)), gains],
        [in_hbm] * 6 + [in_vmem],
        [in_vmem],
        [((rows, columns), low)],
        scratch=[pltpu.SemaphoreType.DMA((8,))],
        memory=8,
    )[0]


def attention_shard_kernel(core_ref, *refs):
    attention = refs[:4]
    gain_ref, arrived_ref, out_ref, semaphores = refs[4:]
    inner = attention[0].shape[1] // 2
    targets = [out_ref.at[0, :, n * inner : (n + 1) * inner] for n in range(4)]
    copies = column_copies(core_ref[0], attention, targets, semaphores)
    source = arrived_ref.at[:, : 4 * inner]
    copies.append(pltpu.make_async_copy(source, out_ref.at[1], semaphores.at[4]))
    run_copies(copies)
    out_ref[0, :, : 3 * inner] = scaled(out_ref[0, :, : 3 * inner], gain_ref[:, :1])


def attention_shard(steps, core, weights, gains, arrived):
    rows = weights[0].shape[0]
    columns = sum(weight.shape[1] for weight in weights) // 2
    return steps.launch(
        "attention_shard",
        attention_shard_kernel,
        [core, *map(pinned, weights), gains, arrived],
        [in_hbm] * 4 + [in_vmem, anywhere],
        [in_vmem],
        [((2, rows, columns), low)],
        scratch=[pltpu.SemaphoreType.DMA((5,))],
        memory=8,
    )[0]


def hidden_shard_kernel(core_ref, *refs, part):
    feed = refs[:2]
    gain_ref, arrived_ref, out_ref, semaphores = refs[2:]
    hidden = out_ref.shape[3]
    targets = [out_ref.at[0, number] for number in (0, 1)]
    copies = column_copies(core_ref[0], feed, targets, semaphores, 0, 2, part)
    for number in (0, 1):
        start = 2 * hidden * (1 + part) + number * hidden
        source = arrived_ref.at[:, start : start + hidden]
        copies.append(
            pltpu.make_async_copy(source, out_ref.at[1, number], semaphores.at[2 + number])
        )
    run_copies(copies)
    out_ref[0, 0] = scaled(out_ref[0, 0], gain_ref[:, 1:])


def hidden_shard(steps, core, part, weights, gains, arrived):
    rows, columns = weights[0].shape
    return steps.launch(
        "hidden_shard",
        functools.partial(hidden_shard_kernel, part=part),
        [core, *map(pinned, weights), gains, arrived],
        [in_hbm] * 2 + [in_vmem, anywhere],
        [in_vmem],
        [((2, 2, rows, columns // 4), low)],
        scratch=[pltpu.SemaphoreType.DMA((4,))],
        memory=8,
    )[0]


def token_kernel(place_ref, *refs, normed, chips, ordered):
    halves = refs[:2]
    plain_ref, first_ref, first_t_ref, semaphores = refs[-4:]
    total = plain_ref.shape[0]
    step = total // 4
    copies = []
    for number in range(4):
        where = pl.ds(pl.multiple_of(place_ref[number] * step, step), step)
        source = halves[number // 2].at[number % 2]
        copies.append(
            pltpu.make_async_copy(source, plain_ref.at[where, :], semaphores.at[number])
        )
    for copy in copies:
        copy.start()
    for copy in copies:
        copy.wait()
    for block in range(4):
        rows = slice(block * step, (block + 1) * step)
        values = plain_ref[rows, :].astype(wide)
        if normed:
            values = normalize(values)[0]
        else:
            position = block * step + lax.broadcasted_iota(jnp.int32, values.shape, 0)
            values = jnp.where(position < place_ref[4], values, 0.0)
        first_ref[rows, :] = values.astype(low)
        transposed_rows(
            place_ref.at[pl.ds(5, chips)],
            first_ref.at[rows, :],
            first_t_ref,
            rows,
            chips,
            ordered,
        )


def token_rows_of(steps, places, pieces, normed, chips, ordered):
    total, width = 4 * pieces[0].shape[1], pieces[0].shape[2]
    return steps.launch(
        "token_rows" if normed else "cotangent_rows",
        functools.partial(token_kernel, normed=normed, chips=chips, ordered=ordered),
        [places, *pieces],
        [anywhere] * 2,
        [in_vmem] * 3,
        [((total, width), low), ((total, width), low), ((width, total), low)],
        scratch=[pltpu.SemaphoreType.DMA((4,))],
        memory=24,
        stored=() if normed else (1, 2),
        estimate=(0, 10 << 20),
    )


def rows_product_kernel(place_ref, *refs, factors, count, columns, across):
    rows = refs[:factors]
    pieces = refs[factors : factors + count]
    out_ref, weight, semaphores = refs[factors + count :]

    @pl.when(pl.program_id(0) == 0)
    def _():
        for copy in start_copies(place_ref, pieces, weight, semaphores, columns):
            copy.wait()

    operand = beside(rows)
    out_ref[...] = dot(operand, weight[...], 1, 1 if across else 0).astype(low)


def rows_product(steps, places, rows, pieces, first, last, across, name, step=256):
    total, depth = rows[0].shape
    count = len(pieces)
    whole = (2 * count * pieces[0].shape[1], last - first)
    width = whole[0] if across else whole[1]
    return steps.launch(
        name,
        functools.partial(
            rows_product_kernel,
            factors=len(rows),
            count=count,
            columns=pl.ds(first, last - first),
            across=across,
        ),
        [places, *rows, *pieces],
        [pl.BlockSpec((step, depth), lambda i, _: (i, 0))] * len(rows) + [anywhere] * count,
        [pl.BlockSpec((step, width), lambda i, _: (i, 0))],
        [((total, width), low)],
        grid=(total // step,),
        scratch=[pltpu.VMEM(whole, low), pltpu.SemaphoreType.DMA((2 * count,))],
        estimate=(2 * total * whole[0] * whole[1], 8 << 20),
    )[0]


def second_norm_kernel(
    order_ref, token_ref, mine_ref, other_ref, hidden_ref, normed_ref, normed_t_ref, *, chips, ordered
):
    attended = mine_ref[...].astype(wide) + other_ref[...].astype(wide)
    hidden = token_ref[...].astype(wide) + attended
    hidden_ref[...] = hidden
    normed_ref[...] = normalize(hidden)[0].astype(low)
    transposed_rows(order_ref, normed_ref, normed_t_ref, slice(None), chips, ordered)


def second_norm(steps, order, tokens, mine, other, chips, ordered, step=256):
    total, width = tokens.shape
    block = pl.BlockSpec((step, width), lambda i, _: (i, 0))
    return steps.launch(
        "second_norm",
        functools.partial(second_norm_kernel, chips=chips, ordered=ordered),
        [order, tokens, mine, other],
        [block] * 3,
        [block, block, pl.BlockSpec((width, step), lambda i, _: (0, i))],
        [((total, width), wide), ((total, width), low), ((width, total), low)],
        grid=(total // step,),
        stored=(0, 1, 2),
        estimate=(0, 14 << 20),
    )


def feed_forward_kernel(
    place_ref, normed_ref, normed_t_ref, grad_ref, grad_t_ref, *refs, count, first
):
    pieces = refs[:count]
    refs = refs[count:]
    if first:
        mixed_sum, normed_sum, keep_ref, send_ref, weight, semaphores = refs
        before = ()
    else:
        before = refs[:2]
        own_ref, other_ref, normed_grad_ref, keep_ref, send_ref = refs[2:7]
        weight, semaphores, mixed_sum, normed_sum = refs[7:]
    index = pl.program_id(0)
    step = keep_ref.shape[2]
    half = keep_ref.shape[1]
    carried = [
        pltpu.make_async_copy(source, target, semaphores.at[2 * count + number])
        for number, (source, target) in enumerate(zip(before, (mixed_sum, normed_sum)))
    ]

    @pl.when(index == 0)
    def _():
        copies = start_copies(place_ref, pieces, weight, semaphores)
        for copy in carried:
            copy.start()
        for copy in copies:
            copy.wait()

    columns = pl.ds(pl.multiple_of(index * step, step), step)
    expand = weight[0, :, columns]
    contract = weight[1, :, columns]
    pre_act = dot(normed_ref[...], expand, 1, 0)
    act_grad = dot(grad_ref[...], contract, 1, 0).astype(low).astype(wide)
    activated, slope = gelu_and_slope(pre_act)
    activated = activated.astype(low)
    pre_grad = (act_grad * slope).astype(low)
    for part, (rows_ref, values) in enumerate(
        ((normed_t_ref, pre_grad), (grad_t_ref, activated))
    ):
        keep_ref[part] = dot(rows_ref[:half, :], values, 1, 0).astype(low)
        send_ref[part] = dot(rows_ref[half:, :], values, 1, 0).astype(low)
    mixed = dot(activated, contract, 1, 1)
    normed_grad = dot(pre_grad, expand, 1, 1)
    if first:

        @pl.when(index == 0)
        def _():
            mixed_sum[...] = mixed
            normed_sum[...] = normed_grad

        @pl.when(index > 0)
        def _():
            mixed_sum[...] += mixed
            normed_sum[...] += normed_grad

    else:

        @pl.when(index == 0)
        def _():
            for copy in carried:
                copy.wait()

        mixed_sum[...] += mixed
        normed_sum[...] += normed_grad

        @pl.when(index == pl.num_programs(0) - 1)
        def _():
            rows = own_ref.shape[0]
            core = place_ref[2 * count]
            own = pl.multiple_of(core * rows, rows)
            away = pl.multiple_of((1 - core) * rows, rows)
            own_ref[...] = mixed_sum[pl.ds(own, rows), :].astype(low)
            other_ref[...] = mixed_sum[pl.ds(away, rows), :].astype(low)
            normed_grad_ref[...] = normed_sum[...].astype(low)


def feed_forward(steps, places, normed, normed_t, grad, grad_t, pieces, before=None, step=1024):
    rows, width = normed.shape
    count = len(pieces)
    hidden = pieces[0].shape[3]
    first = before is None

    def fixed(shape):
        return pl.BlockSpec(shape, lambda i, _: (0,) * len(shape), pipeline_mode=pl.Buffered(1))

    whole = fixed((rows, width))
    scratch = [
        pltpu.VMEM((2, width, hidden), low),
        pltpu.SemaphoreType.DMA((2 * count + 2,)),
    ]
    if first:
        before = ()
        out_specs = [whole, whole]
        out_shape = [((rows, width), wide)] * 2
    else:
        part = fixed((rows // 2, width))
        out_specs = [part, part, whole]
        out_shape = [((rows // 2, width), low)] * 2 + [((rows, width), low)]
        scratch += [pltpu.VMEM((rows, width), wide)] * 2
    return steps.launch(
        "feed_forward",
        functools.partial(feed_forward_kernel, count=count, first=first),
        [places, *map(pinned, (normed, normed_t, grad, grad_t)), *pieces, *before],
        [whole, fixed((width, rows))] * 2 + [anywhere] * (count + len(before)),
        out_specs + [pl.BlockSpec((2, width // 2, step), lambda i, _: (0, 0, i))] * 2,
        out_shape + [((2, width // 2, hidden), low)] * 2,
        grid=(hidden // step,),
        scratch=scratch,
        memory=58,
        stored=(0, 1) if first else (),
        estimate=(20 * rows * width * hidden, 40 << 20),
    )


def hidden_back_kernel(
    place_ref, mine_ref, other_ref, hidden_ref, grad_ref, *refs, count, columns, chips, ordered
):
    pieces = refs[:count]
    hidden_grad_ref, low_ref, low_t_ref, context_grad_ref, weight, semaphores = refs[count:]

    @pl.when(pl.program_id(0) == 0)
    def _():
        for copy in start_copies(place_ref, pieces, weight, semaphores, columns):
            copy.wait()

    upstream = mine_ref[...].astype(wide) + other_ref[...].astype(wide)
    hidden = hidden_ref[...]
    scale = normalize(hidden)[1]
    hidden_grad = grad_ref[...].astype(wide) + normalize_back(hidden, scale, upstream)
    hidden_grad_ref[...] = hidden_grad
    low_ref[...] = hidden_grad.astype(low)
    context_grad_ref[...] = dot(low_ref[...], weight[...], 1, 0).astype(low)
    order_ref = place_ref.at[pl.ds(2 * count + 1, chips)]
    transposed_rows(order_ref, low_ref, low_t_ref, slice(None), chips, ordered)


def hidden_back(
    steps, places, mine, other, hidden, grad, pieces, first, last, chips, ordered, step=256
):
    total, width = hidden.shape
    count = len(pieces)
    inner = last - first
    block = pl.BlockSpec((step, width), lambda i, _: (i, 0))
    return steps.launch(
        "hidden_back",
        functools.partial(
            hidden_back_kernel,
            count=count,
            columns=pl.ds(first, inner),
            chips=chips,
            ordered=ordered,
        ),
        [places, mine, other, pinned(hidden), pinned(grad), *pieces],
        [block] * 4 + [anywhere] * count,
        [
            block,
            block,
            pl.BlockSpec((width, step), lambda i, _: (0, i)),
            pl.BlockSpec((step, inner), lambda i, _: (i, 0)),
        ],
        [((total, width), wide), ((total, width), low), ((width, total), low), ((total, inner), low)],
        grid=(total // step,),
        scratch=[pltpu.VMEM((width, inner), low), pltpu.SemaphoreType.DMA((2 * count,))],
        estimate=(4 * total * width * inner, 24 << 20),
    )


def terms_kernel(*refs, contexts):
    grad_t_ref, normed_t_ref = refs[:2]
    factors = refs[2:-2]
    for number, target in enumerate(refs[-2:]):

        @pl.when(pl.program_id(0) == number)
        def _():
            first = 0
            if contexts:
                part = dot(grad_t_ref[...], beside(factors[:contexts]), 1, 0)
                first = part.shape[1]
                target[:, :first] = part.astype(low)
            part = dot(normed_t_ref[...], beside(factors[contexts:]), 1, 0)
            target[:, first:] = part.astype(low)


def attention_terms(steps, grad_t, normed_t, contexts, grads):
    width, total = normed_t.shape
    factors = list(contexts) + list(grads)
    columns = sum(factor.shape[1] for factor in factors)
    block = pl.BlockSpec((width // 2, total), lambda i: (i, 0))
    fixed = pl.BlockSpec((width // 2, columns), lambda i: (0, 0))
    return steps.launch(
        "attention_terms",
        functools.partial(terms_kernel, contexts=len(contexts)),
        [grad_t, normed_t, *factors],
        [block, block]
        + [
            pl.BlockSpec(factor.shape, lambda i: (0, 0), pipeline_mode=pl.Buffered(1))
            for factor in factors
        ],
        [fixed, fixed],
        [((width // 2, columns), low)] * 2,
        grid=(2,),
        prefetch=0,
        estimate=(2 * total * width * columns, 10 << 20),
    )


def sum_kernel(*refs):
    total = refs[0][...].astype(wide)
    for ref in refs[1:-1]:
        total += ref[...].astype(wide)
    refs[-1][...] = total.astype(low)


def row_sums(steps, parts):
    first = parts[0]
    rows = first[0].shape[-2] // (1 if first[1] is None else 2)
    shape = first[0].shape[:-2] + (rows, first[0].shape[-1])
    count = 4
    block = shape[:-2] + (rows // count, shape[-1])
    leading = (0,) * (len(shape) - 2)

    def spec(offset):
        return pl.BlockSpec(block, lambda i: leading + (i + offset, 0))

    return steps.launch(
        "row_sums",
        sum_kernel,
        [part for part, _ in parts],
        [spec(count if which else 0) for _, which in parts],
        [spec(0)],
        [(shape, low)],
        grid=(count,),
        prefetch=0,
        memory=12,
        estimate=(0, 4 << 20),
    )[0]


def input_product_kernel(place_ref, *refs, count, factors):
    grads = refs[:factors]
    pieces = refs[factors : factors + count]
    own_ref, other_ref, weight, semaphores = refs[factors + count :]
    index = pl.program_id(0)

    @pl.when(index == 0)
    def _():
        columns = pl.ds(0, weight.shape[1])
        for copy in start_copies(place_ref, pieces, weight, semaphores, columns):
            copy.wait()

    ordered = [ref for block in range(3) for ref in grads[block::3]]
    product = dot(beside(ordered), weight[...], 1, 1)

    @pl.when(index < 2)
    def _():
        other_ref[...] = product.astype(low)

    @pl.when(index >= 2)
    def _():
        own_ref[...] = product


def input_product(steps, places, grads, pieces):
    total = grads[0].shape[0]
    count = len(pieces)
    inner = sum(grad.shape[1] for grad in grads)
    width = 2 * count * pieces[0].shape[1]
    step = total // 4

    def rows(i, place_ref):
        core = place_ref[2 * count]
        return (jnp.where(i < 2, 2 * (1 - core) + i, 2 * core + i - 2), 0)

    return steps.launch(
        "input_product",
        functools.partial(input_product_kernel, count=count, factors=len(grads)),
        [places, *grads, *pieces],
        [pl.BlockSpec((step, grad.shape[1]), rows) for grad in grads] + [anywhere] * count,
        [
            pl.BlockSpec((step, width), lambda i, _: (jnp.maximum(i - 2, 0), 0)),
            pl.BlockSpec((step, width), lambda i, _: (jnp.minimum(i, 1), 0)),
        ],
        [((total // 2, width), wide), ((total // 2, width), low)],
        grid=(4,),
        scratch=[pltpu.VMEM((width, inner), low), pltpu.SemaphoreType.DMA((2 * count,))],
        memory=24,
        estimate=(2 * total * width * inner, 14 << 20),
    )


def finish_kernel(
    place_ref, own_ref, other_ref, base_ref, token_ref, first_ref, second_ref, *, back
):
    index = pl.program_id(0)
    summed = own_ref[...].astype(wide) + other_ref[...].astype(wide)
    if back:
        tokens = token_ref[...].astype(wide)
        values = base_ref[...] + normalize_back(tokens, normalize(tokens)[1], summed)
    else:
        row = (2 * place_ref[0] + index) * summed.shape[0]
        position = row + lax.broadcasted_iota(jnp.int32, summed.shape, 0)
        values = jnp.where(position < place_ref[2], base_ref[...] + summed, 0.0)
    values = values.astype(low)

    @pl.when(index == place_ref[1])
    def _():
        first_ref[...] = values

    @pl.when(index != place_ref[1])
    def _():
        second_ref[...] = values


def finish_half(steps, core, odd, length, own, other, base, tokens, back):
    rows, width = own.shape
    step = rows // 2
    half = pl.BlockSpec((step, width), lambda i, _: (i, 0))
    whole = pl.BlockSpec((step, width), lambda i, place_ref: (2 * place_ref[0] + i, 0))
    quarter = pl.BlockSpec((step, width), lambda i, _: (0, 0))
    return steps.launch(
        "input_gradient_rows" if back else "result_rows",
        functools.partial(finish_kernel, back=back),
        [jnp.stack([core, odd, length]).astype(jnp.int32), own, other, base, tokens],
        [half, half, whole, whole],
        [quarter, quarter],
        [((step, width), low)] * 2,
        grid=(2,),
        memory=12,
        estimate=(0, 6 << 20),
    )


def pick_kernel(slot_ref, *refs, count):
    pieces = refs[:count]
    own_ref, other_ref, semaphores = refs[count:]
    for row in range(4):
        target = (own_ref if row < 2 else other_ref).at[row % 2]
        for number in range(2 * count):

            @pl.when(slot_ref[row] == slot_ref[4 + number])
            def _():
                source = pieces[number // 2].at[number % 2]
                copy = pltpu.make_async_copy(source, target, semaphores.at[row])
                copy.start()
                copy.wait()


def pick_slots(steps, slots, pieces):
    count = len(pieces)
    return steps.launch(
        "pick_slots",
        functools.partial(pick_kernel, count=count),
        [slots, *pieces],
        [anywhere] * count,
        [in_vmem] * 2,
        [(pieces[0].shape, low)] * 2,
        scratch=[pltpu.SemaphoreType.DMA((4,))],
        memory=8,
        estimate=(0, 4 << 20),
    )


def normalize(values):
    scaled = lax.rsqrt(jnp.mean(values * values, axis=-1, keepdims=True) + epsilon)
    return (values * scaled, scaled)


def normalize_back(values, scaled, upstream):
    unit_rows = values * scaled
    return scaled * (upstream - unit_rows * jnp.mean(upstream * unit_rows, axis=-1, keepdims=True))


class Links:
    def __init__(self, buckets):
        self.buckets = buckets
        self.shards = lax.axis_size("fsdp")
        self.depth = lax.axis_size("ctx")
        self.shard = lax.axis_index("fsdp")
        self.level = lax.axis_index("ctx")
        self.chips = self.shards // 2
        self.chip = self.shard // 2
        self.core = self.shard % 2
        self.groups = [list(range(core, self.shards, 2)) for core in (0, 1)]
        self.square = self.chips == 4

    def sibling(self, array):
        return lax.ppermute(array, "fsdp", [(i, i ^ 1) for i in range(self.shards)])

    def across(self, array, bit):
        return lax.ppermute(array, "fsdp", [(i, i ^ (2 * bit)) for i in range(self.shards)])

    def in_order(self, mine, other):
        return jnp.concatenate(
            [jnp.where(self.core == 0, mine, other), jnp.where(self.core == 0, other, mine)], axis=0
        )

    def turn(self, array, second):
        pairs = [(i, i ^ (2 if (i % 2 == 0) != second else 4)) for i in range(self.shards)]
        return lax.ppermute(array, "fsdp", pairs)

    def order(self):
        if not self.square:
            return list(range(self.chips))
        return [self.chip, self.chip ^ (1 + self.core), self.chip ^ (2 - self.core), self.chip ^ 3]

    def gather_first(self, shard):
        if not self.square:
            whole = lax.all_gather(shard, "fsdp", axis=0, axis_index_groups=self.groups)
            return [whole[chip] for chip in range(self.chips)]
        return [shard, self.turn(shard, False), self.turn(shard, True)]

    def gather_last(self, pieces, arrived):
        return [*pieces, self.turn(arrived, True)] if self.square else pieces

    def gather(self, shard):
        pieces = self.gather_first(shard)
        return self.gather_last(pieces, pieces[1])

    def weight_places(self):
        return [2 * chip + side for chip in self.order() for side in (self.core, 1 - self.core)]

    def scatter(self, keep, send):
        dim = keep.ndim - 2
        if not self.square:
            summed = lax.psum_scatter(
                jnp.concatenate([keep, send], axis=dim),
                "fsdp",
                scatter_dimension=dim,
                tiled=True,
                axis_index_groups=self.groups,
            )
            return keep, summed.astype(low)
        return keep, self.turn(send, True)

    def scatter_near(self, steps, terms):
        keep, arrived = terms
        if not self.square:
            return keep, arrived, None
        near = row_sums(steps, [(keep, True), (arrived, True)])
        return keep, arrived, self.turn(near, False)

    def scatter_own(self, steps, terms):
        keep, arrived, last = terms
        total = arrived
        if self.square:
            total = row_sums(steps, [(keep, False), (arrived, False), (last, None)])
        return total, lax.ppermute(total, "ctx", [(0, 1), (3, 2)])

    def small_hops(self, small):
        hops = []
        bit = 1
        while bit < self.chips:
            hops.append(("fsdp", [(i, i ^ (2 * bit)) for i in range(self.shards)]))
            bit *= 2
        bit = 1
        while bit < self.depth:
            hops.append(("ctx", [(i, i ^ bit) for i in range(self.depth)]))
            bit *= 2
        for axis, pairs in hops:
            other = lax.ppermute(small, axis, pairs)
            lane = lax.broadcasted_iota(jnp.int32, small.shape, 1)
            small = jnp.where(lane < self.buckets, small + other, jnp.maximum(small, other))
            yield small

    def level_across(self, steps, terms):
        joined = row_sums(steps, [(part, None) for part in terms])
        return joined, lax.ppermute(joined, "ctx", [(1, 2), (2, 1)])

    def level_out(self, steps, terms):
        total = row_sums(steps, [(part, None) for part in terms])
        return total, lax.ppermute(total, "ctx", [(1, 0), (2, 3)])

    def level_done(self, terms):
        total, outward = terms
        inner = (self.level == 1) | (self.level == 2)
        return self.exchange_rows(jnp.where(inner, total, outward))

    def exchange_rows(self, rows):
        dim = rows.ndim - 2
        half = rows.shape[dim] // 2
        mine = lax.dynamic_slice_in_dim(rows, self.core * half, half, dim)
        other = self.sibling(lax.dynamic_slice_in_dim(rows, (1 - self.core) * half, half, dim))
        return jnp.where(self.core == 0, mine, other), jnp.where(self.core == 0, other, mine)

    def trade(self, array, outward, swapped):
        pairs = []
        for level in range(self.depth):
            for shard in range(self.shards):
                chip, core = divmod(shard, 2)
                side, odd = divmod(level, 2)
                slot = odd if not swapped else 1 - odd
                held = level * self.shards + shard
                worked = (2 * core + slot) * self.shards + 2 * chip + side
                pairs.append((held, worked) if outward else (worked, held))
        return lax.ppermute(array, ("ctx", "fsdp"), pairs)

    def to_slot(self, sends):
        return self.trade(sends[0], True, False), self.trade(sends[1], True, True)

    def both_halves(self, steps, trades):
        half = pair(steps, *trades)
        return half, self.sibling(half)

    def quarter_places(self):
        odd = self.level % 2
        near, far = 2 * self.core, 2 * (1 - self.core)
        return [near + odd, near + 1 - odd, far + odd, far + 1 - odd]

    def from_slot(self, quarters):
        return self.trade(quarters[0], False, False), self.trade(quarters[1], False, True)

    def received(self, trades):
        first, second = trades
        flip = self.level % 2 == 0
        return jnp.stack([jnp.where(flip, first, second), jnp.where(flip, second, first)])


def local(
    tokens,
    cotangent,
    sequence_lengths,
    slot_sequence,
    offset_bucket,
    first_gain,
    second_gain,
    query_weight,
    key_weight,
    value_weight,
    output_weight,
    expand_weight,
    contract_weight,
    bias_table,
    clip_limit,
):
    links = Links(bias_table.shape[0])
    core = links.core
    held_count, local_length, model_width = tokens.shape
    total_length = local_length * links.depth
    bucket_count, head_count = bias_table.shape
    inner_width = query_weight.shape[1]
    head_size = inner_width // head_count
    own_heads = head_count // 2
    own_inner = inner_width // 2
    slot_count = slot_sequence.shape[0]
    assert held_count == 2 and links.depth == 4

    slots = jnp.arange(slot_count)
    slot = links.chip * (2 * held_count) + links.level
    sequence = jnp.sum(jnp.where(slots == slot, slot_sequence, 0))
    length = jnp.sum(jnp.where(slots == sequence, sequence_lengths, 0)).astype(jnp.int32)
    odd = links.level % 2

    def numbers(*values):
        return jnp.stack([jnp.asarray(value, jnp.int32) for value in values])

    core_line = numbers(core)
    first_column = first_gain.astype(wide)[:, None]
    second_column = second_gain.astype(wide)[:, None]
    gains = jnp.concatenate([first_column, second_column], axis=1)
    attention_weights = (query_weight, key_weight, value_weight, output_weight)
    feed_weights = (expand_weight, contract_weight)
    steps = Steps()
    odd_line = odd.reshape(1)
    chips, square = links.chips, links.square
    order = links.order()
    places = numbers(*links.weight_places(), core, *order)
    order_line = numbers(*order)
    slot_places = numbers(*links.quarter_places(), length, *order)
    length_line = length.reshape(1)

    line_width = 2 * total_length
    falling = jnp.concatenate([jnp.flip(offset_bucket), jnp.full((1,), -1, jnp.int32)])
    matching = falling[:, None] == jnp.arange(bucket_count)[None, :]
    own_table = lax.dynamic_slice_in_dim(bias_table, core * own_heads, own_heads, 1)
    lines = dot(own_table, matching.astype(low), 0, 1)

    token_trades = links.to_slot(send_blocks(steps, odd_line, tokens))
    arrived = links.sibling(other_side(steps, core_line, attention_weights, feed_weights, gains))
    attention_pieces = links.gather(
        attention_shard(steps, core_line, attention_weights, gains, arrived)
    )
    strips = bias_strips(steps, lines.reshape(own_heads, 1, line_width))
    cotangent_sends = send_blocks(steps, odd_line, cotangent)
    late_shard = hidden_shard(steps, core_line, 1, feed_weights, gains, arrived)
    token_halves = links.both_halves(steps, token_trades)
    steps.wait(*attention_pieces[1:3])
    early_shard = hidden_shard(steps, core_line, 0, feed_weights, gains, arrived)
    cotangent_trades = links.to_slot(cotangent_sends)
    early_pieces = links.gather(early_shard)
    token_low, normed_one, normed_one_t = token_rows_of(
        steps, slot_places, token_halves, True, chips, square
    )
    qkv_width = 3 * own_inner
    qkv = rows_product(
        steps, places, [normed_one], attention_pieces, 0, qkv_width, False, "qkv_product"
    )
    pairs = own_inner // tile
    half_pairs = pairs // 2
    forward = functools.partial(attention_forward, steps, length_line, qkv, strips)
    first_context, first_totals, first_tops = forward(0, half_pairs)
    cotangent_halves = links.both_halves(steps, cotangent_trades)
    steps.wait(*early_pieces[1:3])
    last_context, last_totals, last_tops = forward(half_pairs, half_pairs)
    contexts = [first_context, last_context]
    output_columns = (qkv_width, qkv_width + own_inner)
    attended = rows_product(
        steps, places, contexts, attention_pieces, *output_columns, True, "attended_product"
    )
    attended_other = links.sibling(attended)
    _, out_low, out_low_t = token_rows_of(
        steps, slot_places, cotangent_halves, False, chips, square
    )
    late_pieces = links.gather_first(late_shard)
    hidden_one, normed_two, normed_two_t = second_norm(
        steps, order_line, token_low, attended, attended_other, chips, square
    )
    operands = (normed_two, normed_two_t, out_low, out_low_t)
    late_pieces = links.gather_last(late_pieces, relay(steps, late_pieces[1]))
    mixed_sum, normed_sum, *early_terms = feed_forward(steps, places, *operands, early_pieces)
    early = links.scatter(*early_terms)
    mixed_own, mixed_away, normed_two_part, *late_terms = feed_forward(
        steps, places, *operands, late_pieces, (mixed_sum, normed_sum)
    )
    normed_two_other = links.sibling(normed_two_part)
    mixed_other = links.sibling(mixed_away)
    late = links.scatter(*late_terms)
    early = links.scatter_near(steps, early)
    hidden_grad, attended_grad, attended_grad_t, context_grad = hidden_back(
        steps,
        places,
        normed_two_part,
        normed_two_other,
        hidden_one,
        out_low,
        attention_pieces,
        *output_columns,
        chips,
        square,
    )
    result_quarters = finish_half(
        steps, core, odd, length, mixed_own, mixed_other, hidden_one, token_low, False
    )
    result_trades = links.from_slot(result_quarters)

    def backward(pair):
        half = pair // half_pairs
        return attention_backward(
            steps,
            length_line,
            qkv,
            contexts[half],
            context_grad,
            (first_totals, last_totals)[half],
            strips,
            pair,
            half * half_pairs,
        )

    *grads_a, strips_a = backward(0)
    *grads_b, strips_b = backward(1)
    steps.wait(*result_trades)
    early = links.scatter_own(steps, early)
    late = links.scatter_near(steps, late)
    first = links.scatter(
        *attention_terms(steps, attended_grad_t, normed_one_t, contexts, grads_a + grads_b)
    )
    *grads_c, strips_c = backward(2)
    late = links.scatter_own(steps, late)
    *grads_d, strips_d = backward(3)
    early = links.level_across(steps, early)
    first = links.scatter_near(steps, first)
    last = links.scatter(
        *attention_terms(steps, attended_grad_t, normed_one_t, (), grads_c + grads_d)
    )
    own_part, away_part = input_product(
        steps, places, grads_a + grads_b + grads_c + grads_d, attention_pieces
    )
    away_other = links.sibling(away_part)
    first = links.scatter_own(steps, first)
    late = links.level_across(steps, late)
    last = links.scatter_near(steps, last)
    early = links.level_out(steps, early)
    last = links.scatter_own(steps, last)
    first = links.level_across(steps, first)
    input_quarters = finish_half(
        steps, core, odd, length, own_part, away_other, hidden_grad, token_low, True
    )
    input_trades = links.from_slot(input_quarters)
    steps.wait(early[1])
    late = links.level_out(steps, late)
    last = links.level_across(steps, last)
    result_pieces = links.gather(links.received(result_trades))
    first = links.level_out(steps, first)
    early_left, early_right = links.level_done(early)
    steps.wait(late[1], *input_trades)
    diagonals = jnp.concatenate(
        [diagonal_sums(steps, part) for part in (strips_a, strips_b, strips_c, strips_d)], axis=0
    ).reshape(own_heads, line_width)
    table_grad = lax.dot_general(
        diagonals,
        matching.astype(wide),
        (((1,), (0,)), ((), ())),
        precision=lax.Precision.HIGHEST,
        preferred_element_type=wide,
    )
    tops = jnp.concatenate([first_tops, last_tops], axis=0).reshape(own_heads, tile)
    small = jnp.concatenate([table_grad, tops[:, : tile - bucket_count]], axis=1)
    for small in links.small_hops(small):
        pass
    last = links.level_out(steps, last)
    late_left, late_right = links.level_done(late)
    first_left, first_right = links.level_done(first)
    last_left, last_right = links.level_done(last)
    input_gradient = links.received(input_trades).astype(wide)

    def slot_of(wanted):
        return jnp.sum(jnp.where(slot_sequence == wanted, slots, 0))

    own_slots = [slot_of(links.shard * held_count + row) for row in range(held_count)]
    other_slots = [slot_of((links.shard ^ 1) * held_count + row) for row in range(held_count)]
    piece_slots = [
        (2 * chip + core) * held_count + row
        for chip in order
        for row in range(held_count)
    ]
    picked, picked_other = pick_slots(
        steps,
        numbers(*own_slots, *other_slots, *piece_slots),
        result_pieces,
    )
    from_other = links.sibling(picked_other)
    output = jnp.stack(
        [
            jnp.where((s // held_count) % 2 == core, picked[row], from_other[row])
            for row, s in enumerate(own_slots)
        ]
    )

    def side_by_side(*parts):
        return jnp.concatenate(parts, axis=1).astype(wide)

    raw_two = side_by_side(early_left[0], late_left[0], early_right[0], late_right[0])
    contract_weight_gradient = side_by_side(
        early_left[1], late_left[1], early_right[1], late_right[1]
    )

    output_weight_gradient = side_by_side(first_left[:, :own_inner], first_right[:, :own_inner])

    def inner_columns(block):
        pieces = []
        for first_side, last_side in ((first_left, last_left), (first_right, last_right)):
            for start, side in ((own_inner, first_side), (0, last_side)):
                for pair in range(half_pairs):
                    first = start + (3 * pair + block) * tile
                    pieces.append(side[:, first : first + tile])
        return side_by_side(*pieces)

    raw_query, raw_key, raw_value = (inner_columns(block) for block in range(3))
    first_gain_gradient = jnp.sum(
        query_weight.astype(wide) * raw_query
        + key_weight.astype(wide) * raw_key
        + value_weight.astype(wide) * raw_value,
        axis=1,
    )
    second_gain_gradient = jnp.sum(expand_weight.astype(wide) * raw_two, axis=1)
    query_weight_gradient = first_column * raw_query
    key_weight_gradient = first_column * raw_key
    value_weight_gradient = first_column * raw_value
    expand_weight_gradient = second_column * raw_two

    small = links.in_order(small, links.sibling(small))
    table_rows = bucket_count // links.shards
    bias_table_gradient = lax.dynamic_slice_in_dim(
        small[:, :bucket_count].T, links.shard * table_rows, table_rows, 0
    )
    largest = small[:, bucket_count]
    shrink = clip_limit / jnp.maximum(clip_limit, largest)
    column_scale = jnp.repeat(jnp.sqrt(shrink), head_size)
    new_query_weight = query_weight.astype(wide) * column_scale[None, :]
    new_key_weight = key_weight.astype(wide) * column_scale[None, :]
    return (
        output,
        input_gradient,
        first_gain_gradient,
        second_gain_gradient,
        query_weight_gradient,
        key_weight_gradient,
        value_weight_gradient,
        output_weight_gradient,
        expand_weight_gradient,
        contract_weight_gradient,
        bias_table_gradient,
        largest,
        new_query_weight,
        new_key_weight,
    )


def solution(mesh):
    return jax.shard_map(
        local,
        mesh=mesh,
        in_specs=(
            P("fsdp", "ctx", None),
            P("fsdp", "ctx", None),
            P(),
            P(),
            P(),
            P("fsdp"),
            P("fsdp"),
            P("fsdp", None),
            P("fsdp", None),
            P("fsdp", None),
            P("fsdp", None),
            P("fsdp", None),
            P("fsdp", None),
            P(),
            P(),
        ),
        out_specs=(
            P("fsdp", "ctx", None),
            P("fsdp", "ctx", None),
            P("fsdp"),
            P("fsdp"),
            P("fsdp", None),
            P("fsdp", None),
            P("fsdp", None),
            P("fsdp", None),
            P("fsdp", None),
            P("fsdp", None),
            P("fsdp", None),
            P(),
            P("fsdp", None),
            P("fsdp", None),
        ),
        check_vma=False,
    )
```

```python
import functools
import math

import jax
import jax.numpy as jnp
from jax import lax
from jax.experimental import pallas as pl
from jax.experimental.pallas import tpu as pltpu
from jax.sharding import PartitionSpec as P

epsilon = 1e-06
masked = -1e30
tile = 128
half_tile = 64
wide = jnp.float32
low = jnp.bfloat16
anywhere = pl.BlockSpec(memory_space=pl.ANY)
in_vmem = pl.BlockSpec(memory_space=pltpu.VMEM)
in_hbm = pl.BlockSpec(memory_space=pltpu.HBM)


def pinned(array):
    return pltpu.with_memory_space_constraint(array, pltpu.HBM)


class Steps:
    def __init__(self):
        self.behind = ()

    def wait(self, *arrays):
        self.behind += arrays

    def launch(
        self,
        name,
        kernel,
        operands,
        in_specs,
        out_specs,
        out_shape,
        grid=(1,),
        prefetch=1,
        scratch=(),
        estimate=(0, 1 << 20),
        memory=24,
        stored=(),
    ):
        inputs, idle = len(operands), self.behind

        def run(*refs):
            refs = list(refs)
            mark_ref = refs.pop(inputs + len(idle) + len(out_specs))
            mark_ref[...] = jnp.zeros_like(mark_ref)
            kernel(*refs[:inputs], *refs[inputs + len(idle) :])

        out_specs, out_shape = list(out_specs), list(out_shape)
        outs = pl.pallas_call(
            run,
            grid_spec=pltpu.PrefetchScalarGridSpec(
                num_scalar_prefetch=prefetch,
                grid=grid,
                in_specs=list(in_specs) + [anywhere] * len(idle),
                out_specs=out_specs + [pl.BlockSpec((8, tile), lambda *_: (0, 0))],
                scratch_shapes=list(scratch),
            ),
            out_shape=[
                pltpu.HBM(shape, kind) if number in stored else jax.ShapeDtypeStruct(shape, kind)
                for number, (shape, kind) in enumerate(out_shape + [((8, tile), wide)])
            ],
            compiler_params=pltpu.CompilerParams(vmem_limit_bytes=memory << 20),
            cost_estimate=pl.CostEstimate(
                flops=int(estimate[0]), bytes_accessed=int(estimate[1]), transcendentals=0
            ),
            name=name,
        )(*operands, *idle)
        self.behind = (outs[-1],)
        return outs[:-1]


def dot(left, right, left_dim, right_dim):
    return lax.dot_general(
        left, right, (((left_dim,), (right_dim,)), ((), ())), preferred_element_type=wide
    )


def strip_kernel(line_ref, strip_ref):
    width = line_ref.shape[-1]
    rows = jnp.broadcast_to(line_ref[0], (tile, width))
    strip_ref[0] = pltpu.roll(rows, width - (tile - 1), 1, stride=1, stride_axis=0)


def bias_strips(steps, lines):
    heads, _, width = lines.shape
    return steps.launch(
        "bias_strips",
        strip_kernel,
        [lines],
        [pl.BlockSpec((1, 1, width), lambda h: (h, 0, 0))],
        [pl.BlockSpec((1, tile, width), lambda h: (h, 0, 0))],
        [((heads, tile, width), wide)],
        grid=(heads,),
        prefetch=0,
        memory=16,
        stored=(0,),
        estimate=(0, 8 << 20),
    )[0]


def diagonal_kernel(strip_ref, line_ref):
    strip = strip_ref[0]
    rows = tile
    while rows > 1:
        rows //= 2
        strip = pltpu.roll(strip[:rows], rows, 1) + strip[rows:]
    line_ref[0] = strip


def diagonal_sums(steps, strips):
    heads, _, width = strips.shape
    return steps.launch(
        "diagonal_sums",
        diagonal_kernel,
        [strips],
        [pl.BlockSpec((1, tile, width), lambda h: (h, 0, 0))],
        [pl.BlockSpec((1, 1, width), lambda h: (h, 0, 0))],
        [((heads, 1, width), wide)],
        grid=(heads,),
        prefetch=0,
        memory=16,
        estimate=(0, 2 << 20),
    )[0]


def one_head(block, head, extra=None):
    lane = lax.broadcasted_iota(jnp.int32, block.shape, 1)
    kept = jnp.where((lane >= half_tile) if head else (lane < half_tile), block, 0)
    if extra is None:
        return kept
    return jnp.where(lane == (0 if head else half_tile), extra, kept)


def key_masks(total, length):
    position = lax.broadcasted_iota(jnp.int32, (total, tile), 0)
    return jnp.where(position < length, 0.0, masked).astype(low)


def strip_columns(total, first, width):
    return [
        pl.ds(pl.multiple_of(total - tile - row + first, tile), width)
        for row in range(0, total, tile)
    ]


def add_bias(products, strip_ref, head, columns):
    return jnp.concatenate(
        [
            products[block * tile : (block + 1) * tile] + strip_ref[head, :, where]
            for block, where in enumerate(columns)
        ],
        axis=0,
    )


def forward_kernel(
    length_ref, query_ref, key_ref, value_ref, strip_ref, context_ref, total_ref, top_ref, *, step
):
    length = length_ref[0]
    total = query_ref.shape[0]
    masks = key_masks(total, length)
    ones = jnp.ones((step, tile), low)
    keys = [one_head(key_ref[...], head, masks) for head in (0, 1)]
    values = [one_head(value_ref[...], head).astype(wide).T.astype(low) for head in (0, 1)]

    def body(index, tops):
        first = pl.multiple_of(index * step, step)
        queries = query_ref[pl.ds(first, step), :]
        columns = strip_columns(total, first, step)
        query_okay = first + lax.broadcasted_iota(jnp.int32, (1, step), 1) < length
        context = None
        peaks = []
        for head in (0, 1):
            products = dot(keys[head], one_head(queries, head, ones), 1, 1)
            scores = add_bias(products, strip_ref, head, columns)
            row_max = jnp.max(scores, axis=0, keepdims=True)
            exponent = jnp.exp(scores - row_max)
            summed = jnp.sum(exponent, axis=0, keepdims=True)
            part = dot(values[head], exponent.astype(low), 1, 0) * (1.0 / summed)
            context = part if context is None else context + part
            total_ref[0, head : head + 1, pl.ds(first, step)] = row_max + jnp.log(summed)
            peaks.append(
                jnp.where(query_okay, jnp.max(products, axis=0, keepdims=True), masked)
            )
        context_ref[pl.ds(first, step), :] = context.T.astype(low)
        return tuple(jnp.maximum(top, peak) for top, peak in zip(tops, peaks))

    tops = lax.fori_loop(
        0, total // step, body, tuple(jnp.full((1, step), masked, wide) for _ in (0, 1))
    )
    for head in (0, 1):
        peak = jnp.max(tops[head], axis=1, keepdims=True)
        top_ref[0, head : head + 1, :] = jnp.broadcast_to(peak, (1, tile))


def attention_forward(steps, length, qkv, strips, start, count, step=512):
    total = qkv.shape[0]
    pairs = qkv.shape[1] // (3 * tile)
    strip_width = strips.shape[2]

    def columns(which):
        return pl.BlockSpec((total, tile), lambda p, _: (0, which * pairs + start + p))

    return steps.launch(
        "attention_forward",
        functools.partial(forward_kernel, step=step),
        [length, qkv, qkv, qkv, strips],
        [columns(which) for which in range(3)]
        + [pl.BlockSpec((2, tile, strip_width), lambda p, _: (start + p, 0, 0))],
        [
            pl.BlockSpec((total, tile), lambda p, _: (0, p)),
            pl.BlockSpec((1, 2, total), lambda p, _: (p, 0, 0)),
            pl.BlockSpec((1, 2, tile), lambda p, _: (p, 0, 0)),
        ],
        [((total, count * tile), low), ((count, 2, total), wide), ((count, 2, tile), wide)],
        grid=(count,),
        memory=32,
        estimate=(6e9 * count, (3 << 20) * count),
    )


def backward_kernel(
    length_ref,
    query_ref,
    key_ref,
    value_ref,
    context_ref,
    grad_ref,
    total_ref,
    strip_ref,
    query_grad_ref,
    key_grad_ref,
    value_grad_ref,
    strip_grad_ref,
    key_sum,
    value_sum,
    *,
    step,
):
    length = length_ref[0]
    total = query_ref.shape[0]
    masks = key_masks(total, length)
    ones = jnp.ones((step, tile), low)
    keys = [one_head(key_ref[...], head, masks) for head in (0, 1)]
    plain_keys = [one_head(key_ref[...], head) for head in (0, 1)]
    values = [one_head(value_ref[...], head) for head in (0, 1)]
    key_sum[...] = jnp.zeros_like(key_sum)
    value_sum[...] = jnp.zeros_like(value_sum)
    strip_grad_ref[...] = jnp.zeros_like(strip_grad_ref)

    def body(index, carry):
        first = pl.multiple_of(index * step, step)
        queries = query_ref[pl.ds(first, step), :]
        grads = grad_ref[pl.ds(first, step), :]
        columns = strip_columns(total, first, step)
        inner = grads.astype(wide) * context_ref[pl.ds(first, step), :].astype(wide)
        query_grad = None
        for head in (0, 1):
            head_grads = one_head(grads, head)
            pick = one_head(jnp.ones((8, tile), wide), head)
            row_inner = lax.dot_general(
                pick,
                inner,
                (((1,), (1,)), ((), ())),
                precision=lax.Precision.HIGHEST,
                preferred_element_type=wide,
            )[:1]
            log_total = total_ref[0, head : head + 1, pl.ds(first, step)]
            products = dot(keys[head], one_head(queries, head, ones), 1, 1)
            probs = jnp.exp(add_bias(products, strip_ref, head, columns) - log_total)
            value_sum[...] += dot(probs.astype(low), head_grads, 1, 0)
            score_grad = probs * (dot(values[head], head_grads, 1, 1) - row_inner)
            for block, where in enumerate(columns):
                strip_grad_ref[head, :, where] += score_grad[block * tile : (block + 1) * tile]
            score_low = score_grad.astype(low)
            key_sum[...] += dot(score_low, one_head(queries, head), 1, 0)
            part = dot(score_low, plain_keys[head], 0, 0)
            query_grad = part if query_grad is None else query_grad + part
        query_grad_ref[pl.ds(first, step), :] = query_grad.astype(low)
        return carry

    lax.fori_loop(0, total // step, body, 0)
    key_grad_ref[...] = key_sum[...].astype(low)
    value_grad_ref[...] = value_sum[...].astype(low)


def attention_backward(
    steps, length, qkv, context, context_grad, log_totals, strips, start, held, step=256
):
    total = qkv.shape[0]
    pairs = qkv.shape[1] // (3 * tile)
    strip_width = strips.shape[2]

    def columns(which, first=start):
        return pl.BlockSpec((total, tile), lambda p, _: (0, which * pairs + first + p))

    part = pl.BlockSpec((total, tile), lambda p, _: (0, p))
    return steps.launch(
        "attention_backward",
        functools.partial(backward_kernel, step=step),
        [length, qkv, qkv, qkv, context, context_grad, log_totals, pinned(strips)],
        [
            columns(0),
            columns(1),
            columns(2),
            columns(0, start - held),
            columns(0),
            pl.BlockSpec((1, 2, total), lambda p, _: (start - held + p, 0, 0)),
            pl.BlockSpec((2, tile, strip_width), lambda p, _: (start + p, 0, 0)),
        ],
        [part, part, part, pl.BlockSpec((2, tile, strip_width), lambda p, _: (p, 0, 0))],
        [((total, tile), low)] * 3 + [((2, tile, strip_width), wide)],
        scratch=[pltpu.VMEM((total, tile), wide)] * 2,
        memory=32,
        stored=(3,),
        estimate=(1e10, 6 << 20),
    )


def gelu_and_slope(values):
    distance = jnp.abs(values) * math.sqrt(0.5)
    ratio = 1.0 / (1.0 + 0.3275911 * distance)
    density = jnp.exp(-distance * distance)
    poly = 1.061405429 * ratio - 1.453152027
    poly = poly * ratio + 1.421413741
    poly = poly * ratio - 0.284496736
    poly = poly * ratio + 0.254829592
    tail = (0.5 * ratio) * poly * density
    cumulative = jnp.where(values >= 0, 1.0 - tail, tail)
    slope = cumulative + values * density * (1.0 / math.sqrt(2.0 * math.pi))
    return values * cumulative, slope


def beside(refs):
    return jnp.concatenate([ref[...] for ref in refs], axis=1)


def start_copies(index_ref, pieces, target, semaphores, columns=None):
    copies = []
    for number, piece in enumerate(pieces):
        for side in (0, 1):
            entry = 2 * number + side
            rows = piece.shape[-2]
            where = pl.ds(pl.multiple_of(index_ref[entry] * rows, rows), rows)
            if columns is not None:
                source, place = piece.at[side, :, columns], target.at[where, :]
            else:
                source, place = piece.at[side], target.at[:, where, :]
            copies.append(pltpu.make_async_copy(source, place, semaphores.at[entry]))
    for copy in copies:
        copy.start()
    return copies


def transposed_rows(order_ref, source_ref, target_ref, columns, chips, ordered):
    share = source_ref.shape[1] // chips
    for block in range(chips):
        if ordered:
            first = pl.multiple_of(order_ref[block] * share, share)
            part = source_ref[:, pl.ds(first, share)]
        else:
            part = source_ref[:, block * share : (block + 1) * share]
        target_ref[block * share : (block + 1) * share, columns] = part.T.astype(low)


def send_kernel(odd_ref, block_ref, first_ref, second_ref):
    @pl.when(pl.program_id(0) == 0)
    def _():
        first_ref[...] = block_ref[0]

    @pl.when(pl.program_id(0) == 1)
    def _():
        second_ref[...] = block_ref[0]


def send_blocks(steps, odd, blocks):
    shape = blocks.shape[1:]
    out = pl.BlockSpec(shape, lambda i, _: (0, 0))
    return steps.launch(
        "send_blocks",
        send_kernel,
        [odd, pinned(blocks)],
        [pl.BlockSpec((1,) + shape, lambda i, odd_ref: ((odd_ref[0] + i) % 2, 0, 0))],
        [out, out],
        [(shape, low)] * 2,
        grid=(2,),
        memory=8,
        estimate=(0, 2 << 20),
    )


def scaled(block, gain):
    return (gain * block.astype(wide)).astype(low)


def column_copies(core, weights, targets, semaphores, first=0, parts=1, part=0):
    copies = []
    for number, (weight, target) in enumerate(zip(weights, targets)):
        width = weight.shape[1] // (2 * parts)
        columns = pl.ds(pl.multiple_of((parts * core + part) * width, width), width)
        copies.append(
            pltpu.make_async_copy(weight.at[:, columns], target, semaphores.at[first + number])
        )
    return copies


def run_copies(copies):
    for copy in copies:
        copy.start()
    for copy in copies:
        copy.wait()


def side_kernel(core_ref, *refs):
    attention, feed = refs[:4], refs[4:6]
    gain_ref, out_ref, semaphores = refs[6:]
    core = 1 - core_ref[0]
    inner = attention[0].shape[1] // 2
    hidden = feed[0].shape[1] // 4
    targets = [out_ref.at[:, n * inner : (n + 1) * inner] for n in range(4)]
    copies = column_copies(core, attention, targets, semaphores)
    first = 4 * inner
    for part in (0, 1):
        start = first + 2 * part * hidden
        targets = [out_ref.at[:, start + n * hidden : start + (n + 1) * hidden] for n in (0, 1)]
        copies += column_copies(core, feed, targets, semaphores, 4 + 2 * part, 2, part)
    run_copies(copies)
    out_ref[:, : 3 * inner] = scaled(out_ref[:, : 3 * inner], gain_ref[:, :1])
    for part in (0, 1):
        columns = slice(first + 2 * part * hidden, first + (2 * part + 1) * hidden)
        out_ref[:, columns] = scaled(out_ref[:, columns], gain_ref[:, 1:])


def relay_kernel(first_ref, second_ref, first_out_ref, second_out_ref):
    first_out_ref[...] = first_ref[...]
    second_out_ref[...] = second_ref[...]


def relay(steps, first, second):
    block = pl.BlockSpec((1,) + first.shape[1:], lambda i: (i,) + (0,) * (first.ndim - 1))
    return steps.launch(
        "relay",
        relay_kernel,
        [first, second],
        [block, block],
        [block, block],
        [(first.shape, low)] * 2,
        grid=(first.shape[0],),
        prefetch=0,
        memory=8,
    )


def pair_kernel(first_ref, second_ref, out_ref):
    out_ref[0] = first_ref[...]
    out_ref[1] = second_ref[...]


def pair(steps, first, second):
    rows, width = first.shape
    step = rows // 2
    block = pl.BlockSpec((step, width), lambda i: (i, 0))
    return steps.launch(
        "pair",
        pair_kernel,
        [first, second],
        [block] * 2,
        [pl.BlockSpec((2, step, width), lambda i: (0, i, 0))],
        [((2, rows, width), low)],
        grid=(2,),
        prefetch=0,
        memory=8,
    )[0]


def other_side(steps, core, attention, feed, gains):
    rows = attention[0].shape[0]
    columns = sum(weight.shape[1] for weight in attention + feed) // 2
    return steps.launch(
        "other_side",
        side_kernel,
        [core, *map(pinned, (*attention, *feed)), gains],
        [in_hbm] * 6 + [in_vmem],
        [in_vmem],
        [((rows, columns), low)],
        scratch=[pltpu.SemaphoreType.DMA((8,))],
        memory=8,
    )[0]


def attention_shard_kernel(core_ref, *refs):
    attention = refs[:4]
    gain_ref, arrived_ref, out_ref, semaphores = refs[4:]
    inner = attention[0].shape[1] // 2
    targets = [out_ref.at[0, :, n * inner : (n + 1) * inner] for n in range(4)]
    copies = column_copies(core_ref[0], attention, targets, semaphores)
    source = arrived_ref.at[:, : 4 * inner]
    copies.append(pltpu.make_async_copy(source, out_ref.at[1], semaphores.at[4]))
    run_copies(copies)
    out_ref[0, :, : 3 * inner] = scaled(out_ref[0, :, : 3 * inner], gain_ref[:, :1])


def attention_shard(steps, core, weights, gains, arrived):
    rows = weights[0].shape[0]
    columns = sum(weight.shape[1] for weight in weights) // 2
    return steps.launch(
        "attention_shard",
        attention_shard_kernel,
        [core, *map(pinned, weights), gains, pinned(arrived)],
        [in_hbm] * 4 + [in_vmem, anywhere],
        [in_vmem],
        [((2, rows, columns), low)],
        scratch=[pltpu.SemaphoreType.DMA((5,))],
        memory=8,
    )[0]


def hidden_shard_kernel(core_ref, *refs, part):
    feed = refs[:2]
    gain_ref, arrived_ref, out_ref, semaphores = refs[2:]
    hidden = out_ref.shape[3]
    targets = [out_ref.at[0, number] for number in (0, 1)]
    copies = column_copies(core_ref[0], feed, targets, semaphores, 0, 2, part)
    for number in (0, 1):
        start = 2 * hidden * (1 + part) + number * hidden
        source = arrived_ref.at[:, start : start + hidden]
        copies.append(
            pltpu.make_async_copy(source, out_ref.at[1, number], semaphores.at[2 + number])
        )
    run_copies(copies)
    out_ref[0, 0] = scaled(out_ref[0, 0], gain_ref[:, 1:])


def hidden_shard(steps, core, part, weights, gains, arrived):
    rows, columns = weights[0].shape
    return steps.launch(
        "hidden_shard",
        functools.partial(hidden_shard_kernel, part=part),
        [core, *map(pinned, weights), gains, pinned(arrived)],
        [in_hbm] * 2 + [in_vmem, anywhere],
        [in_vmem],
        [((2, 2, rows, columns // 4), low)],
        scratch=[pltpu.SemaphoreType.DMA((4,))],
        memory=8,
    )[0]


def token_kernel(place_ref, *refs, normed, chips, ordered):
    halves = refs[:2]
    plain_ref, first_ref, first_t_ref, semaphores = refs[-4:]
    total = plain_ref.shape[0]
    step = total // 4
    copies = []
    for number in range(4):
        where = pl.ds(pl.multiple_of(place_ref[number] * step, step), step)
        source = halves[number // 2].at[number % 2]
        copies.append(
            pltpu.make_async_copy(source, plain_ref.at[where, :], semaphores.at[number])
        )
    for copy in copies:
        copy.start()
    for copy in copies:
        copy.wait()
    for block in range(4):
        rows = slice(block * step, (block + 1) * step)
        values = plain_ref[rows, :].astype(wide)
        if normed:
            values = normalize(values)[0]
        else:
            position = block * step + lax.broadcasted_iota(jnp.int32, values.shape, 0)
            values = jnp.where(position < place_ref[4], values, 0.0)
        first_ref[rows, :] = values.astype(low)
        transposed_rows(
            place_ref.at[pl.ds(5, chips)],
            first_ref.at[rows, :],
            first_t_ref,
            rows,
            chips,
            ordered,
        )


def token_rows_of(steps, places, pieces, normed, chips, ordered):
    total, width = 4 * pieces[0].shape[1], pieces[0].shape[2]
    return steps.launch(
        "token_rows" if normed else "cotangent_rows",
        functools.partial(token_kernel, normed=normed, chips=chips, ordered=ordered),
        [places, *map(pinned, pieces)],
        [anywhere] * 2,
        [in_vmem] * 3,
        [((total, width), low), ((total, width), low), ((width, total), low)],
        scratch=[pltpu.SemaphoreType.DMA((4,))],
        memory=24,
        stored=() if normed else (1, 2),
        estimate=(0, 10 << 20),
    )


def rows_product_kernel(place_ref, *refs, factors, count, columns, across):
    rows = refs[:factors]
    pieces = refs[factors : factors + count]
    out_ref, weight, semaphores = refs[factors + count :]

    @pl.when(pl.program_id(0) == 0)
    def _():
        for copy in start_copies(place_ref, pieces, weight, semaphores, columns):
            copy.wait()

    operand = beside(rows)
    out_ref[...] = dot(operand, weight[...], 1, 1 if across else 0).astype(low)


def rows_product(steps, places, rows, pieces, first, last, across, name, step=256):
    total, depth = rows[0].shape
    count = len(pieces)
    whole = (2 * count * pieces[0].shape[1], last - first)
    width = whole[0] if across else whole[1]
    return steps.launch(
        name,
        functools.partial(
            rows_product_kernel,
            factors=len(rows),
            count=count,
            columns=pl.ds(first, last - first),
            across=across,
        ),
        [places, *rows, *pieces],
        [pl.BlockSpec((step, depth), lambda i, _: (i, 0))] * len(rows) + [anywhere] * count,
        [pl.BlockSpec((step, width), lambda i, _: (i, 0))],
        [((total, width), low)],
        grid=(total // step,),
        scratch=[pltpu.VMEM(whole, low), pltpu.SemaphoreType.DMA((2 * count,))],
        estimate=(2 * total * whole[0] * whole[1], 8 << 20),
    )[0]


def second_norm_kernel(
    order_ref, token_ref, mine_ref, other_ref, hidden_ref, normed_ref, normed_t_ref, *, chips, ordered
):
    attended = mine_ref[...].astype(wide) + other_ref[...].astype(wide)
    hidden = token_ref[...].astype(wide) + attended
    hidden_ref[...] = hidden
    normed_ref[...] = normalize(hidden)[0].astype(low)
    transposed_rows(order_ref, normed_ref, normed_t_ref, slice(None), chips, ordered)


def second_norm(steps, order, tokens, mine, other, chips, ordered, step=256):
    total, width = tokens.shape
    block = pl.BlockSpec((step, width), lambda i, _: (i, 0))
    return steps.launch(
        "second_norm",
        functools.partial(second_norm_kernel, chips=chips, ordered=ordered),
        [order, tokens, mine, other],
        [block] * 3,
        [block, block, pl.BlockSpec((width, step), lambda i, _: (0, i))],
        [((total, width), wide), ((total, width), low), ((width, total), low)],
        grid=(total // step,),
        stored=(0, 1, 2),
        estimate=(0, 14 << 20),
    )


def feed_forward_kernel(
    place_ref, normed_ref, normed_t_ref, grad_ref, grad_t_ref, *refs, count, first
):
    pieces = refs[:count]
    refs = refs[count:]
    if first:
        mixed_sum, normed_sum, keep_ref, send_ref, weight, semaphores = refs
        before = ()
    else:
        before = refs[:2]
        own_ref, other_ref, normed_grad_ref, keep_ref, send_ref = refs[2:7]
        weight, semaphores, mixed_sum, normed_sum = refs[7:]
    index = pl.program_id(0)
    step = keep_ref.shape[2]
    half = keep_ref.shape[1]
    carried = [
        pltpu.make_async_copy(source, target, semaphores.at[2 * count + number])
        for number, (source, target) in enumerate(zip(before, (mixed_sum, normed_sum)))
    ]

    @pl.when(index == 0)
    def _():
        copies = start_copies(place_ref, pieces, weight, semaphores)
        for copy in carried:
            copy.start()
        for copy in copies:
            copy.wait()

    columns = pl.ds(pl.multiple_of(index * step, step), step)
    expand = weight[0, :, columns]
    contract = weight[1, :, columns]
    pre_act = dot(normed_ref[...], expand, 1, 0)
    act_grad = dot(grad_ref[...], contract, 1, 0).astype(low).astype(wide)
    activated, slope = gelu_and_slope(pre_act)
    activated = activated.astype(low)
    pre_grad = (act_grad * slope).astype(low)
    for part, (rows_ref, values) in enumerate(
        ((normed_t_ref, pre_grad), (grad_t_ref, activated))
    ):
        keep_ref[part] = dot(rows_ref[:half, :], values, 1, 0).astype(low)
        send_ref[part] = dot(rows_ref[half:, :], values, 1, 0).astype(low)
    mixed = dot(activated, contract, 1, 1)
    normed_grad = dot(pre_grad, expand, 1, 1)
    if first:

        @pl.when(index == 0)
        def _():
            mixed_sum[...] = mixed
            normed_sum[...] = normed_grad

        @pl.when(index > 0)
        def _():
            mixed_sum[...] += mixed
            normed_sum[...] += normed_grad

    else:

        @pl.when(index == 0)
        def _():
            for copy in carried:
                copy.wait()

        mixed_sum[...] += mixed
        normed_sum[...] += normed_grad

        @pl.when(index == pl.num_programs(0) - 1)
        def _():
            rows = own_ref.shape[0]
            core = place_ref[2 * count]
            own = pl.multiple_of(core * rows, rows)
            away = pl.multiple_of((1 - core) * rows, rows)
            own_ref[...] = mixed_sum[pl.ds(own, rows), :].astype(low)
            other_ref[...] = mixed_sum[pl.ds(away, rows), :].astype(low)
            normed_grad_ref[...] = normed_sum[...].astype(low)


def feed_forward(steps, places, normed, normed_t, grad, grad_t, pieces, before=None, step=1024):
    rows, width = normed.shape
    count = len(pieces)
    hidden = pieces[0].shape[3]
    first = before is None

    def fixed(shape):
        return pl.BlockSpec(shape, lambda i, _: (0,) * len(shape), pipeline_mode=pl.Buffered(1))

    whole = fixed((rows, width))
    scratch = [
        pltpu.VMEM((2, width, hidden), low),
        pltpu.SemaphoreType.DMA((2 * count + 2,)),
    ]
    if first:
        before = ()
        out_specs = [whole, whole]
        out_shape = [((rows, width), wide)] * 2
    else:
        part = fixed((rows // 2, width))
        out_specs = [part, part, whole]
        out_shape = [((rows // 2, width), low)] * 2 + [((rows, width), low)]
        scratch += [pltpu.VMEM((rows, width), wide)] * 2
    return steps.launch(
        "feed_forward",
        functools.partial(feed_forward_kernel, count=count, first=first),
        [places, *map(pinned, (normed, normed_t, grad, grad_t)), *pieces, *before],
        [whole, fixed((width, rows))] * 2 + [anywhere] * (count + len(before)),
        out_specs + [pl.BlockSpec((2, width // 2, step), lambda i, _: (0, 0, i))] * 2,
        out_shape + [((2, width // 2, hidden), low)] * 2,
        grid=(hidden // step,),
        scratch=scratch,
        memory=58,
        stored=(0, 1) if first else (),
        estimate=(20 * rows * width * hidden, 40 << 20),
    )


def hidden_back_kernel(
    place_ref, mine_ref, other_ref, hidden_ref, grad_ref, *refs, count, columns, chips, ordered
):
    pieces = refs[:count]
    hidden_grad_ref, low_ref, low_t_ref, context_grad_ref, weight, semaphores = refs[count:]

    @pl.when(pl.program_id(0) == 0)
    def _():
        for copy in start_copies(place_ref, pieces, weight, semaphores, columns):
            copy.wait()

    upstream = mine_ref[...].astype(wide) + other_ref[...].astype(wide)
    hidden = hidden_ref[...]
    scale = normalize(hidden)[1]
    hidden_grad = grad_ref[...].astype(wide) + normalize_back(hidden, scale, upstream)
    hidden_grad_ref[...] = hidden_grad
    low_ref[...] = hidden_grad.astype(low)
    context_grad_ref[...] = dot(low_ref[...], weight[...], 1, 0).astype(low)
    order_ref = place_ref.at[pl.ds(2 * count + 1, chips)]
    transposed_rows(order_ref, low_ref, low_t_ref, slice(None), chips, ordered)


def hidden_back(
    steps, places, mine, other, hidden, grad, pieces, first, last, chips, ordered, step=256
):
    total, width = hidden.shape
    count = len(pieces)
    inner = last - first
    block = pl.BlockSpec((step, width), lambda i, _: (i, 0))
    return steps.launch(
        "hidden_back",
        functools.partial(
            hidden_back_kernel,
            count=count,
            columns=pl.ds(first, inner),
            chips=chips,
            ordered=ordered,
        ),
        [places, mine, other, pinned(hidden), pinned(grad), *pieces],
        [block] * 4 + [anywhere] * count,
        [
            block,
            block,
            pl.BlockSpec((width, step), lambda i, _: (0, i)),
            pl.BlockSpec((step, inner), lambda i, _: (i, 0)),
        ],
        [((total, width), wide), ((total, width), low), ((width, total), low), ((total, inner), low)],
        grid=(total // step,),
        scratch=[pltpu.VMEM((width, inner), low), pltpu.SemaphoreType.DMA((2 * count,))],
        estimate=(4 * total * width * inner, 24 << 20),
    )


def terms_kernel(*refs, contexts):
    grad_t_ref, normed_t_ref = refs[:2]
    factors = refs[2:-2]
    for number, target in enumerate(refs[-2:]):

        @pl.when(pl.program_id(0) == number)
        def _():
            first = 0
            if contexts:
                part = dot(grad_t_ref[...], beside(factors[:contexts]), 1, 0)
                first = part.shape[1]
                target[:, :first] = part.astype(low)
            part = dot(normed_t_ref[...], beside(factors[contexts:]), 1, 0)
            target[:, first:] = part.astype(low)


def attention_terms(steps, grad_t, normed_t, contexts, grads):
    width, total = normed_t.shape
    factors = list(contexts) + list(grads)
    columns = sum(factor.shape[1] for factor in factors)
    block = pl.BlockSpec((width // 2, total), lambda i: (i, 0))
    fixed = pl.BlockSpec((width // 2, columns), lambda i: (0, 0))
    return steps.launch(
        "attention_terms",
        functools.partial(terms_kernel, contexts=len(contexts)),
        [grad_t, normed_t, *factors],
        [block, block]
        + [
            pl.BlockSpec(factor.shape, lambda i: (0, 0), pipeline_mode=pl.Buffered(1))
            for factor in factors
        ],
        [fixed, fixed],
        [((width // 2, columns), low)] * 2,
        grid=(2,),
        prefetch=0,
        estimate=(2 * total * width * columns, 10 << 20),
    )


def sum_kernel(*refs):
    total = refs[0][...].astype(wide)
    for ref in refs[1:-1]:
        total += ref[...].astype(wide)
    refs[-1][...] = total.astype(low)


def row_sums(steps, parts):
    first = parts[0]
    rows = first[0].shape[-2] // (1 if first[1] is None else 2)
    shape = first[0].shape[:-2] + (rows, first[0].shape[-1])
    count = 4
    block = shape[:-2] + (rows // count, shape[-1])
    leading = (0,) * (len(shape) - 2)

    def spec(offset):
        return pl.BlockSpec(block, lambda i: leading + (i + offset, 0))

    return steps.launch(
        "row_sums",
        sum_kernel,
        [part for part, _ in parts],
        [spec(count if which else 0) for _, which in parts],
        [spec(0)],
        [(shape, low)],
        grid=(count,),
        prefetch=0,
        memory=12,
        estimate=(0, 4 << 20),
    )[0]


def input_product_kernel(place_ref, *refs, count, factors):
    grads = refs[:factors]
    pieces = refs[factors : factors + count]
    own_ref, other_ref, weight, semaphores = refs[factors + count :]
    index = pl.program_id(0)

    @pl.when(index == 0)
    def _():
        columns = pl.ds(0, weight.shape[1])
        for copy in start_copies(place_ref, pieces, weight, semaphores, columns):
            copy.wait()

    ordered = [ref for block in range(3) for ref in grads[block::3]]
    product = dot(beside(ordered), weight[...], 1, 1)

    @pl.when(index < 2)
    def _():
        other_ref[...] = product.astype(low)

    @pl.when(index >= 2)
    def _():
        own_ref[...] = product


def input_product(steps, places, grads, pieces):
    total = grads[0].shape[0]
    count = len(pieces)
    inner = sum(grad.shape[1] for grad in grads)
    width = 2 * count * pieces[0].shape[1]
    step = total // 4

    def rows(i, place_ref):
        core = place_ref[2 * count]
        return (jnp.where(i < 2, 2 * (1 - core) + i, 2 * core + i - 2), 0)

    return steps.launch(
        "input_product",
        functools.partial(input_product_kernel, count=count, factors=len(grads)),
        [places, *grads, *pieces],
        [pl.BlockSpec((step, grad.shape[1]), rows) for grad in grads] + [anywhere] * count,
        [
            pl.BlockSpec((step, width), lambda i, _: (jnp.maximum(i - 2, 0), 0)),
            pl.BlockSpec((step, width), lambda i, _: (jnp.minimum(i, 1), 0)),
        ],
        [((total // 2, width), wide), ((total // 2, width), low)],
        grid=(4,),
        scratch=[pltpu.VMEM((width, inner), low), pltpu.SemaphoreType.DMA((2 * count,))],
        memory=24,
        estimate=(2 * total * width * inner, 14 << 20),
    )


def finish_kernel(
    place_ref, own_ref, other_ref, base_ref, token_ref, first_ref, second_ref, *, back
):
    index = pl.program_id(0)
    summed = own_ref[...].astype(wide) + other_ref[...].astype(wide)
    if back:
        tokens = token_ref[...].astype(wide)
        values = base_ref[...] + normalize_back(tokens, normalize(tokens)[1], summed)
    else:
        row = (2 * place_ref[0] + index) * summed.shape[0]
        position = row + lax.broadcasted_iota(jnp.int32, summed.shape, 0)
        values = jnp.where(position < place_ref[2], base_ref[...] + summed, 0.0)
    values = values.astype(low)

    @pl.when(index == place_ref[1])
    def _():
        first_ref[...] = values

    @pl.when(index != place_ref[1])
    def _():
        second_ref[...] = values


def finish_half(steps, core, odd, length, own, other, base, tokens, back):
    rows, width = own.shape
    step = rows // 2
    half = pl.BlockSpec((step, width), lambda i, _: (i, 0))
    whole = pl.BlockSpec((step, width), lambda i, place_ref: (2 * place_ref[0] + i, 0))
    quarter = pl.BlockSpec((step, width), lambda i, _: (0, 0))
    return steps.launch(
        "input_gradient_rows" if back else "result_rows",
        functools.partial(finish_kernel, back=back),
        [jnp.stack([core, odd, length]).astype(jnp.int32), pinned(own), other, base, tokens],
        [half, half, whole, whole],
        [quarter, quarter],
        [((step, width), low)] * 2,
        grid=(2,),
        memory=12,
        estimate=(0, 6 << 20),
    )


def pick_kernel(slot_ref, *refs, count):
    pieces = refs[:count]
    own_ref, other_ref, semaphores = refs[count:]
    for row in range(4):
        target = (own_ref if row < 2 else other_ref).at[row % 2]
        for number in range(2 * count):

            @pl.when(slot_ref[row] == slot_ref[4 + number])
            def _():
                source = pieces[number // 2].at[number % 2]
                copy = pltpu.make_async_copy(source, target, semaphores.at[row])
                copy.start()
                copy.wait()


def pick_slots(steps, slots, pieces):
    count = len(pieces)
    return steps.launch(
        "pick_slots",
        functools.partial(pick_kernel, count=count),
        [slots, *pieces],
        [anywhere] * count,
        [in_vmem] * 2,
        [(pieces[0].shape, low)] * 2,
        scratch=[pltpu.SemaphoreType.DMA((4,))],
        memory=8,
        estimate=(0, 4 << 20),
    )


def normalize(values):
    scaled = lax.rsqrt(jnp.mean(values * values, axis=-1, keepdims=True) + epsilon)
    return (values * scaled, scaled)


def normalize_back(values, scaled, upstream):
    unit_rows = values * scaled
    return scaled * (upstream - unit_rows * jnp.mean(upstream * unit_rows, axis=-1, keepdims=True))


class Links:
    def __init__(self, buckets):
        self.buckets = buckets
        self.shards = lax.axis_size("fsdp")
        self.depth = lax.axis_size("ctx")
        self.shard = lax.axis_index("fsdp")
        self.level = lax.axis_index("ctx")
        self.chips = self.shards // 2
        self.chip = self.shard // 2
        self.core = self.shard % 2
        self.groups = [list(range(core, self.shards, 2)) for core in (0, 1)]
        self.square = self.chips == 4

    def sibling(self, array):
        return lax.ppermute(array, "fsdp", [(i, i ^ 1) for i in range(self.shards)])

    def across(self, array, bit):
        return lax.ppermute(array, "fsdp", [(i, i ^ (2 * bit)) for i in range(self.shards)])

    def in_order(self, mine, other):
        return jnp.concatenate(
            [jnp.where(self.core == 0, mine, other), jnp.where(self.core == 0, other, mine)], axis=0
        )

    def turn(self, array, second):
        pairs = [(i, i ^ (2 if (i % 2 == 0) != second else 4)) for i in range(self.shards)]
        return lax.ppermute(array, "fsdp", pairs)

    def order(self):
        if not self.square:
            return list(range(self.chips))
        return [self.chip, self.chip ^ (1 + self.core), self.chip ^ (2 - self.core), self.chip ^ 3]

    def gather_whole(self, shard):
        whole = lax.all_gather(shard, "fsdp", axis=0, axis_index_groups=self.groups)
        return [whole[chip] for chip in range(self.chips)]

    def gather(self, shard):
        if not self.square:
            return self.gather_whole(shard)
        first = self.turn(shard, False)
        return [shard, first, self.turn(shard, True), self.turn(first, True)]

    def gather_slowly(self, steps, shard, first):
        if not self.square:
            return self.gather_whole(shard)
        arrived, own = relay(steps, first, shard)
        return [shard, first, self.turn(own, True), self.turn(arrived, True)]

    def weight_places(self):
        return [2 * chip + side for chip in self.order() for side in (self.core, 1 - self.core)]

    def scatter(self, keep, send):
        dim = keep.ndim - 2
        if not self.square:
            summed = lax.psum_scatter(
                jnp.concatenate([keep, send], axis=dim),
                "fsdp",
                scatter_dimension=dim,
                tiled=True,
                axis_index_groups=self.groups,
            )
            return keep, summed.astype(low)
        return keep, self.turn(send, True)

    def scatter_near(self, steps, terms):
        keep, arrived = terms
        if not self.square:
            return keep, arrived, None
        near = row_sums(steps, [(keep, True), (arrived, True)])
        return keep, arrived, self.turn(near, False)

    def scatter_own(self, steps, terms):
        keep, arrived, last = terms
        total = arrived
        if self.square:
            total = row_sums(steps, [(keep, False), (arrived, False), (last, None)])
        return total, lax.ppermute(total, "ctx", [(0, 1), (3, 2)])

    def small_hops(self, small):
        hops = []
        bit = 1
        while bit < self.chips:
            hops.append(("fsdp", [(i, i ^ (2 * bit)) for i in range(self.shards)]))
            bit *= 2
        bit = 1
        while bit < self.depth:
            hops.append(("ctx", [(i, i ^ bit) for i in range(self.depth)]))
            bit *= 2
        for axis, pairs in hops:
            other = lax.ppermute(small, axis, pairs)
            lane = lax.broadcasted_iota(jnp.int32, small.shape, 1)
            small = jnp.where(lane < self.buckets, small + other, jnp.maximum(small, other))
            yield small

    def level_across(self, steps, terms):
        joined = row_sums(steps, [(part, None) for part in terms])
        return joined, lax.ppermute(joined, "ctx", [(1, 2), (2, 1)])

    def level_out(self, steps, terms):
        total = row_sums(steps, [(part, None) for part in terms])
        return total, lax.ppermute(total, "ctx", [(1, 0), (2, 3)])

    def level_done(self, terms):
        total, outward = terms
        inner = (self.level == 1) | (self.level == 2)
        return self.exchange_rows(jnp.where(inner, total, outward))

    def exchange_rows(self, rows):
        dim = rows.ndim - 2
        half = rows.shape[dim] // 2
        mine = lax.dynamic_slice_in_dim(rows, self.core * half, half, dim)
        other = self.sibling(lax.dynamic_slice_in_dim(rows, (1 - self.core) * half, half, dim))
        return jnp.where(self.core == 0, mine, other), jnp.where(self.core == 0, other, mine)

    def trade(self, array, outward, swapped):
        pairs = []
        for level in range(self.depth):
            for shard in range(self.shards):
                chip, core = divmod(shard, 2)
                side, odd = divmod(level, 2)
                slot = odd if not swapped else 1 - odd
                held = level * self.shards + shard
                worked = (2 * core + slot) * self.shards + 2 * chip + side
                pairs.append((held, worked) if outward else (worked, held))
        return lax.ppermute(array, ("ctx", "fsdp"), pairs)

    def to_slot(self, sends):
        return self.trade(sends[0], True, False), self.trade(sends[1], True, True)

    def both_halves(self, steps, trades):
        half = pair(steps, *trades)
        return half, self.sibling(half)

    def quarter_places(self):
        odd = self.level % 2
        near, far = 2 * self.core, 2 * (1 - self.core)
        return [near + odd, near + 1 - odd, far + odd, far + 1 - odd]

    def from_slot(self, quarters):
        return self.trade(quarters[0], False, False), self.trade(quarters[1], False, True)

    def received(self, trades):
        first, second = trades
        flip = self.level % 2 == 0
        return jnp.stack([jnp.where(flip, first, second), jnp.where(flip, second, first)])


def local(
    tokens,
    cotangent,
    sequence_lengths,
    slot_sequence,
    offset_bucket,
    first_gain,
    second_gain,
    query_weight,
    key_weight,
    value_weight,
    output_weight,
    expand_weight,
    contract_weight,
    bias_table,
    clip_limit,
):
    links = Links(bias_table.shape[0])
    core = links.core
    held_count, local_length, model_width = tokens.shape
    total_length = local_length * links.depth
    bucket_count, head_count = bias_table.shape
    inner_width = query_weight.shape[1]
    head_size = inner_width // head_count
    own_heads = head_count // 2
    own_inner = inner_width // 2
    slot_count = slot_sequence.shape[0]
    assert held_count == 2 and links.depth == 4

    slots = jnp.arange(slot_count)
    slot = links.chip * (2 * held_count) + links.level
    sequence = jnp.sum(jnp.where(slots == slot, slot_sequence, 0))
    length = jnp.sum(jnp.where(slots == sequence, sequence_lengths, 0)).astype(jnp.int32)
    odd = links.level % 2

    def numbers(*values):
        return jnp.stack([jnp.asarray(value, jnp.int32) for value in values])

    core_line = numbers(core)
    first_column = first_gain.astype(wide)[:, None]
    second_column = second_gain.astype(wide)[:, None]
    gains = jnp.concatenate([first_column, second_column], axis=1)
    attention_weights = (query_weight, key_weight, value_weight, output_weight)
    feed_weights = (expand_weight, contract_weight)
    steps = Steps()
    odd_line = odd.reshape(1)
    chips, square = links.chips, links.square
    order = links.order()
    places = numbers(*links.weight_places(), core, *order)
    order_line = numbers(*order)
    slot_places = numbers(*links.quarter_places(), length, *order)
    length_line = length.reshape(1)

    line_width = 2 * total_length
    falling = jnp.concatenate([jnp.flip(offset_bucket), jnp.full((1,), -1, jnp.int32)])
    matching = falling[:, None] == jnp.arange(bucket_count)[None, :]
    own_table = lax.dynamic_slice_in_dim(bias_table, core * own_heads, own_heads, 1)
    lines = dot(own_table, matching.astype(low), 0, 1)

    arrived = links.sibling(other_side(steps, core_line, attention_weights, feed_weights, gains))
    token_trades = links.to_slot(send_blocks(steps, odd_line, tokens))
    attention_pieces = links.gather(
        attention_shard(steps, core_line, attention_weights, gains, arrived)
    )
    strips = bias_strips(steps, lines.reshape(own_heads, 1, line_width))
    late_shard = hidden_shard(steps, core_line, 1, feed_weights, gains, arrived)
    steps.wait(*attention_pieces[1:3])
    token_halves = links.both_halves(steps, token_trades)
    token_low, normed_one, normed_one_t = token_rows_of(
        steps, slot_places, token_halves, True, chips, square
    )
    early_shard = hidden_shard(steps, core_line, 0, feed_weights, gains, arrived)
    early_pieces = links.gather(early_shard)
    cotangent_trades = links.to_slot(send_blocks(steps, odd_line, cotangent))
    qkv_width = 3 * own_inner
    qkv = rows_product(
        steps, places, [normed_one], attention_pieces, 0, qkv_width, False, "qkv_product"
    )
    pairs = own_inner // tile
    half_pairs = pairs // 2
    forward = functools.partial(attention_forward, steps, length_line, qkv, strips)
    first_context, first_totals, first_tops = forward(0, half_pairs)
    cotangent_halves = links.both_halves(steps, cotangent_trades)
    steps.wait(*early_pieces[1:3])
    last_context, last_totals, last_tops = forward(half_pairs, half_pairs)
    contexts = [first_context, last_context]
    steps.wait(early_pieces[-1])
    output_columns = (qkv_width, qkv_width + own_inner)
    attended = rows_product(
        steps, places, contexts, attention_pieces, *output_columns, True, "attended_product"
    )
    attended_other = links.sibling(attended)
    late_first = links.turn(late_shard, False)
    _, out_low, out_low_t = token_rows_of(
        steps, slot_places, cotangent_halves, False, chips, square
    )
    hidden_one, normed_two, normed_two_t = second_norm(
        steps, order_line, token_low, attended, attended_other, chips, square
    )
    late_pieces = links.gather_slowly(steps, late_shard, late_first)
    operands = (normed_two, normed_two_t, out_low, out_low_t)
    mixed_sum, normed_sum, *early_terms = feed_forward(steps, places, *operands, early_pieces)
    early = links.scatter(*early_terms)
    mixed_own, mixed_away, normed_two_part, *late_terms = feed_forward(
        steps, places, *operands, late_pieces, (mixed_sum, normed_sum)
    )
    normed_two_other = links.sibling(normed_two_part)
    mixed_other = links.sibling(mixed_away)
    late = links.scatter(*late_terms)
    early = links.scatter_near(steps, early)
    hidden_grad, attended_grad, attended_grad_t, context_grad = hidden_back(
        steps,
        places,
        normed_two_part,
        normed_two_other,
        hidden_one,
        out_low,
        attention_pieces,
        *output_columns,
        chips,
        square,
    )
    result_quarters = finish_half(
        steps, core, odd, length, mixed_own, mixed_other, hidden_one, token_low, False
    )
    result_trades = links.from_slot(result_quarters)

    def backward(pair):
        half = pair // half_pairs
        return attention_backward(
            steps,
            length_line,
            qkv,
            contexts[half],
            context_grad,
            (first_totals, last_totals)[half],
            strips,
            pair,
            half * half_pairs,
        )

    *grads_a, strips_a = backward(0)
    *grads_b, strips_b = backward(1)
    steps.wait(*result_trades)
    early = links.scatter_own(steps, early)
    late = links.scatter_near(steps, late)
    first = links.scatter(
        *attention_terms(steps, attended_grad_t, normed_one_t, contexts, grads_a + grads_b)
    )
    *grads_c, strips_c = backward(2)
    late = links.scatter_own(steps, late)
    *grads_d, strips_d = backward(3)
    early = links.level_across(steps, early)
    first = links.scatter_near(steps, first)
    last = links.scatter(
        *attention_terms(steps, attended_grad_t, normed_one_t, (), grads_c + grads_d)
    )
    own_part, away_part = input_product(
        steps, places, grads_a + grads_b + grads_c + grads_d, attention_pieces
    )
    away_other = links.sibling(away_part)
    first = links.scatter_own(steps, first)
    late = links.level_across(steps, late)
    last = links.scatter_near(steps, last)
    early = links.level_out(steps, early)
    last = links.scatter_own(steps, last)
    first = links.level_across(steps, first)
    input_quarters = finish_half(
        steps, core, odd, length, own_part, away_other, hidden_grad, token_low, True
    )
    input_trades = links.from_slot(input_quarters)
    steps.wait(early[1])
    late = links.level_out(steps, late)
    last = links.level_across(steps, last)
    result_pieces = links.gather(links.received(result_trades))
    first = links.level_out(steps, first)
    early_left, early_right = links.level_done(early)
    steps.wait(late[1], *input_trades)
    diagonals = jnp.concatenate(
        [diagonal_sums(steps, part) for part in (strips_a, strips_b, strips_c, strips_d)], axis=0
    ).reshape(own_heads, line_width)
    table_grad = lax.dot_general(
        diagonals,
        matching.astype(wide),
        (((1,), (0,)), ((), ())),
        precision=lax.Precision.HIGHEST,
        preferred_element_type=wide,
    )
    tops = jnp.concatenate([first_tops, last_tops], axis=0).reshape(own_heads, tile)
    small = jnp.concatenate([table_grad, tops[:, : tile - bucket_count]], axis=1)
    for small in links.small_hops(small):
        pass
    last = links.level_out(steps, last)
    late_left, late_right = links.level_done(late)
    first_left, first_right = links.level_done(first)
    last_left, last_right = links.level_done(last)
    input_gradient = links.received(input_trades).astype(wide)

    def slot_of(wanted):
        return jnp.sum(jnp.where(slot_sequence == wanted, slots, 0))

    own_slots = [slot_of(links.shard * held_count + row) for row in range(held_count)]
    other_slots = [slot_of((links.shard ^ 1) * held_count + row) for row in range(held_count)]
    piece_slots = [
        (2 * chip + core) * held_count + row
        for chip in order
        for row in range(held_count)
    ]
    picked, picked_other = pick_slots(
        steps,
        numbers(*own_slots, *other_slots, *piece_slots),
        result_pieces,
    )
    from_other = links.sibling(picked_other)
    output = jnp.stack(
        [
            jnp.where((s // held_count) % 2 == core, picked[row], from_other[row])
            for row, s in enumerate(own_slots)
        ]
    )

    def side_by_side(*parts):
        return jnp.concatenate(parts, axis=1).astype(wide)

    raw_two = side_by_side(early_left[0], late_left[0], early_right[0], late_right[0])
    contract_weight_gradient = side_by_side(
        early_left[1], late_left[1], early_right[1], late_right[1]
    )

    output_weight_gradient = side_by_side(first_left[:, :own_inner], first_right[:, :own_inner])

    def inner_columns(block):
        pieces = []
        for first_side, last_side in ((first_left, last_left), (first_right, last_right)):
            for start, side in ((own_inner, first_side), (0, last_side)):
                for pair in range(half_pairs):
                    first = start + (3 * pair + block) * tile
                    pieces.append(side[:, first : first + tile])
        return side_by_side(*pieces)

    raw_query, raw_key, raw_value = (inner_columns(block) for block in range(3))
    first_gain_gradient = jnp.sum(
        query_weight.astype(wide) * raw_query
        + key_weight.astype(wide) * raw_key
        + value_weight.astype(wide) * raw_value,
        axis=1,
    )
    second_gain_gradient = jnp.sum(expand_weight.astype(wide) * raw_two, axis=1)
    query_weight_gradient = first_column * raw_query
    key_weight_gradient = first_column * raw_key
    value_weight_gradient = first_column * raw_value
    expand_weight_gradient = second_column * raw_two

    small = links.in_order(small, links.sibling(small))
    table_rows = bucket_count // links.shards
    bias_table_gradient = lax.dynamic_slice_in_dim(
        small[:, :bucket_count].T, links.shard * table_rows, table_rows, 0
    )
    largest = small[:, bucket_count]
    shrink = clip_limit / jnp.maximum(clip_limit, largest)
    column_scale = jnp.repeat(jnp.sqrt(shrink), head_size)
    new_query_weight = query_weight.astype(wide) * column_scale[None, :]
    new_key_weight = key_weight.astype(wide) * column_scale[None, :]
    return (
        output,
        input_gradient,
        first_gain_gradient,
        second_gain_gradient,
        query_weight_gradient,
        key_weight_gradient,
        value_weight_gradient,
        output_weight_gradient,
        expand_weight_gradient,
        contract_weight_gradient,
        bias_table_gradient,
        largest,
        new_query_weight,
        new_key_weight,
    )


def solution(mesh):
    return jax.shard_map(
        local,
        mesh=mesh,
        in_specs=(
            P("fsdp", "ctx", None),
            P("fsdp", "ctx", None),
            P(),
            P(),
            P(),
            P("fsdp"),
            P("fsdp"),
            P("fsdp", None),
            P("fsdp", None),
            P("fsdp", None),
            P("fsdp", None),
            P("fsdp", None),
            P("fsdp", None),
            P(),
            P(),
        ),
        out_specs=(
            P("fsdp", "ctx", None),
            P("fsdp", "ctx", None),
            P("fsdp"),
            P("fsdp"),
            P("fsdp", None),
            P("fsdp", None),
            P("fsdp", None),
            P("fsdp", None),
            P("fsdp", None),
            P("fsdp", None),
            P("fsdp", None),
            P(),
            P("fsdp", None),
            P("fsdp", None),
        ),
        check_vma=False,
    )
```

```python
import functools
import math

import jax
import jax.numpy as jnp
from jax import lax
from jax.experimental import pallas as pl
from jax.experimental.pallas import tpu as pltpu
from jax.sharding import PartitionSpec as P

epsilon = 1e-06
masked = -1e30
tile = 128
half_tile = 64
wide = jnp.float32
low = jnp.bfloat16
anywhere = pl.BlockSpec(memory_space=pl.ANY)
in_vmem = pl.BlockSpec(memory_space=pltpu.VMEM)
in_hbm = pl.BlockSpec(memory_space=pltpu.HBM)


def pinned(array):
    return pltpu.with_memory_space_constraint(array, pltpu.HBM)


class Steps:
    def __init__(self):
        self.behind = ()

    def wait(self, *arrays):
        self.behind += arrays

    def launch(
        self,
        name,
        kernel,
        operands,
        in_specs,
        out_specs,
        out_shape,
        grid=(1,),
        prefetch=1,
        scratch=(),
        estimate=(0, 1 << 20),
        memory=24,
        stored=(),
    ):
        inputs, idle = len(operands), self.behind

        def run(*refs):
            refs = list(refs)
            mark_ref = refs.pop(inputs + len(idle) + len(out_specs))
            mark_ref[...] = jnp.zeros_like(mark_ref)
            kernel(*refs[:inputs], *refs[inputs + len(idle) :])

        out_specs, out_shape = list(out_specs), list(out_shape)
        outs = pl.pallas_call(
            run,
            grid_spec=pltpu.PrefetchScalarGridSpec(
                num_scalar_prefetch=prefetch,
                grid=grid,
                in_specs=list(in_specs) + [anywhere] * len(idle),
                out_specs=out_specs + [pl.BlockSpec((8, tile), lambda *_: (0, 0))],
                scratch_shapes=list(scratch),
            ),
            out_shape=[
                pltpu.HBM(shape, kind) if number in stored else jax.ShapeDtypeStruct(shape, kind)
                for number, (shape, kind) in enumerate(out_shape + [((8, tile), wide)])
            ],
            compiler_params=pltpu.CompilerParams(vmem_limit_bytes=memory << 20),
            cost_estimate=pl.CostEstimate(
                flops=int(estimate[0]), bytes_accessed=int(estimate[1]), transcendentals=0
            ),
            name=name,
        )(*operands, *idle)
        self.behind = (outs[-1],)
        return outs[:-1]


def dot(left, right, left_dim, right_dim):
    return lax.dot_general(
        left, right, (((left_dim,), (right_dim,)), ((), ())), preferred_element_type=wide
    )


def strip_kernel(line_ref, strip_ref):
    width = line_ref.shape[-1]
    rows = jnp.broadcast_to(line_ref[0], (tile, width))
    strip_ref[0] = pltpu.roll(rows, width - (tile - 1), 1, stride=1, stride_axis=0)


def bias_strips(steps, lines):
    heads, _, width = lines.shape
    return steps.launch(
        "bias_strips",
        strip_kernel,
        [lines],
        [pl.BlockSpec((1, 1, width), lambda h: (h, 0, 0))],
        [pl.BlockSpec((1, tile, width), lambda h: (h, 0, 0))],
        [((heads, tile, width), wide)],
        grid=(heads,),
        prefetch=0,
        memory=16,
        stored=(0,),
        estimate=(0, 8 << 20),
    )[0]


def diagonal_kernel(strip_ref, line_ref):
    strip = strip_ref[0]
    rows = tile
    while rows > 1:
        rows //= 2
        strip = pltpu.roll(strip[:rows], rows, 1) + strip[rows:]
    line_ref[0] = strip


def diagonal_sums(steps, strips):
    heads, _, width = strips.shape
    return steps.launch(
        "diagonal_sums",
        diagonal_kernel,
        [strips],
        [pl.BlockSpec((1, tile, width), lambda h: (h, 0, 0))],
        [pl.BlockSpec((1, 1, width), lambda h: (h, 0, 0))],
        [((heads, 1, width), wide)],
        grid=(heads,),
        prefetch=0,
        memory=16,
        estimate=(0, 2 << 20),
    )[0]


def one_head(block, head, extra=None):
    lane = lax.broadcasted_iota(jnp.int32, block.shape, 1)
    kept = jnp.where((lane >= half_tile) if head else (lane < half_tile), block, 0)
    if extra is None:
        return kept
    return jnp.where(lane == (0 if head else half_tile), extra, kept)


def key_masks(total, length):
    position = lax.broadcasted_iota(jnp.int32, (total, tile), 0)
    return jnp.where(position < length, 0.0, masked).astype(low)


def strip_columns(total, first, width):
    return [
        pl.ds(pl.multiple_of(total - tile - row + first, tile), width)
        for row in range(0, total, tile)
    ]


def add_bias(products, strip_ref, head, columns):
    return jnp.concatenate(
        [
            products[block * tile : (block + 1) * tile] + strip_ref[head, :, where]
            for block, where in enumerate(columns)
        ],
        axis=0,
    )


def forward_kernel(
    length_ref, query_ref, key_ref, value_ref, strip_ref, context_ref, total_ref, top_ref, *, step
):
    length = length_ref[0]
    total = query_ref.shape[0]
    masks = key_masks(total, length)
    ones = jnp.ones((step, tile), low)
    keys = [one_head(key_ref[...], head, masks) for head in (0, 1)]
    values = [one_head(value_ref[...], head).astype(wide).T.astype(low) for head in (0, 1)]

    def body(index, tops):
        first = pl.multiple_of(index * step, step)
        queries = query_ref[pl.ds(first, step), :]
        columns = strip_columns(total, first, step)
        query_okay = first + lax.broadcasted_iota(jnp.int32, (1, step), 1) < length
        context = None
        peaks = []
        for head in (0, 1):
            products = dot(keys[head], one_head(queries, head, ones), 1, 1)
            scores = add_bias(products, strip_ref, head, columns)
            row_max = jnp.max(scores, axis=0, keepdims=True)
            exponent = jnp.exp(scores - row_max)
            summed = jnp.sum(exponent, axis=0, keepdims=True)
            part = dot(values[head], exponent.astype(low), 1, 0) * (1.0 / summed)
            context = part if context is None else context + part
            total_ref[0, head : head + 1, pl.ds(first, step)] = row_max + jnp.log(summed)
            peaks.append(
                jnp.where(query_okay, jnp.max(products, axis=0, keepdims=True), masked)
            )
        context_ref[pl.ds(first, step), :] = context.T.astype(low)
        return tuple(jnp.maximum(top, peak) for top, peak in zip(tops, peaks))

    tops = lax.fori_loop(
        0, total // step, body, tuple(jnp.full((1, step), masked, wide) for _ in (0, 1))
    )
    for head in (0, 1):
        peak = jnp.max(tops[head], axis=1, keepdims=True)
        top_ref[0, head : head + 1, :] = jnp.broadcast_to(peak, (1, tile))


def attention_forward(steps, length, qkv, strips, start, count, step=512):
    total = qkv.shape[0]
    pairs = qkv.shape[1] // (3 * tile)
    strip_width = strips.shape[2]

    def columns(which):
        return pl.BlockSpec((total, tile), lambda p, _: (0, which * pairs + start + p))

    return steps.launch(
        "attention_forward",
        functools.partial(forward_kernel, step=step),
        [length, qkv, qkv, qkv, strips],
        [columns(which) for which in range(3)]
        + [pl.BlockSpec((2, tile, strip_width), lambda p, _: (start + p, 0, 0))],
        [
            pl.BlockSpec((total, tile), lambda p, _: (0, p)),
            pl.BlockSpec((1, 2, total), lambda p, _: (p, 0, 0)),
            pl.BlockSpec((1, 2, tile), lambda p, _: (p, 0, 0)),
        ],
        [((total, count * tile), low), ((count, 2, total), wide), ((count, 2, tile), wide)],
        grid=(count,),
        memory=32,
        estimate=(6e9 * count, (3 << 20) * count),
    )


def backward_kernel(
    length_ref,
    query_ref,
    key_ref,
    value_ref,
    context_ref,
    grad_ref,
    total_ref,
    strip_ref,
    query_grad_ref,
    key_grad_ref,
    value_grad_ref,
    strip_grad_ref,
    key_sum,
    value_sum,
    *,
    step,
):
    length = length_ref[0]
    total = query_ref.shape[0]
    masks = key_masks(total, length)
    ones = jnp.ones((step, tile), low)
    keys = [one_head(key_ref[...], head, masks) for head in (0, 1)]
    plain_keys = [one_head(key_ref[...], head) for head in (0, 1)]
    values = [one_head(value_ref[...], head) for head in (0, 1)]
    key_sum[...] = jnp.zeros_like(key_sum)
    value_sum[...] = jnp.zeros_like(value_sum)
    strip_grad_ref[...] = jnp.zeros_like(strip_grad_ref)

    def body(index, carry):
        first = pl.multiple_of(index * step, step)
        queries = query_ref[pl.ds(first, step), :]
        grads = grad_ref[pl.ds(first, step), :]
        columns = strip_columns(total, first, step)
        inner = grads.astype(wide) * context_ref[pl.ds(first, step), :].astype(wide)
        query_grad = None
        for head in (0, 1):
            head_grads = one_head(grads, head)
            pick = one_head(jnp.ones((8, tile), wide), head)
            row_inner = lax.dot_general(
                pick,
                inner,
                (((1,), (1,)), ((), ())),
                precision=lax.Precision.HIGHEST,
                preferred_element_type=wide,
            )[:1]
            log_total = total_ref[0, head : head + 1, pl.ds(first, step)]
            products = dot(keys[head], one_head(queries, head, ones), 1, 1)
            probs = jnp.exp(add_bias(products, strip_ref, head, columns) - log_total)
            value_sum[...] += dot(probs.astype(low), head_grads, 1, 0)
            score_grad = probs * (dot(values[head], head_grads, 1, 1) - row_inner)
            for block, where in enumerate(columns):
                strip_grad_ref[head, :, where] += score_grad[block * tile : (block + 1) * tile]
            score_low = score_grad.astype(low)
            key_sum[...] += dot(score_low, one_head(queries, head), 1, 0)
            part = dot(score_low, plain_keys[head], 0, 0)
            query_grad = part if query_grad is None else query_grad + part
        query_grad_ref[pl.ds(first, step), :] = query_grad.astype(low)
        return carry

    lax.fori_loop(0, total // step, body, 0)
    key_grad_ref[...] = key_sum[...].astype(low)
    value_grad_ref[...] = value_sum[...].astype(low)


def attention_backward(
    steps, length, qkv, context, context_grad, log_totals, strips, start, held, step=256
):
    total = qkv.shape[0]
    pairs = qkv.shape[1] // (3 * tile)
    strip_width = strips.shape[2]

    def columns(which, first=start):
        return pl.BlockSpec((total, tile), lambda p, _: (0, which * pairs + first + p))

    part = pl.BlockSpec((total, tile), lambda p, _: (0, p))
    return steps.launch(
        "attention_backward",
        functools.partial(backward_kernel, step=step),
        [length, qkv, qkv, qkv, context, context_grad, log_totals, pinned(strips)],
        [
            columns(0),
            columns(1),
            columns(2),
            columns(0, start - held),
            columns(0),
            pl.BlockSpec((1, 2, total), lambda p, _: (start - held + p, 0, 0)),
            pl.BlockSpec((2, tile, strip_width), lambda p, _: (start + p, 0, 0)),
        ],
        [part, part, part, pl.BlockSpec((2, tile, strip_width), lambda p, _: (p, 0, 0))],
        [((total, tile), low)] * 3 + [((2, tile, strip_width), wide)],
        scratch=[pltpu.VMEM((total, tile), wide)] * 2,
        memory=32,
        stored=(3,),
        estimate=(1e10, 6 << 20),
    )


def gelu_and_slope(values):
    distance = jnp.abs(values) * math.sqrt(0.5)
    ratio = 1.0 / (1.0 + 0.3275911 * distance)
    density = jnp.exp(-distance * distance)
    poly = 1.061405429 * ratio - 1.453152027
    poly = poly * ratio + 1.421413741
    poly = poly * ratio - 0.284496736
    poly = poly * ratio + 0.254829592
    tail = (0.5 * ratio) * poly * density
    cumulative = jnp.where(values >= 0, 1.0 - tail, tail)
    slope = cumulative + values * density * (1.0 / math.sqrt(2.0 * math.pi))
    return values * cumulative, slope


def beside(refs):
    return jnp.concatenate([ref[...] for ref in refs], axis=1)


def start_copies(index_ref, pieces, target, semaphores, columns=None):
    copies = []
    for number, piece in enumerate(pieces):
        for side in (0, 1):
            entry = 2 * number + side
            rows = piece.shape[-2]
            where = pl.ds(pl.multiple_of(index_ref[entry] * rows, rows), rows)
            if columns is not None:
                source, place = piece.at[side, :, columns], target.at[where, :]
            else:
                source, place = piece.at[side], target.at[:, where, :]
            copies.append(pltpu.make_async_copy(source, place, semaphores.at[entry]))
    for copy in copies:
        copy.start()
    return copies


def transposed_rows(order_ref, source_ref, target_ref, columns, chips, ordered):
    share = source_ref.shape[1] // chips
    for block in range(chips):
        if ordered:
            first = pl.multiple_of(order_ref[block] * share, share)
            part = source_ref[:, pl.ds(first, share)]
        else:
            part = source_ref[:, block * share : (block + 1) * share]
        target_ref[block * share : (block + 1) * share, columns] = part.T.astype(low)


def send_kernel(odd_ref, block_ref, first_ref, second_ref):
    @pl.when(pl.program_id(0) == 0)
    def _():
        first_ref[...] = block_ref[0]

    @pl.when(pl.program_id(0) == 1)
    def _():
        second_ref[...] = block_ref[0]


def send_blocks(steps, odd, blocks):
    shape = blocks.shape[1:]
    out = pl.BlockSpec(shape, lambda i, _: (0, 0))
    return steps.launch(
        "send_blocks",
        send_kernel,
        [odd, pinned(blocks)],
        [pl.BlockSpec((1,) + shape, lambda i, odd_ref: ((odd_ref[0] + i) % 2, 0, 0))],
        [out, out],
        [(shape, low)] * 2,
        grid=(2,),
        memory=8,
        estimate=(0, 2 << 20),
    )


def scaled(block, gain):
    return (gain * block.astype(wide)).astype(low)


def column_copies(core, weights, targets, semaphores, first=0, parts=1, part=0):
    copies = []
    for number, (weight, target) in enumerate(zip(weights, targets)):
        width = weight.shape[1] // (2 * parts)
        columns = pl.ds(pl.multiple_of((parts * core + part) * width, width), width)
        copies.append(
            pltpu.make_async_copy(weight.at[:, columns], target, semaphores.at[first + number])
        )
    return copies


def run_copies(copies):
    for copy in copies:
        copy.start()
    for copy in copies:
        copy.wait()


def side_kernel(core_ref, *refs):
    attention, feed = refs[:4], refs[4:6]
    gain_ref, out_ref, semaphores = refs[6:]
    core = 1 - core_ref[0]
    inner = attention[0].shape[1] // 2
    hidden = feed[0].shape[1] // 4
    targets = [out_ref.at[:, n * inner : (n + 1) * inner] for n in range(4)]
    copies = column_copies(core, attention, targets, semaphores)
    first = 4 * inner
    for part in (0, 1):
        start = first + 2 * part * hidden
        targets = [out_ref.at[:, start + n * hidden : start + (n + 1) * hidden] for n in (0, 1)]
        copies += column_copies(core, feed, targets, semaphores, 4 + 2 * part, 2, part)
    run_copies(copies)
    out_ref[:, : 3 * inner] = scaled(out_ref[:, : 3 * inner], gain_ref[:, :1])
    for part in (0, 1):
        columns = slice(first + 2 * part * hidden, first + (2 * part + 1) * hidden)
        out_ref[:, columns] = scaled(out_ref[:, columns], gain_ref[:, 1:])


def relay_kernel(first_ref, second_ref, first_out_ref, second_out_ref):
    first_out_ref[...] = first_ref[...]
    second_out_ref[...] = second_ref[...]


def relay(steps, first, second):
    block = pl.BlockSpec((1,) + first.shape[1:], lambda i: (i,) + (0,) * (first.ndim - 1))
    return steps.launch(
        "relay",
        relay_kernel,
        [first, second],
        [block, block],
        [block, block],
        [(first.shape, low)] * 2,
        grid=(first.shape[0],),
        prefetch=0,
        memory=8,
    )


def pair_kernel(first_ref, second_ref, out_ref):
    out_ref[0] = first_ref[...]
    out_ref[1] = second_ref[...]


def pair(steps, first, second):
    rows, width = first.shape
    step = rows // 2
    block = pl.BlockSpec((step, width), lambda i: (i, 0))
    return steps.launch(
        "pair",
        pair_kernel,
        [first, second],
        [block] * 2,
        [pl.BlockSpec((2, step, width), lambda i: (0, i, 0))],
        [((2, rows, width), low)],
        grid=(2,),
        prefetch=0,
        memory=8,
    )[0]


def other_side(steps, core, attention, feed, gains):
    rows = attention[0].shape[0]
    columns = sum(weight.shape[1] for weight in attention + feed) // 2
    return steps.launch(
        "other_side",
        side_kernel,
        [core, *map(pinned, (*attention, *feed)), gains],
        [in_hbm] * 6 + [in_vmem],
        [in_vmem],
        [((rows, columns), low)],
        scratch=[pltpu.SemaphoreType.DMA((8,))],
        memory=8,
    )[0]


def attention_shard_kernel(core_ref, *refs):
    attention = refs[:4]
    gain_ref, arrived_ref, out_ref, semaphores = refs[4:]
    inner = attention[0].shape[1] // 2
    targets = [out_ref.at[0, :, n * inner : (n + 1) * inner] for n in range(4)]
    copies = column_copies(core_ref[0], attention, targets, semaphores)
    source = arrived_ref.at[:, : 4 * inner]
    copies.append(pltpu.make_async_copy(source, out_ref.at[1], semaphores.at[4]))
    run_copies(copies)
    out_ref[0, :, : 3 * inner] = scaled(out_ref[0, :, : 3 * inner], gain_ref[:, :1])


def attention_shard(steps, core, weights, gains, arrived):
    rows = weights[0].shape[0]
    columns = sum(weight.shape[1] for weight in weights) // 2
    return steps.launch(
        "attention_shard",
        attention_shard_kernel,
        [core, *map(pinned, weights), gains, pinned(arrived)],
        [in_hbm] * 4 + [in_vmem, anywhere],
        [in_vmem],
        [((2, rows, columns), low)],
        scratch=[pltpu.SemaphoreType.DMA((5,))],
        memory=8,
    )[0]


def hidden_shard_kernel(core_ref, *refs, part):
    feed = refs[:2]
    gain_ref, arrived_ref, out_ref, semaphores = refs[2:]
    hidden = out_ref.shape[3]
    targets = [out_ref.at[0, number] for number in (0, 1)]
    copies = column_copies(core_ref[0], feed, targets, semaphores, 0, 2, part)
    for number in (0, 1):
        start = 2 * hidden * (1 + part) + number * hidden
        source = arrived_ref.at[:, start : start + hidden]
        copies.append(
            pltpu.make_async_copy(source, out_ref.at[1, number], semaphores.at[2 + number])
        )
    run_copies(copies)
    out_ref[0, 0] = scaled(out_ref[0, 0], gain_ref[:, 1:])


def hidden_shard(steps, core, part, weights, gains, arrived):
    rows, columns = weights[0].shape
    return steps.launch(
        "hidden_shard",
        functools.partial(hidden_shard_kernel, part=part),
        [core, *map(pinned, weights), gains, pinned(arrived)],
        [in_hbm] * 2 + [in_vmem, anywhere],
        [in_vmem],
        [((2, 2, rows, columns // 4), low)],
        scratch=[pltpu.SemaphoreType.DMA((4,))],
        memory=8,
    )[0]


def token_kernel(place_ref, *refs, normed, chips, ordered):
    halves = refs[:2]
    plain_ref, first_ref, first_t_ref, semaphores = refs[-4:]
    total = plain_ref.shape[0]
    step = total // 4
    copies = []
    for number in range(4):
        where = pl.ds(pl.multiple_of(place_ref[number] * step, step), step)
        source = halves[number // 2].at[number % 2]
        copies.append(
            pltpu.make_async_copy(source, plain_ref.at[where, :], semaphores.at[number])
        )
    for copy in copies:
        copy.start()
    for copy in copies:
        copy.wait()
    for block in range(4):
        rows = slice(block * step, (block + 1) * step)
        values = plain_ref[rows, :].astype(wide)
        if normed:
            values = normalize(values)[0]
        else:
            position = block * step + lax.broadcasted_iota(jnp.int32, values.shape, 0)
            values = jnp.where(position < place_ref[4], values, 0.0)
        first_ref[rows, :] = values.astype(low)
        transposed_rows(
            place_ref.at[pl.ds(5, chips)],
            first_ref.at[rows, :],
            first_t_ref,
            rows,
            chips,
            ordered,
        )


def token_rows_of(steps, places, pieces, normed, chips, ordered):
    total, width = 4 * pieces[0].shape[1], pieces[0].shape[2]
    return steps.launch(
        "token_rows" if normed else "cotangent_rows",
        functools.partial(token_kernel, normed=normed, chips=chips, ordered=ordered),
        [places, *(map(pinned, pieces) if normed else pieces)],
        [anywhere] * 2,
        [in_vmem] * 3,
        [((total, width), low), ((total, width), low), ((width, total), low)],
        scratch=[pltpu.SemaphoreType.DMA((4,))],
        memory=24,
        stored=() if normed else (1, 2),
        estimate=(0, 10 << 20),
    )


def rows_product_kernel(place_ref, *refs, factors, count, columns, across):
    rows = refs[:factors]
    pieces = refs[factors : factors + count]
    out_ref, weight, semaphores = refs[factors + count :]

    @pl.when(pl.program_id(0) == 0)
    def _():
        for copy in start_copies(place_ref, pieces, weight, semaphores, columns):
            copy.wait()

    operand = beside(rows)
    out_ref[...] = dot(operand, weight[...], 1, 1 if across else 0).astype(low)


def rows_product(steps, places, rows, pieces, first, last, across, name, step=256):
    total, depth = rows[0].shape
    count = len(pieces)
    whole = (2 * count * pieces[0].shape[1], last - first)
    width = whole[0] if across else whole[1]
    return steps.launch(
        name,
        functools.partial(
            rows_product_kernel,
            factors=len(rows),
            count=count,
            columns=pl.ds(first, last - first),
            across=across,
        ),
        [places, *rows, *pieces],
        [pl.BlockSpec((step, depth), lambda i, _: (i, 0))] * len(rows) + [anywhere] * count,
        [pl.BlockSpec((step, width), lambda i, _: (i, 0))],
        [((total, width), low)],
        grid=(total // step,),
        scratch=[pltpu.VMEM(whole, low), pltpu.SemaphoreType.DMA((2 * count,))],
        estimate=(2 * total * whole[0] * whole[1], 8 << 20),
    )[0]


def second_norm_kernel(
    order_ref, token_ref, mine_ref, other_ref, hidden_ref, normed_ref, normed_t_ref, *, chips, ordered
):
    attended = mine_ref[...].astype(wide) + other_ref[...].astype(wide)
    hidden = token_ref[...].astype(wide) + attended
    hidden_ref[...] = hidden
    normed_ref[...] = normalize(hidden)[0].astype(low)
    transposed_rows(order_ref, normed_ref, normed_t_ref, slice(None), chips, ordered)


def second_norm(steps, order, tokens, mine, other, chips, ordered, step=256):
    total, width = tokens.shape
    block = pl.BlockSpec((step, width), lambda i, _: (i, 0))
    return steps.launch(
        "second_norm",
        functools.partial(second_norm_kernel, chips=chips, ordered=ordered),
        [order, tokens, mine, other],
        [block] * 3,
        [block, block, pl.BlockSpec((width, step), lambda i, _: (0, i))],
        [((total, width), wide), ((total, width), low), ((width, total), low)],
        grid=(total // step,),
        stored=(0, 1, 2),
        estimate=(0, 14 << 20),
    )


def feed_forward_kernel(
    place_ref, normed_ref, normed_t_ref, grad_ref, grad_t_ref, *refs, count, first
):
    pieces = refs[:count]
    refs = refs[count:]
    if first:
        mixed_sum, normed_sum, keep_ref, send_ref, weight, semaphores = refs
        before = ()
    else:
        before = refs[:2]
        own_ref, other_ref, normed_grad_ref, keep_ref, send_ref = refs[2:7]
        weight, semaphores, mixed_sum, normed_sum = refs[7:]
    index = pl.program_id(0)
    step = keep_ref.shape[2]
    half = keep_ref.shape[1]
    carried = [
        pltpu.make_async_copy(source, target, semaphores.at[2 * count + number])
        for number, (source, target) in enumerate(zip(before, (mixed_sum, normed_sum)))
    ]

    @pl.when(index == 0)
    def _():
        copies = start_copies(place_ref, pieces, weight, semaphores)
        for copy in carried:
            copy.start()
        for copy in copies:
            copy.wait()

    columns = pl.ds(pl.multiple_of(index * step, step), step)
    expand = weight[0, :, columns]
    contract = weight[1, :, columns]
    pre_act = dot(normed_ref[...], expand, 1, 0)
    act_grad = dot(grad_ref[...], contract, 1, 0).astype(low).astype(wide)
    activated, slope = gelu_and_slope(pre_act)
    activated = activated.astype(low)
    pre_grad = (act_grad * slope).astype(low)
    for part, (rows_ref, values) in enumerate(
        ((normed_t_ref, pre_grad), (grad_t_ref, activated))
    ):
        keep_ref[part] = dot(rows_ref[:half, :], values, 1, 0).astype(low)
        send_ref[part] = dot(rows_ref[half:, :], values, 1, 0).astype(low)
    mixed = dot(activated, contract, 1, 1)
    normed_grad = dot(pre_grad, expand, 1, 1)
    if first:

        @pl.when(index == 0)
        def _():
            mixed_sum[...] = mixed
            normed_sum[...] = normed_grad

        @pl.when(index > 0)
        def _():
            mixed_sum[...] += mixed
            normed_sum[...] += normed_grad

    else:

        @pl.when(index == 0)
        def _():
            for copy in carried:
                copy.wait()

        mixed_sum[...] += mixed
        normed_sum[...] += normed_grad

        @pl.when(index == pl.num_programs(0) - 1)
        def _():
            rows = own_ref.shape[0]
            core = place_ref[2 * count]
            own = pl.multiple_of(core * rows, rows)
            away = pl.multiple_of((1 - core) * rows, rows)
            own_ref[...] = mixed_sum[pl.ds(own, rows), :].astype(low)
            other_ref[...] = mixed_sum[pl.ds(away, rows), :].astype(low)
            normed_grad_ref[...] = normed_sum[...].astype(low)


def feed_forward(steps, places, normed, normed_t, grad, grad_t, pieces, before=None, step=1024):
    rows, width = normed.shape
    count = len(pieces)
    hidden = pieces[0].shape[3]
    first = before is None

    def fixed(shape):
        return pl.BlockSpec(shape, lambda i, _: (0,) * len(shape), pipeline_mode=pl.Buffered(1))

    whole = fixed((rows, width))
    scratch = [
        pltpu.VMEM((2, width, hidden), low),
        pltpu.SemaphoreType.DMA((2 * count + 2,)),
    ]
    if first:
        before = ()
        out_specs = [whole, whole]
        out_shape = [((rows, width), wide)] * 2
    else:
        part = fixed((rows // 2, width))
        out_specs = [part, part, whole]
        out_shape = [((rows // 2, width), low)] * 2 + [((rows, width), low)]
        scratch += [pltpu.VMEM((rows, width), wide)] * 2
    return steps.launch(
        "feed_forward",
        functools.partial(feed_forward_kernel, count=count, first=first),
        [places, *map(pinned, (normed, normed_t, grad, grad_t)), *pieces, *before],
        [whole, fixed((width, rows))] * 2 + [anywhere] * (count + len(before)),
        out_specs + [pl.BlockSpec((2, width // 2, step), lambda i, _: (0, 0, i))] * 2,
        out_shape + [((2, width // 2, hidden), low)] * 2,
        grid=(hidden // step,),
        scratch=scratch,
        memory=58,
        stored=(0, 1) if first else (),
        estimate=(20 * rows * width * hidden, 40 << 20),
    )


def hidden_back_kernel(
    place_ref, mine_ref, other_ref, hidden_ref, grad_ref, *refs, count, columns, chips, ordered
):
    pieces = refs[:count]
    hidden_grad_ref, low_ref, low_t_ref, context_grad_ref, weight, semaphores = refs[count:]

    @pl.when(pl.program_id(0) == 0)
    def _():
        for copy in start_copies(place_ref, pieces, weight, semaphores, columns):
            copy.wait()

    upstream = mine_ref[...].astype(wide) + other_ref[...].astype(wide)
    hidden = hidden_ref[...]
    scale = normalize(hidden)[1]
    hidden_grad = grad_ref[...].astype(wide) + normalize_back(hidden, scale, upstream)
    hidden_grad_ref[...] = hidden_grad
    low_ref[...] = hidden_grad.astype(low)
    context_grad_ref[...] = dot(low_ref[...], weight[...], 1, 0).astype(low)
    order_ref = place_ref.at[pl.ds(2 * count + 1, chips)]
    transposed_rows(order_ref, low_ref, low_t_ref, slice(None), chips, ordered)


def hidden_back(
    steps, places, mine, other, hidden, grad, pieces, first, last, chips, ordered, step=256
):
    total, width = hidden.shape
    count = len(pieces)
    inner = last - first
    block = pl.BlockSpec((step, width), lambda i, _: (i, 0))
    return steps.launch(
        "hidden_back",
        functools.partial(
            hidden_back_kernel,
            count=count,
            columns=pl.ds(first, inner),
            chips=chips,
            ordered=ordered,
        ),
        [places, mine, other, pinned(hidden), pinned(grad), *pieces],
        [block] * 4 + [anywhere] * count,
        [
            block,
            block,
            pl.BlockSpec((width, step), lambda i, _: (0, i)),
            pl.BlockSpec((step, inner), lambda i, _: (i, 0)),
        ],
        [((total, width), wide), ((total, width), low), ((width, total), low), ((total, inner), low)],
        grid=(total // step,),
        scratch=[pltpu.VMEM((width, inner), low), pltpu.SemaphoreType.DMA((2 * count,))],
        estimate=(4 * total * width * inner, 24 << 20),
    )


def terms_kernel(*refs, contexts):
    grad_t_ref, normed_t_ref = refs[:2]
    factors = refs[2:-2]
    for number, target in enumerate(refs[-2:]):

        @pl.when(pl.program_id(0) == number)
        def _():
            first = 0
            if contexts:
                part = dot(grad_t_ref[...], beside(factors[:contexts]), 1, 0)
                first = part.shape[1]
                target[:, :first] = part.astype(low)
            part = dot(normed_t_ref[...], beside(factors[contexts:]), 1, 0)
            target[:, first:] = part.astype(low)


def attention_terms(steps, grad_t, normed_t, contexts, grads):
    width, total = normed_t.shape
    factors = list(contexts) + list(grads)
    columns = sum(factor.shape[1] for factor in factors)
    block = pl.BlockSpec((width // 2, total), lambda i: (i, 0))
    fixed = pl.BlockSpec((width // 2, columns), lambda i: (0, 0))
    return steps.launch(
        "attention_terms",
        functools.partial(terms_kernel, contexts=len(contexts)),
        [grad_t, normed_t, *factors],
        [block, block]
        + [
            pl.BlockSpec(factor.shape, lambda i: (0, 0), pipeline_mode=pl.Buffered(1))
            for factor in factors
        ],
        [fixed, fixed],
        [((width // 2, columns), low)] * 2,
        grid=(2,),
        prefetch=0,
        estimate=(2 * total * width * columns, 10 << 20),
    )


def sum_kernel(*refs):
    total = refs[0][...].astype(wide)
    for ref in refs[1:-1]:
        total += ref[...].astype(wide)
    refs[-1][...] = total.astype(low)


def row_sums(steps, parts):
    first = parts[0]
    rows = first[0].shape[-2] // (1 if first[1] is None else 2)
    shape = first[0].shape[:-2] + (rows, first[0].shape[-1])
    count = 4
    block = shape[:-2] + (rows // count, shape[-1])
    leading = (0,) * (len(shape) - 2)

    def spec(offset):
        return pl.BlockSpec(block, lambda i: leading + (i + offset, 0))

    return steps.launch(
        "row_sums",
        sum_kernel,
        [part for part, _ in parts],
        [spec(count if which else 0) for _, which in parts],
        [spec(0)],
        [(shape, low)],
        grid=(count,),
        prefetch=0,
        memory=12,
        estimate=(0, 4 << 20),
    )[0]


def input_product_kernel(place_ref, *refs, count, factors):
    grads = refs[:factors]
    pieces = refs[factors : factors + count]
    own_ref, other_ref, weight, semaphores = refs[factors + count :]
    index = pl.program_id(0)

    @pl.when(index == 0)
    def _():
        columns = pl.ds(0, weight.shape[1])
        for copy in start_copies(place_ref, pieces, weight, semaphores, columns):
            copy.wait()

    ordered = [ref for block in range(3) for ref in grads[block::3]]
    product = dot(beside(ordered), weight[...], 1, 1)

    @pl.when(index < 2)
    def _():
        other_ref[...] = product.astype(low)

    @pl.when(index >= 2)
    def _():
        own_ref[...] = product


def input_product(steps, places, grads, pieces):
    total = grads[0].shape[0]
    count = len(pieces)
    inner = sum(grad.shape[1] for grad in grads)
    width = 2 * count * pieces[0].shape[1]
    step = total // 4

    def rows(i, place_ref):
        core = place_ref[2 * count]
        return (jnp.where(i < 2, 2 * (1 - core) + i, 2 * core + i - 2), 0)

    return steps.launch(
        "input_product",
        functools.partial(input_product_kernel, count=count, factors=len(grads)),
        [places, *grads, *pieces],
        [pl.BlockSpec((step, grad.shape[1]), rows) for grad in grads] + [anywhere] * count,
        [
            pl.BlockSpec((step, width), lambda i, _: (jnp.maximum(i - 2, 0), 0)),
            pl.BlockSpec((step, width), lambda i, _: (jnp.minimum(i, 1), 0)),
        ],
        [((total // 2, width), wide), ((total // 2, width), low)],
        grid=(4,),
        scratch=[pltpu.VMEM((width, inner), low), pltpu.SemaphoreType.DMA((2 * count,))],
        memory=24,
        estimate=(2 * total * width * inner, 14 << 20),
    )


def finish_kernel(
    place_ref, own_ref, other_ref, base_ref, token_ref, first_ref, second_ref, *, back
):
    index = pl.program_id(0)
    summed = own_ref[...].astype(wide) + other_ref[...].astype(wide)
    if back:
        tokens = token_ref[...].astype(wide)
        values = base_ref[...] + normalize_back(tokens, normalize(tokens)[1], summed)
    else:
        row = (2 * place_ref[0] + index) * summed.shape[0]
        position = row + lax.broadcasted_iota(jnp.int32, summed.shape, 0)
        values = jnp.where(position < place_ref[2], base_ref[...] + summed, 0.0)
    values = values.astype(low)

    @pl.when(index == place_ref[1])
    def _():
        first_ref[...] = values

    @pl.when(index != place_ref[1])
    def _():
        second_ref[...] = values


def finish_half(steps, core, odd, length, own, other, base, tokens, back):
    rows, width = own.shape
    step = rows // 2
    half = pl.BlockSpec((step, width), lambda i, _: (i, 0))
    whole = pl.BlockSpec((step, width), lambda i, place_ref: (2 * place_ref[0] + i, 0))
    quarter = pl.BlockSpec((step, width), lambda i, _: (0, 0))
    return steps.launch(
        "input_gradient_rows" if back else "result_rows",
        functools.partial(finish_kernel, back=back),
        [
            jnp.stack([core, odd, length]).astype(jnp.int32),
            pinned(own) if back else own,
            other,
            pinned(base) if back else base,
            tokens,
        ],
        [half, half, whole, whole],
        [quarter, quarter],
        [((step, width), low)] * 2,
        grid=(2,),
        memory=12,
        estimate=(0, 6 << 20),
    )


def pick_kernel(slot_ref, *refs, count):
    pieces = refs[:count]
    own_ref, other_ref, semaphores = refs[count:]
    for row in range(4):
        target = (own_ref if row < 2 else other_ref).at[row % 2]
        for number in range(2 * count):

            @pl.when(slot_ref[row] == slot_ref[4 + number])
            def _():
                source = pieces[number // 2].at[number % 2]
                copy = pltpu.make_async_copy(source, target, semaphores.at[row])
                copy.start()
                copy.wait()


def pick_slots(steps, slots, pieces):
    count = len(pieces)
    return steps.launch(
        "pick_slots",
        functools.partial(pick_kernel, count=count),
        [slots, *pieces],
        [anywhere] * count,
        [in_vmem] * 2,
        [(pieces[0].shape, low)] * 2,
        scratch=[pltpu.SemaphoreType.DMA((4,))],
        memory=8,
        estimate=(0, 4 << 20),
    )


def normalize(values):
    scaled = lax.rsqrt(jnp.mean(values * values, axis=-1, keepdims=True) + epsilon)
    return (values * scaled, scaled)


def normalize_back(values, scaled, upstream):
    unit_rows = values * scaled
    return scaled * (upstream - unit_rows * jnp.mean(upstream * unit_rows, axis=-1, keepdims=True))


class Links:
    def __init__(self, buckets):
        self.buckets = buckets
        self.shards = lax.axis_size("fsdp")
        self.depth = lax.axis_size("ctx")
        self.shard = lax.axis_index("fsdp")
        self.level = lax.axis_index("ctx")
        self.chips = self.shards // 2
        self.chip = self.shard // 2
        self.core = self.shard % 2
        self.groups = [list(range(core, self.shards, 2)) for core in (0, 1)]
        self.square = self.chips == 4

    def sibling(self, array):
        return lax.ppermute(array, "fsdp", [(i, i ^ 1) for i in range(self.shards)])

    def across(self, array, bit):
        return lax.ppermute(array, "fsdp", [(i, i ^ (2 * bit)) for i in range(self.shards)])

    def in_order(self, mine, other):
        return jnp.concatenate(
            [jnp.where(self.core == 0, mine, other), jnp.where(self.core == 0, other, mine)], axis=0
        )

    def turn(self, array, second):
        pairs = [(i, i ^ (2 if (i % 2 == 0) != second else 4)) for i in range(self.shards)]
        return lax.ppermute(array, "fsdp", pairs)

    def order(self):
        if not self.square:
            return list(range(self.chips))
        return [self.chip, self.chip ^ (1 + self.core), self.chip ^ (2 - self.core), self.chip ^ 3]

    def gather_whole(self, shard):
        whole = lax.all_gather(shard, "fsdp", axis=0, axis_index_groups=self.groups)
        return [whole[chip] for chip in range(self.chips)]

    def gather(self, shard):
        if not self.square:
            return self.gather_whole(shard)
        first = self.turn(shard, False)
        return [shard, first, self.turn(shard, True), self.turn(first, True)]

    def gather_slowly(self, steps, shard, first):
        if not self.square:
            return self.gather_whole(shard)
        arrived, own = relay(steps, first, shard)
        return [shard, first, self.turn(own, True), self.turn(arrived, True)]

    def weight_places(self):
        return [2 * chip + side for chip in self.order() for side in (self.core, 1 - self.core)]

    def scatter(self, keep, send):
        dim = keep.ndim - 2
        if not self.square:
            summed = lax.psum_scatter(
                jnp.concatenate([keep, send], axis=dim),
                "fsdp",
                scatter_dimension=dim,
                tiled=True,
                axis_index_groups=self.groups,
            )
            return keep, summed.astype(low)
        return keep, self.turn(send, True)

    def scatter_near(self, steps, terms):
        keep, arrived = terms
        if not self.square:
            return keep, arrived, None
        near = row_sums(steps, [(keep, True), (arrived, True)])
        return keep, arrived, self.turn(near, False)

    def scatter_own(self, steps, terms):
        keep, arrived, last = terms
        total = arrived
        if self.square:
            total = row_sums(steps, [(keep, False), (arrived, False), (last, None)])
        return total, lax.ppermute(total, "ctx", [(0, 1), (3, 2)])

    def small_hops(self, small):
        hops = []
        bit = 1
        while bit < self.chips:
            hops.append(("fsdp", [(i, i ^ (2 * bit)) for i in range(self.shards)]))
            bit *= 2
        bit = 1
        while bit < self.depth:
            hops.append(("ctx", [(i, i ^ bit) for i in range(self.depth)]))
            bit *= 2
        for axis, pairs in hops:
            other = lax.ppermute(small, axis, pairs)
            lane = lax.broadcasted_iota(jnp.int32, small.shape, 1)
            small = jnp.where(lane < self.buckets, small + other, jnp.maximum(small, other))
            yield small

    def level_across(self, steps, terms):
        joined = row_sums(steps, [(part, None) for part in terms])
        return joined, lax.ppermute(joined, "ctx", [(1, 2), (2, 1)])

    def level_out(self, steps, terms):
        total = row_sums(steps, [(part, None) for part in terms])
        return total, lax.ppermute(total, "ctx", [(1, 0), (2, 3)])

    def level_done(self, terms):
        total, outward = terms
        inner = (self.level == 1) | (self.level == 2)
        return self.exchange_rows(jnp.where(inner, total, outward))

    def exchange_rows(self, rows):
        dim = rows.ndim - 2
        half = rows.shape[dim] // 2
        mine = lax.dynamic_slice_in_dim(rows, self.core * half, half, dim)
        other = self.sibling(lax.dynamic_slice_in_dim(rows, (1 - self.core) * half, half, dim))
        return jnp.where(self.core == 0, mine, other), jnp.where(self.core == 0, other, mine)

    def trade(self, array, outward, swapped):
        pairs = []
        for level in range(self.depth):
            for shard in range(self.shards):
                chip, core = divmod(shard, 2)
                side, odd = divmod(level, 2)
                slot = odd if not swapped else 1 - odd
                held = level * self.shards + shard
                worked = (2 * core + slot) * self.shards + 2 * chip + side
                pairs.append((held, worked) if outward else (worked, held))
        return lax.ppermute(array, ("ctx", "fsdp"), pairs)

    def to_slot(self, sends):
        return self.trade(sends[0], True, False), self.trade(sends[1], True, True)

    def both_halves(self, steps, trades):
        half = pair(steps, *trades)
        return half, self.sibling(half)

    def quarter_places(self):
        odd = self.level % 2
        near, far = 2 * self.core, 2 * (1 - self.core)
        return [near + odd, near + 1 - odd, far + odd, far + 1 - odd]

    def from_slot(self, quarters):
        return self.trade(quarters[0], False, False), self.trade(quarters[1], False, True)

    def received(self, trades):
        first, second = trades
        flip = self.level % 2 == 0
        return jnp.stack([jnp.where(flip, first, second), jnp.where(flip, second, first)])


def local(
    tokens,
    cotangent,
    sequence_lengths,
    slot_sequence,
    offset_bucket,
    first_gain,
    second_gain,
    query_weight,
    key_weight,
    value_weight,
    output_weight,
    expand_weight,
    contract_weight,
    bias_table,
    clip_limit,
):
    links = Links(bias_table.shape[0])
    core = links.core
    held_count, local_length, model_width = tokens.shape
    total_length = local_length * links.depth
    bucket_count, head_count = bias_table.shape
    inner_width = query_weight.shape[1]
    head_size = inner_width // head_count
    own_heads = head_count // 2
    own_inner = inner_width // 2
    slot_count = slot_sequence.shape[0]
    assert held_count == 2 and links.depth == 4

    slots = jnp.arange(slot_count)
    slot = links.chip * (2 * held_count) + links.level
    sequence = jnp.sum(jnp.where(slots == slot, slot_sequence, 0))
    length = jnp.sum(jnp.where(slots == sequence, sequence_lengths, 0)).astype(jnp.int32)
    odd = links.level % 2

    def numbers(*values):
        return jnp.stack([jnp.asarray(value, jnp.int32) for value in values])

    core_line = numbers(core)
    first_column = first_gain.astype(wide)[:, None]
    second_column = second_gain.astype(wide)[:, None]
    gains = jnp.concatenate([first_column, second_column], axis=1)
    attention_weights = (query_weight, key_weight, value_weight, output_weight)
    feed_weights = (expand_weight, contract_weight)
    steps = Steps()
    odd_line = odd.reshape(1)
    chips, square = links.chips, links.square
    order = links.order()
    places = numbers(*links.weight_places(), core, *order)
    order_line = numbers(*order)
    slot_places = numbers(*links.quarter_places(), length, *order)
    length_line = length.reshape(1)

    line_width = 2 * total_length
    falling = jnp.concatenate([jnp.flip(offset_bucket), jnp.full((1,), -1, jnp.int32)])
    matching = falling[:, None] == jnp.arange(bucket_count)[None, :]
    own_table = lax.dynamic_slice_in_dim(bias_table, core * own_heads, own_heads, 1)
    lines = dot(own_table, matching.astype(low), 0, 1)

    arrived = links.sibling(other_side(steps, core_line, attention_weights, feed_weights, gains))
    token_trades = links.to_slot(send_blocks(steps, odd_line, tokens))
    attention_pieces = links.gather(
        attention_shard(steps, core_line, attention_weights, gains, arrived)
    )
    strips = bias_strips(steps, lines.reshape(own_heads, 1, line_width))
    late_shard = hidden_shard(steps, core_line, 1, feed_weights, gains, arrived)
    steps.wait(*attention_pieces[1:3])
    token_halves = links.both_halves(steps, token_trades)
    token_low, normed_one, normed_one_t = token_rows_of(
        steps, slot_places, token_halves, True, chips, square
    )
    early_shard = hidden_shard(steps, core_line, 0, feed_weights, gains, arrived)
    early_pieces = links.gather(early_shard)
    cotangent_trades = links.to_slot(send_blocks(steps, odd_line, cotangent))
    qkv_width = 3 * own_inner
    qkv = rows_product(
        steps, places, [normed_one], attention_pieces, 0, qkv_width, False, "qkv_product"
    )
    pairs = own_inner // tile
    half_pairs = pairs // 2
    forward = functools.partial(attention_forward, steps, length_line, qkv, strips)
    first_context, first_totals, first_tops = forward(0, half_pairs)
    cotangent_halves = links.both_halves(steps, cotangent_trades)
    steps.wait(*early_pieces[1:3])
    last_context, last_totals, last_tops = forward(half_pairs, half_pairs)
    contexts = [first_context, last_context]
    steps.wait(early_pieces[-1])
    output_columns = (qkv_width, qkv_width + own_inner)
    attended = rows_product(
        steps, places, contexts, attention_pieces, *output_columns, True, "attended_product"
    )
    attended_other = links.sibling(attended)
    late_first = links.turn(late_shard, False)
    _, out_low, out_low_t = token_rows_of(
        steps, slot_places, cotangent_halves, False, chips, square
    )
    hidden_one, normed_two, normed_two_t = second_norm(
        steps, order_line, token_low, attended, attended_other, chips, square
    )
    late_pieces = links.gather_slowly(steps, late_shard, late_first)
    operands = (normed_two, normed_two_t, out_low, out_low_t)
    mixed_sum, normed_sum, *early_terms = feed_forward(steps, places, *operands, early_pieces)
    early = links.scatter(*early_terms)
    mixed_own, mixed_away, normed_two_part, *late_terms = feed_forward(
        steps, places, *operands, late_pieces, (mixed_sum, normed_sum)
    )
    normed_two_other = links.sibling(normed_two_part)
    mixed_other = links.sibling(mixed_away)
    late = links.scatter(*late_terms)
    early = links.scatter_near(steps, early)
    hidden_grad, attended_grad, attended_grad_t, context_grad = hidden_back(
        steps,
        places,
        normed_two_part,
        normed_two_other,
        hidden_one,
        out_low,
        attention_pieces,
        *output_columns,
        chips,
        square,
    )
    result_quarters = finish_half(
        steps, core, odd, length, mixed_own, mixed_other, hidden_one, token_low, False
    )
    result_trades = links.from_slot(result_quarters)

    def backward(pair):
        half = pair // half_pairs
        return attention_backward(
            steps,
            length_line,
            qkv,
            contexts[half],
            context_grad,
            (first_totals, last_totals)[half],
            strips,
            pair,
            half * half_pairs,
        )

    *grads_a, strips_a = backward(0)
    *grads_b, strips_b = backward(1)
    steps.wait(*result_trades)
    early = links.scatter_own(steps, early)
    late = links.scatter_near(steps, late)
    first = links.scatter(
        *attention_terms(steps, attended_grad_t, normed_one_t, contexts, grads_a + grads_b)
    )
    *grads_c, strips_c = backward(2)
    late = links.scatter_own(steps, late)
    *grads_d, strips_d = backward(3)
    early = links.level_across(steps, early)
    first = links.scatter_near(steps, first)
    last = links.scatter(
        *attention_terms(steps, attended_grad_t, normed_one_t, (), grads_c + grads_d)
    )
    own_part, away_part = input_product(
        steps, places, grads_a + grads_b + grads_c + grads_d, attention_pieces
    )
    away_other = links.sibling(away_part)
    first = links.scatter_own(steps, first)
    late = links.level_across(steps, late)
    last = links.scatter_near(steps, last)
    early = links.level_out(steps, early)
    last = links.scatter_own(steps, last)
    first = links.level_across(steps, first)
    input_quarters = finish_half(
        steps, core, odd, length, own_part, away_other, hidden_grad, token_low, True
    )
    input_trades = links.from_slot(input_quarters)
    steps.wait(early[1])
    late = links.level_out(steps, late)
    last = links.level_across(steps, last)
    result_pieces = links.gather(links.received(result_trades))
    first = links.level_out(steps, first)
    early_left, early_right = links.level_done(early)
    steps.wait(late[1], *input_trades)
    diagonals = jnp.concatenate(
        [diagonal_sums(steps, part) for part in (strips_a, strips_b, strips_c, strips_d)], axis=0
    ).reshape(own_heads, line_width)
    table_grad = lax.dot_general(
        diagonals,
        matching.astype(wide),
        (((1,), (0,)), ((), ())),
        precision=lax.Precision.HIGHEST,
        preferred_element_type=wide,
    )
    tops = jnp.concatenate([first_tops, last_tops], axis=0).reshape(own_heads, tile)
    small = jnp.concatenate([table_grad, tops[:, : tile - bucket_count]], axis=1)
    for small in links.small_hops(small):
        pass
    last = links.level_out(steps, last)
    late_left, late_right = links.level_done(late)
    first_left, first_right = links.level_done(first)
    last_left, last_right = links.level_done(last)
    input_gradient = links.received(input_trades).astype(wide)

    def slot_of(wanted):
        return jnp.sum(jnp.where(slot_sequence == wanted, slots, 0))

    own_slots = [slot_of(links.shard * held_count + row) for row in range(held_count)]
    other_slots = [slot_of((links.shard ^ 1) * held_count + row) for row in range(held_count)]
    piece_slots = [
        (2 * chip + core) * held_count + row
        for chip in order
        for row in range(held_count)
    ]
    picked, picked_other = pick_slots(
        steps,
        numbers(*own_slots, *other_slots, *piece_slots),
        result_pieces,
    )
    from_other = links.sibling(picked_other)
    output = jnp.stack(
        [
            jnp.where((s // held_count) % 2 == core, picked[row], from_other[row])
            for row, s in enumerate(own_slots)
        ]
    )

    def side_by_side(*parts):
        return jnp.concatenate(parts, axis=1).astype(wide)

    raw_two = side_by_side(early_left[0], late_left[0], early_right[0], late_right[0])
    contract_weight_gradient = side_by_side(
        early_left[1], late_left[1], early_right[1], late_right[1]
    )

    output_weight_gradient = side_by_side(first_left[:, :own_inner], first_right[:, :own_inner])

    def inner_columns(block):
        pieces = []
        for first_side, last_side in ((first_left, last_left), (first_right, last_right)):
            for start, side in ((own_inner, first_side), (0, last_side)):
                for pair in range(half_pairs):
                    first = start + (3 * pair + block) * tile
                    pieces.append(side[:, first : first + tile])
        return side_by_side(*pieces)

    raw_query, raw_key, raw_value = (inner_columns(block) for block in range(3))
    first_gain_gradient = jnp.sum(
        query_weight.astype(wide) * raw_query
        + key_weight.astype(wide) * raw_key
        + value_weight.astype(wide) * raw_value,
        axis=1,
    )
    second_gain_gradient = jnp.sum(expand_weight.astype(wide) * raw_two, axis=1)
    query_weight_gradient = first_column * raw_query
    key_weight_gradient = first_column * raw_key
    value_weight_gradient = first_column * raw_value
    expand_weight_gradient = second_column * raw_two

    small = links.in_order(small, links.sibling(small))
    table_rows = bucket_count // links.shards
    bias_table_gradient = lax.dynamic_slice_in_dim(
        small[:, :bucket_count].T, links.shard * table_rows, table_rows, 0
    )
    largest = small[:, bucket_count]
    shrink = clip_limit / jnp.maximum(clip_limit, largest)
    column_scale = jnp.repeat(jnp.sqrt(shrink), head_size)
    new_query_weight = query_weight.astype(wide) * column_scale[None, :]
    new_key_weight = key_weight.astype(wide) * column_scale[None, :]
    return (
        output,
        input_gradient,
        first_gain_gradient,
        second_gain_gradient,
        query_weight_gradient,
        key_weight_gradient,
        value_weight_gradient,
        output_weight_gradient,
        expand_weight_gradient,
        contract_weight_gradient,
        bias_table_gradient,
        largest,
        new_query_weight,
        new_key_weight,
    )


def solution(mesh):
    return jax.shard_map(
        local,
        mesh=mesh,
        in_specs=(
            P("fsdp", "ctx", None),
            P("fsdp", "ctx", None),
            P(),
            P(),
            P(),
            P("fsdp"),
            P("fsdp"),
            P("fsdp", None),
            P("fsdp", None),
            P("fsdp", None),
            P("fsdp", None),
            P("fsdp", None),
            P("fsdp", None),
            P(),
            P(),
        ),
        out_specs=(
            P("fsdp", "ctx", None),
            P("fsdp", "ctx", None),
            P("fsdp"),
            P("fsdp"),
            P("fsdp", None),
            P("fsdp", None),
            P("fsdp", None),
            P("fsdp", None),
            P("fsdp", None),
            P("fsdp", None),
            P("fsdp", None),
            P(),
            P("fsdp", None),
            P("fsdp", None),
        ),
        check_vma=False,
    )
```

```python
import functools
import math

import jax
import jax.numpy as jnp
from jax import lax
from jax.experimental import pallas as pl
from jax.experimental.pallas import tpu as pltpu
from jax.sharding import PartitionSpec as P

epsilon = 1e-06
masked = -1e30
tile = 128
half_tile = 64
wide = jnp.float32
low = jnp.bfloat16
anywhere = pl.BlockSpec(memory_space=pl.ANY)
in_vmem = pl.BlockSpec(memory_space=pltpu.VMEM)
in_hbm = pl.BlockSpec(memory_space=pltpu.HBM)


def pinned(array):
    return pltpu.with_memory_space_constraint(array, pltpu.HBM)


class Steps:
    def __init__(self):
        self.behind = ()

    def wait(self, *arrays):
        self.behind += arrays

    def launch(
        self,
        name,
        kernel,
        operands,
        in_specs,
        out_specs,
        out_shape,
        grid=(1,),
        prefetch=1,
        scratch=(),
        estimate=(0, 1 << 20),
        memory=24,
        stored=(),
    ):
        inputs, idle = len(operands), self.behind

        def run(*refs):
            refs = list(refs)
            mark_ref = refs.pop(inputs + len(idle) + len(out_specs))
            mark_ref[...] = jnp.zeros_like(mark_ref)
            kernel(*refs[:inputs], *refs[inputs + len(idle) :])

        out_specs, out_shape = list(out_specs), list(out_shape)
        outs = pl.pallas_call(
            run,
            grid_spec=pltpu.PrefetchScalarGridSpec(
                num_scalar_prefetch=prefetch,
                grid=grid,
                in_specs=list(in_specs) + [anywhere] * len(idle),
                out_specs=out_specs + [pl.BlockSpec((8, tile), lambda *_: (0, 0))],
                scratch_shapes=list(scratch),
            ),
            out_shape=[
                pltpu.HBM(shape, kind) if number in stored else jax.ShapeDtypeStruct(shape, kind)
                for number, (shape, kind) in enumerate(out_shape + [((8, tile), wide)])
            ],
            compiler_params=pltpu.CompilerParams(vmem_limit_bytes=memory << 20),
            cost_estimate=pl.CostEstimate(
                flops=int(estimate[0]), bytes_accessed=int(estimate[1]), transcendentals=0
            ),
            name=name,
        )(*operands, *idle)
        self.behind = (outs[-1],)
        return outs[:-1]


def dot(left, right, left_dim, right_dim):
    return lax.dot_general(
        left, right, (((left_dim,), (right_dim,)), ((), ())), preferred_element_type=wide
    )


def strip_kernel(line_ref, strip_ref):
    width = line_ref.shape[-1]
    rows = jnp.broadcast_to(line_ref[0], (tile, width))
    strip_ref[0] = pltpu.roll(rows, width - (tile - 1), 1, stride=1, stride_axis=0)


def bias_strips(steps, lines):
    heads, _, width = lines.shape
    return steps.launch(
        "bias_strips",
        strip_kernel,
        [lines],
        [pl.BlockSpec((1, 1, width), lambda h: (h, 0, 0))],
        [pl.BlockSpec((1, tile, width), lambda h: (h, 0, 0))],
        [((heads, tile, width), wide)],
        grid=(heads,),
        prefetch=0,
        memory=16,
        stored=(0,),
        estimate=(0, 8 << 20),
    )[0]


def diagonal_kernel(strip_ref, line_ref):
    strip = strip_ref[0]
    rows = tile
    while rows > 1:
        rows //= 2
        strip = pltpu.roll(strip[:rows], rows, 1) + strip[rows:]
    line_ref[0] = strip


def diagonal_sums(steps, strips):
    heads, _, width = strips.shape
    return steps.launch(
        "diagonal_sums",
        diagonal_kernel,
        [strips],
        [pl.BlockSpec((1, tile, width), lambda h: (h, 0, 0))],
        [pl.BlockSpec((1, 1, width), lambda h: (h, 0, 0))],
        [((heads, 1, width), wide)],
        grid=(heads,),
        prefetch=0,
        memory=16,
        estimate=(0, 2 << 20),
    )[0]


def one_head(block, head, extra=None):
    lane = lax.broadcasted_iota(jnp.int32, block.shape, 1)
    kept = jnp.where((lane >= half_tile) if head else (lane < half_tile), block, 0)
    if extra is None:
        return kept
    return jnp.where(lane == (0 if head else half_tile), extra, kept)


def key_masks(total, length):
    position = lax.broadcasted_iota(jnp.int32, (total, tile), 0)
    return jnp.where(position < length, 0.0, masked).astype(low)


def strip_columns(total, first, width):
    return [
        pl.ds(pl.multiple_of(total - tile - row + first, tile), width)
        for row in range(0, total, tile)
    ]


def add_bias(products, strip_ref, head, columns):
    return jnp.concatenate(
        [
            products[block * tile : (block + 1) * tile] + strip_ref[head, :, where]
            for block, where in enumerate(columns)
        ],
        axis=0,
    )


def forward_kernel(
    length_ref, query_ref, key_ref, value_ref, strip_ref, context_ref, total_ref, top_ref, *, step
):
    length = length_ref[0]
    total = query_ref.shape[0]
    masks = key_masks(total, length)
    ones = jnp.ones((step, tile), low)
    keys = [one_head(key_ref[...], head, masks) for head in (0, 1)]
    values = [one_head(value_ref[...], head).astype(wide).T.astype(low) for head in (0, 1)]

    def body(index, tops):
        first = pl.multiple_of(index * step, step)
        queries = query_ref[pl.ds(first, step), :]
        columns = strip_columns(total, first, step)
        query_okay = first + lax.broadcasted_iota(jnp.int32, (1, step), 1) < length
        context = None
        peaks = []
        for head in (0, 1):
            products = dot(keys[head], one_head(queries, head, ones), 1, 1)
            scores = add_bias(products, strip_ref, head, columns)
            row_max = jnp.max(scores, axis=0, keepdims=True)
            exponent = jnp.exp(scores - row_max)
            summed = jnp.sum(exponent, axis=0, keepdims=True)
            part = dot(values[head], exponent.astype(low), 1, 0) * (1.0 / summed)
            context = part if context is None else context + part
            total_ref[0, head : head + 1, pl.ds(first, step)] = row_max + jnp.log(summed)
            peaks.append(
                jnp.where(query_okay, jnp.max(products, axis=0, keepdims=True), masked)
            )
        context_ref[pl.ds(first, step), :] = context.T.astype(low)
        return tuple(jnp.maximum(top, peak) for top, peak in zip(tops, peaks))

    tops = lax.fori_loop(
        0, total // step, body, tuple(jnp.full((1, step), masked, wide) for _ in (0, 1))
    )
    for head in (0, 1):
        peak = jnp.max(tops[head], axis=1, keepdims=True)
        top_ref[0, head : head + 1, :] = jnp.broadcast_to(peak, (1, tile))


def attention_forward(steps, length, qkv, strips, start, count, step=512):
    total = qkv.shape[0]
    pairs = qkv.shape[1] // (3 * tile)
    strip_width = strips.shape[2]

    def columns(which):
        return pl.BlockSpec((total, tile), lambda p, _: (0, which * pairs + start + p))

    return steps.launch(
        "attention_forward",
        functools.partial(forward_kernel, step=step),
        [length, qkv, qkv, qkv, strips],
        [columns(which) for which in range(3)]
        + [pl.BlockSpec((2, tile, strip_width), lambda p, _: (start + p, 0, 0))],
        [
            pl.BlockSpec((total, tile), lambda p, _: (0, p)),
            pl.BlockSpec((1, 2, total), lambda p, _: (p, 0, 0)),
            pl.BlockSpec((1, 2, tile), lambda p, _: (p, 0, 0)),
        ],
        [((total, count * tile), low), ((count, 2, total), wide), ((count, 2, tile), wide)],
        grid=(count,),
        memory=32,
        estimate=(6e9 * count, (3 << 20) * count),
    )


def backward_kernel(
    length_ref,
    query_ref,
    key_ref,
    value_ref,
    context_ref,
    grad_ref,
    total_ref,
    strip_ref,
    query_grad_ref,
    key_grad_ref,
    value_grad_ref,
    strip_grad_ref,
    key_sum,
    value_sum,
    *,
    step,
):
    length = length_ref[0]
    total = query_ref.shape[0]
    masks = key_masks(total, length)
    ones = jnp.ones((step, tile), low)
    keys = [one_head(key_ref[...], head, masks) for head in (0, 1)]
    plain_keys = [one_head(key_ref[...], head) for head in (0, 1)]
    values = [one_head(value_ref[...], head) for head in (0, 1)]
    key_sum[...] = jnp.zeros_like(key_sum)
    value_sum[...] = jnp.zeros_like(value_sum)
    strip_grad_ref[...] = jnp.zeros_like(strip_grad_ref)

    def body(index, carry):
        first = pl.multiple_of(index * step, step)
        queries = query_ref[pl.ds(first, step), :]
        grads = grad_ref[pl.ds(first, step), :]
        columns = strip_columns(total, first, step)
        inner = grads.astype(wide) * context_ref[pl.ds(first, step), :].astype(wide)
        query_grad = None
        for head in (0, 1):
            head_grads = one_head(grads, head)
            pick = one_head(jnp.ones((8, tile), wide), head)
            row_inner = lax.dot_general(
                pick,
                inner,
                (((1,), (1,)), ((), ())),
                precision=lax.Precision.HIGHEST,
                preferred_element_type=wide,
            )[:1]
            log_total = total_ref[0, head : head + 1, pl.ds(first, step)]
            products = dot(keys[head], one_head(queries, head, ones), 1, 1)
            probs = jnp.exp(add_bias(products, strip_ref, head, columns) - log_total)
            value_sum[...] += dot(probs.astype(low), head_grads, 1, 0)
            score_grad = probs * (dot(values[head], head_grads, 1, 1) - row_inner)
            for block, where in enumerate(columns):
                strip_grad_ref[head, :, where] += score_grad[block * tile : (block + 1) * tile]
            score_low = score_grad.astype(low)
            key_sum[...] += dot(score_low, one_head(queries, head), 1, 0)
            part = dot(score_low, plain_keys[head], 0, 0)
            query_grad = part if query_grad is None else query_grad + part
        query_grad_ref[pl.ds(first, step), :] = query_grad.astype(low)
        return carry

    lax.fori_loop(0, total // step, body, 0)
    key_grad_ref[...] = key_sum[...].astype(low)
    value_grad_ref[...] = value_sum[...].astype(low)


def attention_backward(
    steps, length, qkv, context, context_grad, log_totals, strips, start, held, step=256
):
    total = qkv.shape[0]
    pairs = qkv.shape[1] // (3 * tile)
    strip_width = strips.shape[2]

    def columns(which, first=start):
        return pl.BlockSpec((total, tile), lambda p, _: (0, which * pairs + first + p))

    part = pl.BlockSpec((total, tile), lambda p, _: (0, p))
    return steps.launch(
        "attention_backward",
        functools.partial(backward_kernel, step=step),
        [length, qkv, qkv, qkv, context, context_grad, log_totals, pinned(strips)],
        [
            columns(0),
            columns(1),
            columns(2),
            columns(0, start - held),
            columns(0),
            pl.BlockSpec((1, 2, total), lambda p, _: (start - held + p, 0, 0)),
            pl.BlockSpec((2, tile, strip_width), lambda p, _: (start + p, 0, 0)),
        ],
        [part, part, part, pl.BlockSpec((2, tile, strip_width), lambda p, _: (p, 0, 0))],
        [((total, tile), low)] * 3 + [((2, tile, strip_width), wide)],
        scratch=[pltpu.VMEM((total, tile), wide)] * 2,
        memory=32,
        stored=(3,),
        estimate=(1e10, 6 << 20),
    )


def gelu_and_slope(values):
    distance = jnp.abs(values) * math.sqrt(0.5)
    ratio = 1.0 / (1.0 + 0.3275911 * distance)
    density = jnp.exp(-distance * distance)
    poly = 1.061405429 * ratio - 1.453152027
    poly = poly * ratio + 1.421413741
    poly = poly * ratio - 0.284496736
    poly = poly * ratio + 0.254829592
    tail = (0.5 * ratio) * poly * density
    cumulative = jnp.where(values >= 0, 1.0 - tail, tail)
    slope = cumulative + values * density * (1.0 / math.sqrt(2.0 * math.pi))
    return values * cumulative, slope


def beside(refs):
    return jnp.concatenate([ref[...] for ref in refs], axis=1)


def start_copies(index_ref, pieces, target, semaphores, columns=None):
    copies = []
    for number, piece in enumerate(pieces):
        for side in (0, 1):
            entry = 2 * number + side
            rows = piece.shape[-2]
            where = pl.ds(pl.multiple_of(index_ref[entry] * rows, rows), rows)
            if columns is not None:
                source, place = piece.at[side, :, columns], target.at[where, :]
            else:
                source, place = piece.at[side], target.at[:, where, :]
            copies.append(pltpu.make_async_copy(source, place, semaphores.at[entry]))
    for copy in copies:
        copy.start()
    return copies


def transposed_rows(order_ref, source_ref, target_ref, columns, chips, ordered):
    share = source_ref.shape[1] // chips
    for block in range(chips):
        if ordered:
            first = pl.multiple_of(order_ref[block] * share, share)
            part = source_ref[:, pl.ds(first, share)]
        else:
            part = source_ref[:, block * share : (block + 1) * share]
        target_ref[block * share : (block + 1) * share, columns] = part.T.astype(low)


def send_kernel(odd_ref, block_ref, first_ref, second_ref):
    @pl.when(pl.program_id(0) == 0)
    def _():
        first_ref[...] = block_ref[0]

    @pl.when(pl.program_id(0) == 1)
    def _():
        second_ref[...] = block_ref[0]


def send_blocks(steps, odd, blocks):
    shape = blocks.shape[1:]
    out = pl.BlockSpec(shape, lambda i, _: (0, 0))
    return steps.launch(
        "send_blocks",
        send_kernel,
        [odd, pinned(blocks)],
        [pl.BlockSpec((1,) + shape, lambda i, odd_ref: ((odd_ref[0] + i) % 2, 0, 0))],
        [out, out],
        [(shape, low)] * 2,
        grid=(2,),
        memory=8,
        estimate=(0, 2 << 20),
    )


def scaled(block, gain):
    return (gain * block.astype(wide)).astype(low)


def column_copies(core, weights, targets, semaphores, first=0, parts=1, part=0):
    copies = []
    for number, (weight, target) in enumerate(zip(weights, targets)):
        width = weight.shape[1] // (2 * parts)
        columns = pl.ds(pl.multiple_of((parts * core + part) * width, width), width)
        copies.append(
            pltpu.make_async_copy(weight.at[:, columns], target, semaphores.at[first + number])
        )
    return copies


def run_copies(copies):
    for copy in copies:
        copy.start()
    for copy in copies:
        copy.wait()


def side_kernel(core_ref, *refs):
    attention, feed = refs[:4], refs[4:6]
    gain_ref, out_ref, semaphores = refs[6:]
    core = 1 - core_ref[0]
    inner = attention[0].shape[1] // 2
    hidden = feed[0].shape[1] // 4
    targets = [out_ref.at[:, n * inner : (n + 1) * inner] for n in range(4)]
    copies = column_copies(core, attention, targets, semaphores)
    first = 4 * inner
    for part in (0, 1):
        start = first + 2 * part * hidden
        targets = [out_ref.at[:, start + n * hidden : start + (n + 1) * hidden] for n in (0, 1)]
        copies += column_copies(core, feed, targets, semaphores, 4 + 2 * part, 2, part)
    run_copies(copies)
    out_ref[:, : 3 * inner] = scaled(out_ref[:, : 3 * inner], gain_ref[:, :1])
    for part in (0, 1):
        columns = slice(first + 2 * part * hidden, first + (2 * part + 1) * hidden)
        out_ref[:, columns] = scaled(out_ref[:, columns], gain_ref[:, 1:])


def relay_kernel(first_ref, second_ref, first_out_ref, second_out_ref):
    first_out_ref[...] = first_ref[...]
    second_out_ref[...] = second_ref[...]


def relay(steps, first, second):
    block = pl.BlockSpec((1,) + first.shape[1:], lambda i: (i,) + (0,) * (first.ndim - 1))
    return steps.launch(
        "relay",
        relay_kernel,
        [first, second],
        [block, block],
        [block, block],
        [(first.shape, low)] * 2,
        grid=(first.shape[0],),
        prefetch=0,
        memory=8,
    )


def pair_kernel(first_ref, second_ref, out_ref):
    out_ref[0] = first_ref[...]
    out_ref[1] = second_ref[...]


def pair(steps, first, second):
    rows, width = first.shape
    step = rows // 2
    block = pl.BlockSpec((step, width), lambda i: (i, 0))
    return steps.launch(
        "pair",
        pair_kernel,
        [first, second],
        [block] * 2,
        [pl.BlockSpec((2, step, width), lambda i: (0, i, 0))],
        [((2, rows, width), low)],
        grid=(2,),
        prefetch=0,
        memory=8,
    )[0]


def other_side(steps, core, attention, feed, gains):
    rows = attention[0].shape[0]
    columns = sum(weight.shape[1] for weight in attention + feed) // 2
    return steps.launch(
        "other_side",
        side_kernel,
        [core, *map(pinned, (*attention, *feed)), gains],
        [in_hbm] * 6 + [in_vmem],
        [in_vmem],
        [((rows, columns), low)],
        scratch=[pltpu.SemaphoreType.DMA((8,))],
        memory=8,
    )[0]


def attention_shard_kernel(core_ref, *refs):
    attention = refs[:4]
    gain_ref, arrived_ref, out_ref, semaphores = refs[4:]
    inner = attention[0].shape[1] // 2
    targets = [out_ref.at[0, :, n * inner : (n + 1) * inner] for n in range(4)]
    copies = column_copies(core_ref[0], attention, targets, semaphores)
    source = arrived_ref.at[:, : 4 * inner]
    copies.append(pltpu.make_async_copy(source, out_ref.at[1], semaphores.at[4]))
    run_copies(copies)
    out_ref[0, :, : 3 * inner] = scaled(out_ref[0, :, : 3 * inner], gain_ref[:, :1])


def attention_shard(steps, core, weights, gains, arrived):
    rows = weights[0].shape[0]
    columns = sum(weight.shape[1] for weight in weights) // 2
    return steps.launch(
        "attention_shard",
        attention_shard_kernel,
        [core, *map(pinned, weights), gains, pinned(arrived)],
        [in_hbm] * 4 + [in_vmem, anywhere],
        [in_vmem],
        [((2, rows, columns), low)],
        scratch=[pltpu.SemaphoreType.DMA((5,))],
        memory=8,
    )[0]


def hidden_shard_kernel(core_ref, *refs, part):
    feed = refs[:2]
    gain_ref, arrived_ref, out_ref, semaphores = refs[2:]
    hidden = out_ref.shape[3]
    targets = [out_ref.at[0, number] for number in (0, 1)]
    copies = column_copies(core_ref[0], feed, targets, semaphores, 0, 2, part)
    for number in (0, 1):
        start = 2 * hidden * (1 + part) + number * hidden
        source = arrived_ref.at[:, start : start + hidden]
        copies.append(
            pltpu.make_async_copy(source, out_ref.at[1, number], semaphores.at[2 + number])
        )
    run_copies(copies)
    out_ref[0, 0] = scaled(out_ref[0, 0], gain_ref[:, 1:])


def hidden_shard(steps, core, part, weights, gains, arrived):
    rows, columns = weights[0].shape
    return steps.launch(
        "hidden_shard",
        functools.partial(hidden_shard_kernel, part=part),
        [core, *map(pinned, weights), gains, pinned(arrived)],
        [in_hbm] * 2 + [in_vmem, anywhere],
        [in_vmem],
        [((2, 2, rows, columns // 4), low)],
        scratch=[pltpu.SemaphoreType.DMA((4,))],
        memory=8,
    )[0]


def token_kernel(place_ref, *refs, normed, chips, ordered):
    halves = refs[:2]
    plain_ref, first_ref, first_t_ref, semaphores = refs[-4:]
    total = plain_ref.shape[0]
    step = total // 4
    copies = []
    for number in range(4):
        where = pl.ds(pl.multiple_of(place_ref[number] * step, step), step)
        source = halves[number // 2].at[number % 2]
        copies.append(
            pltpu.make_async_copy(source, plain_ref.at[where, :], semaphores.at[number])
        )
    for copy in copies:
        copy.start()
    for copy in copies:
        copy.wait()
    for block in range(4):
        rows = slice(block * step, (block + 1) * step)
        values = plain_ref[rows, :].astype(wide)
        if normed:
            values = normalize(values)[0]
        else:
            position = block * step + lax.broadcasted_iota(jnp.int32, values.shape, 0)
            values = jnp.where(position < place_ref[4], values, 0.0)
        first_ref[rows, :] = values.astype(low)
        transposed_rows(
            place_ref.at[pl.ds(5, chips)],
            first_ref.at[rows, :],
            first_t_ref,
            rows,
            chips,
            ordered,
        )


def token_rows_of(steps, places, pieces, normed, chips, ordered):
    total, width = 4 * pieces[0].shape[1], pieces[0].shape[2]
    return steps.launch(
        "token_rows" if normed else "cotangent_rows",
        functools.partial(token_kernel, normed=normed, chips=chips, ordered=ordered),
        [places, *(map(pinned, pieces) if normed else pieces)],
        [anywhere] * 2,
        [in_vmem] * 3,
        [((total, width), low), ((total, width), low), ((width, total), low)],
        scratch=[pltpu.SemaphoreType.DMA((4,))],
        memory=24,
        stored=() if normed else (1, 2),
        estimate=(0, 10 << 20),
    )


def rows_product_kernel(place_ref, *refs, factors, count, columns, across):
    rows = refs[:factors]
    pieces = refs[factors : factors + count]
    out_ref, weight, semaphores = refs[factors + count :]

    @pl.when(pl.program_id(0) == 0)
    def _():
        for copy in start_copies(place_ref, pieces, weight, semaphores, columns):
            copy.wait()

    operand = beside(rows)
    out_ref[...] = dot(operand, weight[...], 1, 1 if across else 0).astype(low)


def rows_product(steps, places, rows, pieces, first, last, across, name, step=256):
    total, depth = rows[0].shape
    count = len(pieces)
    whole = (2 * count * pieces[0].shape[1], last - first)
    width = whole[0] if across else whole[1]
    return steps.launch(
        name,
        functools.partial(
            rows_product_kernel,
            factors=len(rows),
            count=count,
            columns=pl.ds(first, last - first),
            across=across,
        ),
        [places, *rows, *pieces],
        [pl.BlockSpec((step, depth), lambda i, _: (i, 0))] * len(rows) + [anywhere] * count,
        [pl.BlockSpec((step, width), lambda i, _: (i, 0))],
        [((total, width), low)],
        grid=(total // step,),
        scratch=[pltpu.VMEM(whole, low), pltpu.SemaphoreType.DMA((2 * count,))],
        estimate=(2 * total * whole[0] * whole[1], 8 << 20),
    )[0]


def second_norm_kernel(
    order_ref, token_ref, mine_ref, other_ref, hidden_ref, normed_ref, normed_t_ref, *, chips, ordered
):
    attended = mine_ref[...].astype(wide) + other_ref[...].astype(wide)
    hidden = token_ref[...].astype(wide) + attended
    hidden_ref[...] = hidden
    normed_ref[...] = normalize(hidden)[0].astype(low)
    transposed_rows(order_ref, normed_ref, normed_t_ref, slice(None), chips, ordered)


def second_norm(steps, order, tokens, mine, other, chips, ordered, step=256):
    total, width = tokens.shape
    block = pl.BlockSpec((step, width), lambda i, _: (i, 0))
    return steps.launch(
        "second_norm",
        functools.partial(second_norm_kernel, chips=chips, ordered=ordered),
        [order, tokens, mine, other],
        [block] * 3,
        [block, block, pl.BlockSpec((width, step), lambda i, _: (0, i))],
        [((total, width), wide), ((total, width), low), ((width, total), low)],
        grid=(total // step,),
        stored=(0, 1, 2),
        estimate=(0, 14 << 20),
    )


def feed_forward_kernel(
    place_ref, normed_ref, normed_t_ref, grad_ref, grad_t_ref, *refs, count, first
):
    pieces = refs[:count]
    refs = refs[count:]
    if first:
        mixed_sum, normed_sum, keep_ref, send_ref, weight, semaphores = refs
        before = ()
    else:
        before = refs[:2]
        own_ref, other_ref, normed_grad_ref, keep_ref, send_ref = refs[2:7]
        weight, semaphores, mixed_sum, normed_sum = refs[7:]
    index = pl.program_id(0)
    step = keep_ref.shape[2]
    half = keep_ref.shape[1]
    carried = [
        pltpu.make_async_copy(source, target, semaphores.at[2 * count + number])
        for number, (source, target) in enumerate(zip(before, (mixed_sum, normed_sum)))
    ]

    @pl.when(index == 0)
    def _():
        copies = start_copies(place_ref, pieces, weight, semaphores)
        for copy in carried:
            copy.start()
        for copy in copies:
            copy.wait()

    columns = pl.ds(pl.multiple_of(index * step, step), step)
    expand = weight[0, :, columns]
    contract = weight[1, :, columns]
    pre_act = dot(normed_ref[...], expand, 1, 0)
    act_grad = dot(grad_ref[...], contract, 1, 0).astype(low).astype(wide)
    activated, slope = gelu_and_slope(pre_act)
    activated = activated.astype(low)
    pre_grad = (act_grad * slope).astype(low)
    for part, (rows_ref, values) in enumerate(
        ((normed_t_ref, pre_grad), (grad_t_ref, activated))
    ):
        keep_ref[part] = dot(rows_ref[:half, :], values, 1, 0).astype(low)
        send_ref[part] = dot(rows_ref[half:, :], values, 1, 0).astype(low)
    mixed = dot(activated, contract, 1, 1)
    normed_grad = dot(pre_grad, expand, 1, 1)
    if first:

        @pl.when(index == 0)
        def _():
            mixed_sum[...] = mixed
            normed_sum[...] = normed_grad

        @pl.when(index > 0)
        def _():
            mixed_sum[...] += mixed
            normed_sum[...] += normed_grad

    else:

        @pl.when(index == 0)
        def _():
            for copy in carried:
                copy.wait()

        mixed_sum[...] += mixed
        normed_sum[...] += normed_grad

        @pl.when(index == pl.num_programs(0) - 1)
        def _():
            rows = own_ref.shape[0]
            core = place_ref[2 * count]
            own = pl.multiple_of(core * rows, rows)
            away = pl.multiple_of((1 - core) * rows, rows)
            own_ref[...] = mixed_sum[pl.ds(own, rows), :].astype(low)
            other_ref[...] = mixed_sum[pl.ds(away, rows), :].astype(low)
            normed_grad_ref[...] = normed_sum[...].astype(low)


def feed_forward(steps, places, normed, normed_t, grad, grad_t, pieces, before=None, step=1024):
    rows, width = normed.shape
    count = len(pieces)
    hidden = pieces[0].shape[3]
    first = before is None

    def fixed(shape):
        return pl.BlockSpec(shape, lambda i, _: (0,) * len(shape), pipeline_mode=pl.Buffered(1))

    whole = fixed((rows, width))
    scratch = [
        pltpu.VMEM((2, width, hidden), low),
        pltpu.SemaphoreType.DMA((2 * count + 2,)),
    ]
    if first:
        before = ()
        out_specs = [whole, whole]
        out_shape = [((rows, width), wide)] * 2
    else:
        part = fixed((rows // 2, width))
        out_specs = [part, part, whole]
        out_shape = [((rows // 2, width), low)] * 2 + [((rows, width), low)]
        scratch += [pltpu.VMEM((rows, width), wide)] * 2
    return steps.launch(
        "feed_forward",
        functools.partial(feed_forward_kernel, count=count, first=first),
        [places, *map(pinned, (normed, normed_t, grad, grad_t)), *pieces, *before],
        [whole, fixed((width, rows))] * 2 + [anywhere] * (count + len(before)),
        out_specs + [pl.BlockSpec((2, width // 2, step), lambda i, _: (0, 0, i))] * 2,
        out_shape + [((2, width // 2, hidden), low)] * 2,
        grid=(hidden // step,),
        scratch=scratch,
        memory=58,
        stored=(0, 1) if first else (),
        estimate=(20 * rows * width * hidden, 40 << 20),
    )


def hidden_back_kernel(
    place_ref, mine_ref, other_ref, hidden_ref, grad_ref, *refs, count, columns, chips, ordered
):
    pieces = refs[:count]
    hidden_grad_ref, low_ref, low_t_ref, context_grad_ref, weight, semaphores = refs[count:]

    @pl.when(pl.program_id(0) == 0)
    def _():
        for copy in start_copies(place_ref, pieces, weight, semaphores, columns):
            copy.wait()

    upstream = mine_ref[...].astype(wide) + other_ref[...].astype(wide)
    hidden = hidden_ref[...]
    scale = normalize(hidden)[1]
    hidden_grad = grad_ref[...].astype(wide) + normalize_back(hidden, scale, upstream)
    hidden_grad_ref[...] = hidden_grad
    low_ref[...] = hidden_grad.astype(low)
    context_grad_ref[...] = dot(low_ref[...], weight[...], 1, 0).astype(low)
    order_ref = place_ref.at[pl.ds(2 * count + 1, chips)]
    transposed_rows(order_ref, low_ref, low_t_ref, slice(None), chips, ordered)


def hidden_back(
    steps, places, mine, other, hidden, grad, pieces, first, last, chips, ordered, step=256
):
    total, width = hidden.shape
    count = len(pieces)
    inner = last - first
    block = pl.BlockSpec((step, width), lambda i, _: (i, 0))
    return steps.launch(
        "hidden_back",
        functools.partial(
            hidden_back_kernel,
            count=count,
            columns=pl.ds(first, inner),
            chips=chips,
            ordered=ordered,
        ),
        [places, mine, other, pinned(hidden), pinned(grad), *pieces],
        [block] * 4 + [anywhere] * count,
        [
            block,
            block,
            pl.BlockSpec((width, step), lambda i, _: (0, i)),
            pl.BlockSpec((step, inner), lambda i, _: (i, 0)),
        ],
        [((total, width), wide), ((total, width), low), ((width, total), low), ((total, inner), low)],
        grid=(total // step,),
        scratch=[pltpu.VMEM((width, inner), low), pltpu.SemaphoreType.DMA((2 * count,))],
        estimate=(4 * total * width * inner, 24 << 20),
    )


def terms_kernel(*refs, contexts):
    grad_t_ref, normed_t_ref = refs[:2]
    factors = refs[2:-2]
    for number, target in enumerate(refs[-2:]):

        @pl.when(pl.program_id(0) == number)
        def _():
            first = 0
            if contexts:
                part = dot(grad_t_ref[...], beside(factors[:contexts]), 1, 0)
                first = part.shape[1]
                target[:, :first] = part.astype(low)
            part = dot(normed_t_ref[...], beside(factors[contexts:]), 1, 0)
            target[:, first:] = part.astype(low)


def attention_terms(steps, grad_t, normed_t, contexts, grads):
    width, total = normed_t.shape
    factors = list(contexts) + list(grads)
    columns = sum(factor.shape[1] for factor in factors)
    block = pl.BlockSpec((width // 2, total), lambda i: (i, 0))
    fixed = pl.BlockSpec((width // 2, columns), lambda i: (0, 0))
    return steps.launch(
        "attention_terms",
        functools.partial(terms_kernel, contexts=len(contexts)),
        [grad_t, normed_t, *factors],
        [block, block]
        + [
            pl.BlockSpec(factor.shape, lambda i: (0, 0), pipeline_mode=pl.Buffered(1))
            for factor in factors
        ],
        [fixed, fixed],
        [((width // 2, columns), low)] * 2,
        grid=(2,),
        prefetch=0,
        estimate=(2 * total * width * columns, 10 << 20),
    )


def sum_kernel(*refs):
    total = refs[0][...].astype(wide)
    for ref in refs[1:-1]:
        total += ref[...].astype(wide)
    refs[-1][...] = total.astype(low)


def row_sums(steps, parts):
    first = parts[0]
    rows = first[0].shape[-2] // (1 if first[1] is None else 2)
    shape = first[0].shape[:-2] + (rows, first[0].shape[-1])
    count = 2
    block = shape[:-2] + (rows // count, shape[-1])
    leading = (0,) * (len(shape) - 2)

    def spec(offset):
        return pl.BlockSpec(block, lambda i: leading + (i + offset, 0))

    return steps.launch(
        "row_sums",
        sum_kernel,
        [part for part, _ in parts],
        [spec(count if which else 0) for _, which in parts],
        [spec(0)],
        [(shape, low)],
        grid=(count,),
        prefetch=0,
        memory=12,
        estimate=(0, 4 << 20),
    )[0]


def input_product_kernel(place_ref, *refs, count, factors):
    grads = refs[:factors]
    pieces = refs[factors : factors + count]
    own_ref, other_ref, weight, semaphores = refs[factors + count :]
    index = pl.program_id(0)

    @pl.when(index == 0)
    def _():
        columns = pl.ds(0, weight.shape[1])
        for copy in start_copies(place_ref, pieces, weight, semaphores, columns):
            copy.wait()

    ordered = [ref for block in range(3) for ref in grads[block::3]]
    product = dot(beside(ordered), weight[...], 1, 1)

    @pl.when(index < 2)
    def _():
        other_ref[...] = product.astype(low)

    @pl.when(index >= 2)
    def _():
        own_ref[...] = product


def input_product(steps, places, grads, pieces):
    total = grads[0].shape[0]
    count = len(pieces)
    inner = sum(grad.shape[1] for grad in grads)
    width = 2 * count * pieces[0].shape[1]
    step = total // 4

    def rows(i, place_ref):
        core = place_ref[2 * count]
        return (jnp.where(i < 2, 2 * (1 - core) + i, 2 * core + i - 2), 0)

    return steps.launch(
        "input_product",
        functools.partial(input_product_kernel, count=count, factors=len(grads)),
        [places, *grads, *pieces],
        [pl.BlockSpec((step, grad.shape[1]), rows) for grad in grads] + [anywhere] * count,
        [
            pl.BlockSpec((step, width), lambda i, _: (jnp.maximum(i - 2, 0), 0)),
            pl.BlockSpec((step, width), lambda i, _: (jnp.minimum(i, 1), 0)),
        ],
        [((total // 2, width), wide), ((total // 2, width), low)],
        grid=(4,),
        scratch=[pltpu.VMEM((width, inner), low), pltpu.SemaphoreType.DMA((2 * count,))],
        memory=24,
        estimate=(2 * total * width * inner, 14 << 20),
    )


def finish_kernel(
    place_ref, own_ref, other_ref, base_ref, token_ref, first_ref, second_ref, *, back
):
    index = pl.program_id(0)
    summed = own_ref[...].astype(wide) + other_ref[...].astype(wide)
    if back:
        tokens = token_ref[...].astype(wide)
        values = base_ref[...] + normalize_back(tokens, normalize(tokens)[1], summed)
    else:
        row = (2 * place_ref[0] + index) * summed.shape[0]
        position = row + lax.broadcasted_iota(jnp.int32, summed.shape, 0)
        values = jnp.where(position < place_ref[2], base_ref[...] + summed, 0.0)
    values = values.astype(low)

    @pl.when(index == place_ref[1])
    def _():
        first_ref[...] = values

    @pl.when(index != place_ref[1])
    def _():
        second_ref[...] = values


def finish_half(steps, core, odd, length, own, other, base, tokens, back):
    rows, width = own.shape
    step = rows // 2
    half = pl.BlockSpec((step, width), lambda i, _: (i, 0))
    whole = pl.BlockSpec((step, width), lambda i, place_ref: (2 * place_ref[0] + i, 0))
    quarter = pl.BlockSpec((step, width), lambda i, _: (0, 0))
    return steps.launch(
        "input_gradient_rows" if back else "result_rows",
        functools.partial(finish_kernel, back=back),
        [
            jnp.stack([core, odd, length]).astype(jnp.int32),
            pinned(own) if back else own,
            other,
            pinned(base) if back else base,
            tokens,
        ],
        [half, half, whole, whole],
        [quarter, quarter],
        [((step, width), low)] * 2,
        grid=(2,),
        memory=12,
        estimate=(0, 6 << 20),
    )


def pick_kernel(slot_ref, *refs, count):
    pieces = refs[:count]
    own_ref, other_ref, semaphores = refs[count:]
    for row in range(4):
        target = (own_ref if row < 2 else other_ref).at[row % 2]
        for number in range(2 * count):

            @pl.when(slot_ref[row] == slot_ref[4 + number])
            def _():
                source = pieces[number // 2].at[number % 2]
                copy = pltpu.make_async_copy(source, target, semaphores.at[row])
                copy.start()
                copy.wait()


def pick_slots(steps, slots, pieces):
    count = len(pieces)
    return steps.launch(
        "pick_slots",
        functools.partial(pick_kernel, count=count),
        [slots, *pieces],
        [anywhere] * count,
        [in_vmem] * 2,
        [(pieces[0].shape, low)] * 2,
        scratch=[pltpu.SemaphoreType.DMA((4,))],
        memory=8,
        estimate=(0, 4 << 20),
    )


def normalize(values):
    scaled = lax.rsqrt(jnp.mean(values * values, axis=-1, keepdims=True) + epsilon)
    return (values * scaled, scaled)


def normalize_back(values, scaled, upstream):
    unit_rows = values * scaled
    return scaled * (upstream - unit_rows * jnp.mean(upstream * unit_rows, axis=-1, keepdims=True))


class Links:
    def __init__(self, buckets):
        self.buckets = buckets
        self.shards = lax.axis_size("fsdp")
        self.depth = lax.axis_size("ctx")
        self.shard = lax.axis_index("fsdp")
        self.level = lax.axis_index("ctx")
        self.chips = self.shards // 2
        self.chip = self.shard // 2
        self.core = self.shard % 2
        self.groups = [list(range(core, self.shards, 2)) for core in (0, 1)]
        self.square = self.chips == 4

    def sibling(self, array):
        return lax.ppermute(array, "fsdp", [(i, i ^ 1) for i in range(self.shards)])

    def across(self, array, bit):
        return lax.ppermute(array, "fsdp", [(i, i ^ (2 * bit)) for i in range(self.shards)])

    def in_order(self, mine, other):
        return jnp.concatenate(
            [jnp.where(self.core == 0, mine, other), jnp.where(self.core == 0, other, mine)], axis=0
        )

    def turn(self, array, second):
        pairs = [(i, i ^ (2 if (i % 2 == 0) != second else 4)) for i in range(self.shards)]
        return lax.ppermute(array, "fsdp", pairs)

    def order(self):
        if not self.square:
            return list(range(self.chips))
        return [self.chip, self.chip ^ (1 + self.core), self.chip ^ (2 - self.core), self.chip ^ 3]

    def gather_whole(self, shard):
        whole = lax.all_gather(shard, "fsdp", axis=0, axis_index_groups=self.groups)
        return [whole[chip] for chip in range(self.chips)]

    def gather(self, shard):
        if not self.square:
            return self.gather_whole(shard)
        first = self.turn(shard, False)
        return [shard, first, self.turn(shard, True), self.turn(first, True)]

    def gather_slowly(self, steps, shard, first):
        if not self.square:
            return self.gather_whole(shard)
        arrived, own = relay(steps, first, shard)
        return [shard, first, self.turn(own, True), self.turn(arrived, True)]

    def weight_places(self):
        return [2 * chip + side for chip in self.order() for side in (self.core, 1 - self.core)]

    def scatter(self, keep, send):
        dim = keep.ndim - 2
        if not self.square:
            summed = lax.psum_scatter(
                jnp.concatenate([keep, send], axis=dim),
                "fsdp",
                scatter_dimension=dim,
                tiled=True,
                axis_index_groups=self.groups,
            )
            return keep, summed.astype(low)
        return keep, self.turn(send, True)

    def scatter_near(self, steps, terms):
        keep, arrived = terms
        if not self.square:
            return keep, arrived, None
        near = row_sums(steps, [(keep, True), (arrived, True)])
        return keep, arrived, self.turn(near, False)

    def scatter_own(self, steps, terms):
        keep, arrived, last = terms
        total = arrived
        if self.square:
            total = row_sums(steps, [(keep, False), (arrived, False), (last, None)])
        return total, lax.ppermute(total, "ctx", [(0, 1), (3, 2)])

    def small_hops(self, small):
        hops = []
        bit = 1
        while bit < self.chips:
            hops.append(("fsdp", [(i, i ^ (2 * bit)) for i in range(self.shards)]))
            bit *= 2
        bit = 1
        while bit < self.depth:
            hops.append(("ctx", [(i, i ^ bit) for i in range(self.depth)]))
            bit *= 2
        for axis, pairs in hops:
            other = lax.ppermute(small, axis, pairs)
            lane = lax.broadcasted_iota(jnp.int32, small.shape, 1)
            small = jnp.where(lane < self.buckets, small + other, jnp.maximum(small, other))
            yield small

    def level_across(self, steps, terms):
        joined = row_sums(steps, [(part, None) for part in terms])
        return joined, lax.ppermute(joined, "ctx", [(1, 2), (2, 1)])

    def level_out(self, steps, terms):
        total = row_sums(steps, [(part, None) for part in terms])
        return total, lax.ppermute(total, "ctx", [(1, 0), (2, 3)])

    def level_done(self, terms):
        total, outward = terms
        inner = (self.level == 1) | (self.level == 2)
        return self.exchange_rows(jnp.where(inner, total, outward))

    def exchange_rows(self, rows):
        dim = rows.ndim - 2
        half = rows.shape[dim] // 2
        mine = lax.dynamic_slice_in_dim(rows, self.core * half, half, dim)
        other = self.sibling(lax.dynamic_slice_in_dim(rows, (1 - self.core) * half, half, dim))
        return jnp.where(self.core == 0, mine, other), jnp.where(self.core == 0, other, mine)

    def trade(self, array, outward, swapped):
        pairs = []
        for level in range(self.depth):
            for shard in range(self.shards):
                chip, core = divmod(shard, 2)
                side, odd = divmod(level, 2)
                slot = odd if not swapped else 1 - odd
                held = level * self.shards + shard
                worked = (2 * core + slot) * self.shards + 2 * chip + side
                pairs.append((held, worked) if outward else (worked, held))
        return lax.ppermute(array, ("ctx", "fsdp"), pairs)

    def to_slot(self, sends):
        return self.trade(sends[0], True, False), self.trade(sends[1], True, True)

    def both_halves(self, steps, trades):
        half = pair(steps, *trades)
        return half, self.sibling(half)

    def quarter_places(self):
        odd = self.level % 2
        near, far = 2 * self.core, 2 * (1 - self.core)
        return [near + odd, near + 1 - odd, far + odd, far + 1 - odd]

    def from_slot(self, quarters):
        return self.trade(quarters[0], False, False), self.trade(quarters[1], False, True)

    def received(self, trades):
        first, second = trades
        flip = self.level % 2 == 0
        return jnp.stack([jnp.where(flip, first, second), jnp.where(flip, second, first)])


def local(
    tokens,
    cotangent,
    sequence_lengths,
    slot_sequence,
    offset_bucket,
    first_gain,
    second_gain,
    query_weight,
    key_weight,
    value_weight,
    output_weight,
    expand_weight,
    contract_weight,
    bias_table,
    clip_limit,
):
    links = Links(bias_table.shape[0])
    core = links.core
    held_count, local_length, model_width = tokens.shape
    total_length = local_length * links.depth
    bucket_count, head_count = bias_table.shape
    inner_width = query_weight.shape[1]
    head_size = inner_width // head_count
    own_heads = head_count // 2
    own_inner = inner_width // 2
    slot_count = slot_sequence.shape[0]
    assert held_count == 2 and links.depth == 4

    slots = jnp.arange(slot_count)
    slot = links.chip * (2 * held_count) + links.level
    sequence = jnp.sum(jnp.where(slots == slot, slot_sequence, 0))
    length = jnp.sum(jnp.where(slots == sequence, sequence_lengths, 0)).astype(jnp.int32)
    odd = links.level % 2

    def numbers(*values):
        return jnp.stack([jnp.asarray(value, jnp.int32) for value in values])

    core_line = numbers(core)
    first_column = first_gain.astype(wide)[:, None]
    second_column = second_gain.astype(wide)[:, None]
    gains = jnp.concatenate([first_column, second_column], axis=1)
    attention_weights = (query_weight, key_weight, value_weight, output_weight)
    feed_weights = (expand_weight, contract_weight)
    steps = Steps()
    odd_line = odd.reshape(1)
    chips, square = links.chips, links.square
    order = links.order()
    places = numbers(*links.weight_places(), core, *order)
    order_line = numbers(*order)
    slot_places = numbers(*links.quarter_places(), length, *order)
    length_line = length.reshape(1)

    line_width = 2 * total_length
    falling = jnp.concatenate([jnp.flip(offset_bucket), jnp.full((1,), -1, jnp.int32)])
    matching = falling[:, None] == jnp.arange(bucket_count)[None, :]
    own_table = lax.dynamic_slice_in_dim(bias_table, core * own_heads, own_heads, 1)
    lines = dot(own_table, matching.astype(low), 0, 1)

    arrived = links.sibling(other_side(steps, core_line, attention_weights, feed_weights, gains))
    token_trades = links.to_slot(send_blocks(steps, odd_line, tokens))
    attention_pieces = links.gather(
        attention_shard(steps, core_line, attention_weights, gains, arrived)
    )
    strips = bias_strips(steps, lines.reshape(own_heads, 1, line_width))
    late_shard = hidden_shard(steps, core_line, 1, feed_weights, gains, arrived)
    steps.wait(*attention_pieces[1:3])
    token_halves = links.both_halves(steps, token_trades)
    token_low, normed_one, normed_one_t = token_rows_of(
        steps, slot_places, token_halves, True, chips, square
    )
    early_shard = hidden_shard(steps, core_line, 0, feed_weights, gains, arrived)
    early_pieces = links.gather(early_shard)
    cotangent_trades = links.to_slot(send_blocks(steps, odd_line, cotangent))
    qkv_width = 3 * own_inner
    qkv = rows_product(
        steps, places, [normed_one], attention_pieces, 0, qkv_width, False, "qkv_product"
    )
    pairs = own_inner // tile
    half_pairs = pairs // 2
    forward = functools.partial(attention_forward, steps, length_line, qkv, strips)
    first_context, first_totals, first_tops = forward(0, half_pairs)
    cotangent_halves = links.both_halves(steps, cotangent_trades)
    steps.wait(*early_pieces[1:3])
    last_context, last_totals, last_tops = forward(half_pairs, half_pairs)
    contexts = [first_context, last_context]
    steps.wait(early_pieces[-1])
    output_columns = (qkv_width, qkv_width + own_inner)
    attended = rows_product(
        steps, places, contexts, attention_pieces, *output_columns, True, "attended_product"
    )
    attended_other = links.sibling(attended)
    late_first = links.turn(late_shard, False)
    _, out_low, out_low_t = token_rows_of(
        steps, slot_places, cotangent_halves, False, chips, square
    )
    hidden_one, normed_two, normed_two_t = second_norm(
        steps, order_line, token_low, attended, attended_other, chips, square
    )
    late_pieces = links.gather_slowly(steps, late_shard, late_first)
    operands = (normed_two, normed_two_t, out_low, out_low_t)
    mixed_sum, normed_sum, *early_terms = feed_forward(steps, places, *operands, early_pieces)
    early = links.scatter(*early_terms)
    mixed_own, mixed_away, normed_two_part, *late_terms = feed_forward(
        steps, places, *operands, late_pieces, (mixed_sum, normed_sum)
    )
    normed_two_other = links.sibling(normed_two_part)
    mixed_other = links.sibling(mixed_away)
    late = links.scatter(*late_terms)
    early = links.scatter_near(steps, early)
    hidden_grad, attended_grad, attended_grad_t, context_grad = hidden_back(
        steps,
        places,
        normed_two_part,
        normed_two_other,
        hidden_one,
        out_low,
        attention_pieces,
        *output_columns,
        chips,
        square,
    )
    result_quarters = finish_half(
        steps, core, odd, length, mixed_own, mixed_other, hidden_one, token_low, False
    )
    result_trades = links.from_slot(result_quarters)

    def backward(pair):
        half = pair // half_pairs
        return attention_backward(
            steps,
            length_line,
            qkv,
            contexts[half],
            context_grad,
            (first_totals, last_totals)[half],
            strips,
            pair,
            half * half_pairs,
        )

    *grads_a, strips_a = backward(0)
    *grads_b, strips_b = backward(1)
    steps.wait(*result_trades)
    early = links.scatter_own(steps, early)
    late = links.scatter_near(steps, late)
    first = links.scatter(
        *attention_terms(steps, attended_grad_t, normed_one_t, contexts, grads_a + grads_b)
    )
    *grads_c, strips_c = backward(2)
    late = links.scatter_own(steps, late)
    *grads_d, strips_d = backward(3)
    early = links.level_across(steps, early)
    first = links.scatter_near(steps, first)
    last = links.scatter(
        *attention_terms(steps, attended_grad_t, normed_one_t, (), grads_c + grads_d)
    )
    own_part, away_part = input_product(
        steps, places, grads_a + grads_b + grads_c + grads_d, attention_pieces
    )
    away_other = links.sibling(away_part)
    first = links.scatter_own(steps, first)
    late = links.level_across(steps, late)
    last = links.scatter_near(steps, last)
    early = links.level_out(steps, early)
    last = links.scatter_own(steps, last)
    first = links.level_across(steps, first)
    input_quarters = finish_half(
        steps, core, odd, length, own_part, away_other, hidden_grad, token_low, True
    )
    input_trades = links.from_slot(input_quarters)
    steps.wait(early[1])
    late = links.level_out(steps, late)
    last = links.level_across(steps, last)
    result_pieces = links.gather(links.received(result_trades))
    first = links.level_out(steps, first)
    early_left, early_right = links.level_done(early)
    steps.wait(late[1], *input_trades)
    diagonals = jnp.concatenate(
        [diagonal_sums(steps, part) for part in (strips_a, strips_b, strips_c, strips_d)], axis=0
    ).reshape(own_heads, line_width)
    table_grad = lax.dot_general(
        diagonals,
        matching.astype(wide),
        (((1,), (0,)), ((), ())),
        precision=lax.Precision.HIGHEST,
        preferred_element_type=wide,
    )
    tops = jnp.concatenate([first_tops, last_tops], axis=0).reshape(own_heads, tile)
    small = jnp.concatenate([table_grad, tops[:, : tile - bucket_count]], axis=1)
    for small in links.small_hops(small):
        pass
    last = links.level_out(steps, last)
    late_left, late_right = links.level_done(late)
    first_left, first_right = links.level_done(first)
    last_left, last_right = links.level_done(last)
    input_gradient = links.received(input_trades).astype(wide)

    def slot_of(wanted):
        return jnp.sum(jnp.where(slot_sequence == wanted, slots, 0))

    own_slots = [slot_of(links.shard * held_count + row) for row in range(held_count)]
    other_slots = [slot_of((links.shard ^ 1) * held_count + row) for row in range(held_count)]
    piece_slots = [
        (2 * chip + core) * held_count + row
        for chip in order
        for row in range(held_count)
    ]
    picked, picked_other = pick_slots(
        steps,
        numbers(*own_slots, *other_slots, *piece_slots),
        result_pieces,
    )
    from_other = links.sibling(picked_other)
    output = jnp.stack(
        [
            jnp.where((s // held_count) % 2 == core, picked[row], from_other[row])
            for row, s in enumerate(own_slots)
        ]
    )

    def side_by_side(*parts):
        return jnp.concatenate(parts, axis=1).astype(wide)

    raw_two = side_by_side(early_left[0], late_left[0], early_right[0], late_right[0])
    contract_weight_gradient = side_by_side(
        early_left[1], late_left[1], early_right[1], late_right[1]
    )

    output_weight_gradient = side_by_side(first_left[:, :own_inner], first_right[:, :own_inner])

    def inner_columns(block):
        pieces = []
        for first_side, last_side in ((first_left, last_left), (first_right, last_right)):
            for start, side in ((own_inner, first_side), (0, last_side)):
                for pair in range(half_pairs):
                    first = start + (3 * pair + block) * tile
                    pieces.append(side[:, first : first + tile])
        return side_by_side(*pieces)

    raw_query, raw_key, raw_value = (inner_columns(block) for block in range(3))
    first_gain_gradient = jnp.sum(
        query_weight.astype(wide) * raw_query
        + key_weight.astype(wide) * raw_key
        + value_weight.astype(wide) * raw_value,
        axis=1,
    )
    second_gain_gradient = jnp.sum(expand_weight.astype(wide) * raw_two, axis=1)
    query_weight_gradient = first_column * raw_query
    key_weight_gradient = first_column * raw_key
    value_weight_gradient = first_column * raw_value
    expand_weight_gradient = second_column * raw_two

    small = links.in_order(small, links.sibling(small))
    table_rows = bucket_count // links.shards
    bias_table_gradient = lax.dynamic_slice_in_dim(
        small[:, :bucket_count].T, links.shard * table_rows, table_rows, 0
    )
    largest = small[:, bucket_count]
    shrink = clip_limit / jnp.maximum(clip_limit, largest)
    column_scale = jnp.repeat(jnp.sqrt(shrink), head_size)
    new_query_weight = query_weight.astype(wide) * column_scale[None, :]
    new_key_weight = key_weight.astype(wide) * column_scale[None, :]
    return (
        output,
        input_gradient,
        first_gain_gradient,
        second_gain_gradient,
        query_weight_gradient,
        key_weight_gradient,
        value_weight_gradient,
        output_weight_gradient,
        expand_weight_gradient,
        contract_weight_gradient,
        bias_table_gradient,
        largest,
        new_query_weight,
        new_key_weight,
    )


def solution(mesh):
    return jax.shard_map(
        local,
        mesh=mesh,
        in_specs=(
            P("fsdp", "ctx", None),
            P("fsdp", "ctx", None),
            P(),
            P(),
            P(),
            P("fsdp"),
            P("fsdp"),
            P("fsdp", None),
            P("fsdp", None),
            P("fsdp", None),
            P("fsdp", None),
            P("fsdp", None),
            P("fsdp", None),
            P(),
            P(),
        ),
        out_specs=(
            P("fsdp", "ctx", None),
            P("fsdp", "ctx", None),
            P("fsdp"),
            P("fsdp"),
            P("fsdp", None),
            P("fsdp", None),
            P("fsdp", None),
            P("fsdp", None),
            P("fsdp", None),
            P("fsdp", None),
            P("fsdp", None),
            P(),
            P("fsdp", None),
            P("fsdp", None),
        ),
        check_vma=False,
    )
```
